32 devices in a mesh: section: 2 (over core), dp: 16 (over z, y, x).
Axes of the slice: x: 2, y: 2, z: 4, core: 2. Of those that a mesh axis runs over, the one named last changes fastest.
Arguments:
- stream_in: float32 [2, 16, 384, 512], P(None, 'dp'), may hold values from -6 to 6, as said below
- cotangent: float32 [2, 16, 384, 512], P(None, 'dp'), may hold values from -6 to 6, as said below
- segment_ids: int32 [2, 16, 384], P(None, 'dp'), may hold values from 0 to 5, never falling along the last dimension, each value on 1 to 192 neighbouring positions
- pad_mask: int32 [2, 16, 384], P(None, 'dp'), may hold values 0 or 1
- w_query: bfloat16 [2, 512, 512], P('section'), may hold values from -0.25 to 0.25
- w_key: bfloat16 [2, 512, 512], P('section'), may hold values from -0.25 to 0.25
- w_value: bfloat16 [2, 512, 512], P('section'), may hold values from -0.25 to 0.25
- w_out: bfloat16 [2, 512, 512], P('section'), may hold values from -0.75 to 0.75
- w_in: bfloat16 [2, 512, 2048], P('section'), may hold values from -0.25 to 0.25
- w_back: bfloat16 [2, 2048, 512], P('section'), may hold values from -0.125 to 0.125
- alphas: float32 [2, 2], P('section'), may hold values from 0.5 to 1.5
Outputs:
- acts: float32 [2, 2, 16, 384, 512], P('section', None, 'dp')
- input_grads: float32 [2, 2, 16, 384, 512], P('section', None, 'dp')
- grad_query: float32 [2, 512, 512], P('section')
- grad_key: float32 [2, 512, 512], P('section')
- grad_value: float32 [2, 512, 512], P('section')
- grad_out: float32 [2, 512, 512], P('section')
- grad_in: float32 [2, 512, 2048], P('section')
- grad_back: float32 [2, 2048, 512], P('section')
- grad_alphas: float32 [2, 2], P('section')
- norms: float32 [2, 3], P('section')
The draws below stay inside these ranges and needn't reach their ends.
Inputs may be any that keep to these rules, and one draw needn't show every extreme that they name: `stream_in`: independent entries of mean 0 and deviation about 1. `cotangent`: independent entries of mean 0 and deviation about 1.
All inputs are finite; a program needn't handle non-finite values. No bound on the sum of `pad_mask` on one device may be relied on, other than what follows from the above.
Results may differ from the reference program's by a relative error of at most 0.0005.
Values sent between devices are 32-bit elements; how exact they have to be, the bound alone decides.
No kernel may reach another device: no remote copies, remote signals or barrier semaphores. Data moves between devices by JAX's collectives and lax.ppermute only.
A program may use at most 192 MiB of HBM per device.

```python
import math
import jax
import jax.numpy as jnp
import numpy as np
from jax import lax

D = 512
HEADS = 8
HEAD_DIM = 64
FF = 2048
ROW = 384
MICRO = 2
SEQS = 6
ROWS = 16
N_SECTION = 2


def drawn_normal(key, shape):
    values = jax.random.normal(key, shape, jnp.float32)
    return jnp.clip(values, -6.0, 6.0)


def draw_stream_in(key, part):
    key = jax.random.fold_in(key, 11)
    return drawn_normal(key, (MICRO, ROWS, ROW, D))


def draw_cotangent(key, part):
    key = jax.random.fold_in(key, 23)
    return drawn_normal(key, (MICRO, ROWS, ROW, D))


def touch_ends(values, own_key, least, high):
    spot = [jax.random.randint(jax.random.fold_in(own_key, axis), (), 0, length) for axis, length in enumerate(values.shape)]
    main_axis = values.shape.index(max(values.shape))
    beside = spot[:main_axis] + [(spot[main_axis] + 1) % values.shape[main_axis]] + spot[main_axis + 1:]
    return values.at[tuple(spot)].set(least).at[tuple(beside)].set(high)


def levels(rng, dims, split, smallest, top_value):
    factor_of, own = 1.0, jax.random.fold_in(rng, 6)
    for position, parts in split:
        heights = jnp.exp(jax.random.uniform(jax.random.fold_in(own, position), (parts,), jnp.float32, smallest / len(split), top_value / len(split)))
        factor_of = factor_of * jnp.repeat(heights, dims[position] // parts).reshape([-1 if axis == position else 1 for axis in range(len(dims))])
    return factor_of


def split_up(count, total, limit, lean):
    weights = [(1 << 20) // math.isqrt(rank ** lean) + 1 for rank in range(2, count + 1)]
    spare, holding = total - limit - (count - 1), [1] * (count - 1)
    while spare > 0:
        candidates = [i for i in range(count - 1) if holding[i] < limit]
        whole, left = sum([weights[i] for i in candidates]), spare
        for i in candidates:
            extra = min(limit - holding[i], max(1, left * weights[i] // whole), spare)
            holding[i] = holding[i] + extra
            spare = spare - extra
    return np.array([limit] + holding)


def ragged(own_key, number_of, total, reach, slope):
    if number_of == 2:
        one = jax.random.randint(own_key, (), max(1, total - reach), min(reach, total - 1) + 1)
        return jnp.stack([one, total - one])
    tallies = jnp.asarray(split_up(number_of, total, reach, slope), jnp.int32)
    twos = (number_of - 1) // 2
    giver, sink = tallies[1:1 + 2 * twos:2], tallies[2:2 + 2 * twos:2]
    room = jnp.minimum(giver - 1, reach - sink)
    moved = jax.random.randint(jax.random.fold_in(own_key, 1), (twos,), 0, 1 << 20) % (room + 1)
    tallies = tallies.at[1:1 + 2 * twos:2].set(giver - moved).at[2:2 + 2 * twos:2].set(sink + moved)
    return tallies[jax.random.permutation(jax.random.fold_in(own_key, 2), number_of)]


def normal_values(stream_key, shape, spread, bound, shards=(), held_as=jnp.bfloat16):
    entries = spread * jax.random.normal(stream_key, shape, jnp.float32)
    if shards:
        entries = entries * levels(stream_key, shape, shards, -0.22, 0.18)
    return jnp.clip(entries, -bound, bound).astype(held_as)


def setup_inputs(seed: int = 0) -> dict:
    key_list = jax.random.split(jax.random.key(seed), 12)
    return {
        "stream_in": draw_stream_in(jax.random.fold_in(key_list[11], 71), 0),
        "cotangent": draw_cotangent(jax.random.fold_in(key_list[11], 71), 0),
        "segment_ids": jax.vmap(lambda own: jnp.searchsorted(jnp.cumsum(ragged(own, SEQS, ROW, ROW // 2, 2)), jnp.arange(ROW), side="right"))(jax.random.split(key_list[2], MICRO * ROWS)).reshape((MICRO, ROWS, ROW)).astype(jnp.int32),
        "pad_mask": touch_ends((jax.random.randint(key_list[3], (MICRO, ROWS, ROW), 0, 8) < 7).astype(jnp.int32), jax.random.fold_in(key_list[3], 1), 0, 1),
        "w_query": normal_values(key_list[4], (N_SECTION, D, D), D ** -0.5, 0.25, ((0, 2),)),
        "w_key": normal_values(key_list[5], (N_SECTION, D, D), D ** -0.5, 0.25, ((0, 2),)),
        "w_value": normal_values(key_list[6], (N_SECTION, D, D), D ** -0.5, 0.25, ((0, 2),)),
        "w_out": normal_values(key_list[7], (N_SECTION, D, D), (D // 8) ** -0.5, 0.75, ((0, 2),)),
        "w_in": normal_values(key_list[8], (N_SECTION, D, FF), D ** -0.5, 0.25, ((0, 2),)),
        "w_back": normal_values(key_list[9], (N_SECTION, FF, D), FF ** -0.5, 0.125, ((0, 2),)),
        "alphas": jnp.clip(0.5 + 1.0 * jax.random.uniform(key_list[10], (N_SECTION, 2), jnp.float32) ** levels(key_list[10], (N_SECTION, 2), ((0, 2),), -0.2, 0.2), 0.5, 1.5),
    }


@jax.custom_vjp
def low(v):
    return lax.optimization_barrier(v.astype(jnp.bfloat16)).astype(jnp.float32)

@jax.custom_vjp
def low_back(v):
    return v

def low_keep(v):
    return (low(v), None)

def low_pass(kept, grad):
    return (grad,)

def back_keep(v):
    return (v, None)

def back_low(kept, grad):
    return (low(grad),)
low.defvjp(low_keep, low_pass)
low_back.defvjp(back_keep, back_low)

def project(left_side, right_side):
    return jnp.dot(left_side, right_side, precision=lax.Precision.HIGHEST)

def attend(stream, w_query, w_key, w_value, w_out, segment_row, valid_row):
    row_count = stream.shape[0]
    query = project(stream, w_query).reshape(row_count, HEADS, HEAD_DIM)
    keys_all = project(stream, w_key).reshape(row_count, HEADS, HEAD_DIM)
    values_all = project(stream, w_value).reshape(row_count, HEADS, HEAD_DIM)
    scores = jnp.einsum('qhd,khd->hqk', query, keys_all, precision=lax.Precision.HIGHEST) * HEAD_DIM ** (-0.5)
    places = jnp.arange(row_count)
    allowed = (segment_row[:, None] == segment_row[None, :]) & (places[None, :] <= places[:, None])
    allowed = allowed & ((valid_row[None, :] > 0) | (places[None, :] == places[:, None]))
    scores = jnp.where(allowed[None], scores, -1e+30)
    probs = jax.nn.softmax(scores, axis=-1)
    mixed = jnp.einsum('hqk,khd->qhd', probs, values_all, precision=lax.Precision.HIGHEST)
    mixed = mixed.reshape(row_count, HEADS * HEAD_DIM)
    return project(mixed, w_out)

def layer(params, stream, segment_row, valid_row):
    w_query, w_key, w_value, w_out, w_in, w_back, scales = params
    attn_branch = scales[0] * attend(stream, w_query, w_key, w_value, w_out, segment_row, valid_row)
    middle = stream + attn_branch
    before = project(middle, w_in)
    ffn_branch = scales[1] * project(jax.nn.gelu(before), w_back)
    result = middle + ffn_branch
    weighting = valid_row.astype(jnp.float32)[:, None]
    squares = jnp.stack([jnp.sum(result * result * weighting), jnp.sum(attn_branch * attn_branch * weighting), jnp.sum(ffn_branch * ffn_branch * weighting)])
    return (result, squares)

def section_params(params, index):
    return tuple((weight[index] for weight in params))

def reference(stream_in, cotangent, segment_ids, pad_mask, w_query, w_key, w_value, w_out, w_in, w_back, alphas):
    params = tuple((weight.astype(jnp.float32) for weight in (w_query, w_key, w_value, w_out, w_in, w_back))) + (alphas,)
    row_total = MICRO * ROWS
    first_rows = stream_in.reshape(row_total, ROW, D)
    target_rows = cotangent.reshape(row_total, ROW, D)
    segment_rows = segment_ids.reshape(row_total, ROW)
    valid_rows = pad_mask.reshape(row_total, ROW)

    def forward(layer_params, first_in, bump_in):

        def two_layers(items):
            row_in, row_bump, segment_row, valid_row = items
            first_out, first_sums = layer(section_params(layer_params, 0), row_in, segment_row, valid_row)
            second_out, second_sums = layer(section_params(layer_params, 1), first_out + row_bump, segment_row, valid_row)
            return (second_out, (first_out, jnp.stack([first_sums, second_sums])))
        finals, (middles, sums) = lax.map(jax.checkpoint(two_layers), (first_in, bump_in, segment_rows, valid_rows))
        return (finals, (middles, sums))
    bump_zero = jnp.zeros_like(first_rows)
    finals, pullback, (middles, sums) = jax.vjp(forward, params, first_rows, bump_zero, has_aux=True)
    grad_params, grad_first, grad_bump = pullback(target_rows)
    token_count = jnp.sum(pad_mask.astype(jnp.float32))
    totals = lax.optimization_barrier(jnp.sum(sums, axis=0))
    norms = jnp.sqrt(totals / (jnp.maximum(token_count, 1.0) * D))
    acts = jnp.stack([middles, finals]).reshape(2, MICRO, ROWS, ROW, D)
    input_grads = jnp.stack([grad_first, grad_bump]).reshape(2, MICRO, ROWS, ROW, D)
    return (acts, input_grads, grad_params[0], grad_params[1], grad_params[2], grad_params[3], grad_params[4], grad_params[5], grad_params[6], norms)
```

```python
import functools
import math
import jax
import jax.numpy as jnp
from jax import lax
from jax.experimental import pallas as pl
from jax.experimental.pallas import tpu as pltpu
from jax.sharding import PartitionSpec as P

D = 512
HEADS = 8
HEAD_DIM = 64
GELU_A = math.sqrt(2.0 / math.pi)
GELU_B = 0.044715


def start_all(copies):
    for copy in copies:
        copy.start()
    return copies


def wait_all(copies):
    for copy in copies:
        copy.wait()


def split(value):
    high = value.astype(jnp.bfloat16)
    low = (value - high.astype(jnp.float32)).astype(jnp.bfloat16)
    return (high, low)


def stacked(value):
    return jnp.concatenate(split(value), axis=0)


def dot(left_side, right_side):
    return jnp.dot(left_side, right_side, preferred_element_type=jnp.float32)


def dot_rows(left_side, right_side):
    return lax.dot_general(
        left_side, right_side, (((1,), (1,)), ((), ())), preferred_element_type=jnp.float32
    )


def folded(product):
    half = product.shape[0] // 2
    return product[:half] + product[half:]


def gelu_inner(value):
    return jnp.tanh(GELU_A * (value + GELU_B * (value * value * value)))


def tile_of(numbers):
    lane = lax.broadcasted_iota(jnp.int32, (8, 128), 1)
    tile = jnp.zeros((8, 128), jnp.float32)
    for index, number in enumerate(numbers):
        tile = jnp.where(lane == index, number, tile)
    return tile


def fill_bias(bias_ref, segment_row, valid_row):
    blocks = segment_row.shape[1] // 128
    segment_col = jnp.broadcast_to(segment_row, (128, segment_row.shape[1])).T
    valid_col = jnp.broadcast_to(valid_row, (128, valid_row.shape[1])).T
    for kb in range(blocks):
        ks = slice(kb * 128, kb * 128 + 128)
        for qb in range(kb, blocks):
            qs = slice(qb * 128, qb * 128 + 128)
            k_place = lax.broadcasted_iota(jnp.int32, (128, 128), 0) + kb * 128
            q_place = lax.broadcasted_iota(jnp.int32, (128, 128), 1) + qb * 128
            allowed = (segment_col[ks] == segment_row[:, qs]) & (k_place <= q_place)
            allowed = allowed & ((valid_col[ks] > 0) | (k_place == q_place))
            bias_ref[ks, qs] = jnp.where(allowed, 0.0, -1e30)


def halves_of(value):
    lane = lax.broadcasted_iota(jnp.int32, value.shape, 1)
    zero = jnp.zeros_like(value)
    return (jnp.where(lane < HEAD_DIM, value, zero), jnp.where(lane < HEAD_DIM, zero, value))


def pair_scores(keys_cat, queries_high, queries_low):
    sides = []
    for high, low in zip(halves_of(queries_high), halves_of(queries_low)):
        sides.append(jnp.concatenate([high, high, low], axis=1))
    return dot_rows(keys_cat, jnp.concatenate(sides, axis=0))


def three_lanes(value):
    high, low = split(value)
    return jnp.concatenate([high, low, high], axis=1)


def forward_body(tick, *refs):
    (info, alphas, segments, valids, streams, wq, wk, wv, wo, wi, wb) = refs[:11]
    received = streams.at[0] if tick == 0 else refs[11]
    refs = refs[11 + (0 if tick == 0 else 11) :]
    (acts, sent, saved_s, saved_q, saved_k, saved_v, saved_o, saved_l, saved_m, saved_p, sums) = refs[:11]
    (s_v, wq_v, wk_v, wv_v, wo_v, wi_v, wb_v, q_v, k_v, v_v, ot_v, l_v, m_v, p_v, a_v, t_v, bias_v, x_v, in_sem, out_sem) = refs[11:]
    section = info[0]
    micro = tick - section
    rows = s_v.shape[0]
    blocks = rows // 128

    @pl.when((micro >= 0) & (micro < 2))
    def _():
        pairs = [(wq, wq_v), (wk, wk_v), (wv, wv_v), (wo, wo_v), (wi, wi_v), (wb, wb_v)]
        loads = [pltpu.make_async_copy(a, b, in_sem.at[i]) for i, (a, b) in enumerate(pairs)]

        @pl.when(section == 0)
        def _():
            pltpu.make_async_copy(streams.at[micro], s_v, in_sem.at[6]).start()

        @pl.when(section != 0)
        def _():
            pltpu.make_async_copy(received, s_v, in_sem.at[6]).start()

        for load in loads:
            load.start()
        segment_row = segments[micro].astype(jnp.float32)
        valid_row = valids[micro].astype(jnp.float32)
        fill_bias(bias_v, segment_row, valid_row)
        pltpu.make_async_copy(received, s_v, in_sem.at[6]).wait()
        x_v[...] = stacked(s_v[...])
        for index, (weight, target) in enumerate(((wq_v, q_v), (wk_v, k_v), (wv_v, v_v))):
            loads[index].wait()
            value = folded(dot(x_v[...], weight[...]))
            target[...] = value * 0.125 if index == 0 else value

        stores = []

        def store(index, source, target):
            copy = pltpu.make_async_copy(source, target, out_sem.at[index])
            copy.start()
            stores.append(copy)

        store(0, s_v, saved_s.at[micro])
        store(1, q_v, saved_q.at[micro])
        store(2, k_v, saved_k.at[micro])
        store(3, v_v, saved_v.at[micro])

        for pair in range(HEADS // 2):
            lanes = pl.ds(pair * 128, 128)
            keys_cat = three_lanes(k_v[:, lanes])
            queries_high, queries_low = split(q_v[:, lanes])
            values_high, values_low = split(v_v[:, lanes].T)
            for qb in range(blocks):
                qs = slice(qb * 128, qb * 128 + 128)
                ks = (qb + 1) * 128
                scores = pair_scores(keys_cat[:ks], queries_high[qs], queries_low[qs])
                bias = bias_v[:ks, qs]
                for head in range(2):
                    part = scores[:, head * 128 : head * 128 + 128] + bias
                    top = jnp.max(part, axis=0, keepdims=True)
                    probs = jnp.exp(part - top)
                    total = jnp.sum(probs, axis=0, keepdims=True)
                    high, low = split(probs)
                    hs = slice(head * HEAD_DIM, head * HEAD_DIM + HEAD_DIM)
                    both = jnp.concatenate([values_high[hs, :ks], values_low[hs, :ks]], axis=0)
                    mixed = folded(dot(both, high)) + dot(values_high[hs, :ks], low)
                    at = pl.ds(pair * 128 + head * HEAD_DIM, HEAD_DIM)
                    ot_v[at, qs] = mixed / total
                    l_v[pair, head : head + 1, qs] = top + jnp.log(total)

        store(4, ot_v, saved_o.at[micro])
        store(5, l_v, saved_l.at[micro])
        x_v[...] = stacked(ot_v[...].T)
        loads[3].wait()
        attn = folded(dot(x_v[...], wo_v[...])) * alphas[0, 0]
        valid_col = jnp.broadcast_to(valid_row, (128, rows)).T
        weighting = jnp.concatenate([valid_col] * (D // 128), axis=1)
        attn_sum = jnp.sum(attn * attn * weighting)
        middle = s_v[...] + attn
        m_v[...] = middle
        store(6, m_v, saved_m.at[micro])
        x_v[...] = stacked(middle)
        a_v[...] = jnp.zeros_like(a_v)
        loads[4].wait()
        loads[5].wait()

        for part in range(wi_v.shape[1] // 512):
            cols = pl.ds(part * 512, 512)
            before = folded(dot(x_v[...], wi_v[:, cols]))
            p_v[:, cols] = before
            hidden = stacked(0.5 * before * (1.0 + gelu_inner(before)))
            a_v[...] += folded(dot(hidden, wb_v[cols, :]))

        store(7, p_v, saved_p.at[micro])
        ffn = a_v[...] * alphas[0, 1]
        result = m_v[...] + ffn
        a_v[...] = result
        store(8, a_v, acts.at[micro])
        store(9, a_v, sent)
        t_v[...] = tile_of([jnp.sum(result * result * weighting), attn_sum, jnp.sum(ffn * ffn * weighting)])
        store(10, t_v, sums.at[micro])
        for copy in stores:
            copy.wait()


def struct(*shape):
    return pltpu.HBM(shape, jnp.float32)


def loose(*shape):
    return jax.ShapeDtypeStruct(shape, jnp.float32)


def in_hbm(arrays):
    return [pltpu.with_memory_space_constraint(array, pltpu.HBM) for array in arrays]


ANY = pl.BlockSpec(memory_space=pl.ANY)
SCALARS = pl.BlockSpec(memory_space=pltpu.SMEM)
LOCAL = pl.BlockSpec(memory_space=pltpu.VMEM)


def forward_tick(tick, info, alphas, segments, valids, streams, received, weights, state):
    micro_count, rows, width = streams.shape
    inner = weights[4].shape[1]
    whole = struct(micro_count, rows, width)
    shapes = [
        whole,
        struct(rows, width),
        whole,
        whole,
        whole,
        whole,
        struct(micro_count, width, rows),
        struct(micro_count, HEADS // 2, 8, rows),
        whole,
        struct(micro_count, rows, inner),
        struct(micro_count, 8, 128),
    ]
    kept = [0, 2, 3, 4, 5, 6, 7, 8, 9, 10]
    extra = [] if state is None else [received] + in_hbm(state)
    aliases = {} if state is None else {12 + i: out for i, out in enumerate(kept)}
    f32, bf16 = jnp.float32, jnp.bfloat16
    vmem = pltpu.VMEM
    scratch = [vmem((rows, width), f32)] + [vmem(w.shape, bf16) for w in weights]
    scratch += [vmem((rows, width), f32)] * 3 + [vmem((width, rows), f32), vmem((HEADS // 2, 8, rows), f32)]
    scratch += [vmem((rows, width), f32), vmem((rows, inner), f32), vmem((rows, width), f32)]
    scratch += [vmem((8, 128), f32), vmem((rows, rows), f32), vmem((2 * rows, width), bf16)]
    scratch += [pltpu.SemaphoreType.DMA((7,)), pltpu.SemaphoreType.DMA((11,))]
    outs = pl.pallas_call(
        functools.partial(forward_body, tick),
        out_shape=shapes,
        in_specs=[SCALARS, SCALARS, LOCAL, LOCAL] + [ANY] * (7 + len(extra)),
        out_specs=[ANY] * len(shapes),
        scratch_shapes=scratch,
        input_output_aliases=aliases,
        compiler_params=pltpu.CompilerParams(vmem_limit_bytes=28 * 1024 * 1024),
        cost_estimate=pl.CostEstimate(flops=10**10, bytes_accessed=2 * 10**7, transcendentals=10**6),
        name="layer_forward",
    )(info, alphas, segments, valids, *in_hbm([streams, *weights]), *extra)
    return (outs[1], [outs[i] for i in kept])


TOKEN = [None]


def unit_shape(sizes):
    x, y, near, far = sizes
    return (near * far, y, x, 4 * D // (x * y * near * far), D)


def slot_structs(sizes, axis, more=0):
    x, y, near, far = sizes
    shape = [size for index, size in ((3, far), (2, near), (1, y), (0, x)) if index != axis]
    return [struct(*shape, unit_shape(sizes)[3] + more, D)] * sizes[axis]


def put_part(unit, part, value):
    depth = unit.shape[0] // 4
    unit[pl.ds(part * depth, depth)] = value.reshape((depth,) + unit.shape[1:])


def slot_copies(info, sizes, axis, unit, slots, sems, part):
    x, y, near, far = sizes
    depth, rows = near * far // 4, unit.shape[3]
    copies = []
    for by in range(sizes[axis]):
        place = lax.rem(info[1 + axis] + by, sizes[axis])
        if axis == 2:
            pairs = [(unit.at[at * near + place], slots[by].at[at]) for at in range(far) if part * depth < (at + 1) * near <= (part + 1) * depth]
        else:
            pairs = []
            for at in range(part * depth, (part + 1) * depth):
                source = unit.at[at, :, place] if axis == 0 else unit.at[at, place]
                pairs.append((source, slots[by].at[at // near, at % near, :, pl.ds(0, rows)]))
        for source, target in pairs:
            copies.append(pltpu.make_async_copy(source, target, sems.at[part, len(copies)]))
    return copies


def copy_count(sizes, axis):
    return sizes[axis] * max(1, sizes[2] * sizes[3] // 4)


def three_dots(left_high, left_low, right_high, right_low):
    return dot(left_high, right_high) + dot(left_low, right_high) + dot(left_high, right_low)


def back_body(turn, count, sizes, axis, *refs):
    info, alphas = refs[:2]
    upstreams, saved_p = refs[2:4], refs[4]
    slots, refs = refs[6 : 6 + count], refs[7 + count :]
    g_v, gh_v, p_v, w_v, in_sem, out_sem = refs
    parts = p_v.shape[0]
    rows = g_v.shape[1]

    @pl.when(info[0] == 1 - turn)
    def _():
        def load(part, micro):
            cols = pl.ds(part * 512, 512)
            return pltpu.make_async_copy(
                saved_p.at[micro, :, cols], p_v.at[part, pl.ds(micro * rows, rows)], in_sem.at[part, micro]
            )

        firsts = []
        for micro in range(2):
            source = upstreams[micro] if turn else upstreams[micro].at[micro, 0]
            firsts.append(pltpu.make_async_copy(source, g_v.at[micro], in_sem.at[parts, micro]))
        start_all(firsts)
        for part in range(parts):
            for micro in range(2):
                load(part, micro).start()
        wait_all(firsts)
        high, low = split(jnp.concatenate([g_v[0], g_v[1]], axis=0) * alphas[0, 1])
        gh_v[0] = high
        gh_v[1] = low

        stores = []
        for part in range(parts):
            for micro in range(2):
                load(part, micro).wait()
            before = p_v[part].T
            high, low = split(0.5 * before * (1.0 + gelu_inner(before)))
            put_part(w_v, part, three_dots(high, low, gh_v[0], gh_v[1]))
            stores += start_all(slot_copies(info, sizes, axis, w_v, slots, out_sem, part))
        wait_all(stores)


def chain_body(turn, micro, extra, *refs):
    info, alphas, segments, valids, upstream = refs[:5]
    saved_p = refs[5]
    sources = refs[6:11]
    wi, wb = refs[11:13]
    weights = refs[13:17]
    refs = refs[18 + extra :]
    (befores, spreads, firsts, passed, small, sent, _) = refs[:7]
    (g_v, p_v, wi_v, wb_v, gs_v, d_v, b_v) = refs[7:14]
    held = refs[14:19]
    weights_v = refs[19:23]
    (bias_v, do_v, dt_v, dl_v, qt_v, dk_v, dv_v, x_v, f_v, y_v, t_v, in_sem, part_sem, w_sem, out_sem) = refs[23:]
    parts = p_v.shape[0]
    rows = bias_v.shape[0]
    blocks = rows // 128
    (q_v, k_v, v_v, o_v, l_v) = held
    (wq_v, wk_v, wv_v, wo_v) = weights_v

    @pl.when(info[0] == 1 - turn)
    def _():
        def loads(part):
            cols = pl.ds(part * 512, 512)
            return [
                pltpu.make_async_copy(wb.at[cols], wb_v.at[part], part_sem.at[part, 0]),
                pltpu.make_async_copy(saved_p.at[micro, :, cols], p_v.at[part], part_sem.at[part, 1]),
                pltpu.make_async_copy(wi.at[:, cols], wi_v.at[part], part_sem.at[part, 2]),
            ]

        source = upstream if turn else upstream.at[micro, 0]
        first = pltpu.make_async_copy(source, g_v, in_sem.at[5])
        first.start()
        for part in range(parts):
            start_all(loads(part))
        fetches = [pltpu.make_async_copy(a, b, w_sem.at[i]) for i, (a, b) in enumerate(zip(weights, weights_v))]
        start_all(fetches[::-1])
        later = start_all(
            [pltpu.make_async_copy(a.at[micro], b, in_sem.at[i]) for i, (a, b) in enumerate(zip(sources, held))]
        )
        segment_row = segments[micro].astype(jnp.float32)
        valid_row = valids[micro].astype(jnp.float32)
        fill_bias(bias_v, segment_row, valid_row)
        first.wait()
        gs_v[...] = stacked(g_v[...] * alphas[0, 1])
        d_v[...] = jnp.zeros_like(d_v)

        def step(part, total):
            wait_all(loads(part))
            cols = pl.ds(part * 512, 512)
            before = p_v[part]
            grad_hidden = folded(dot_rows(gs_v[...], wb_v[part]))
            inner = gelu_inner(before)
            above = 0.5 * (1.0 + inner)
            total = total + jnp.sum(grad_hidden * (before * above))
            slope = above + 0.5 * before * (1.0 - inner * inner) * (GELU_A * (1.0 + 3.0 * GELU_B * (before * before)))
            high, low = split(grad_hidden * slope)
            b_v[0, :, cols] = high
            b_v[1, :, cols] = low
            d_v[...] += folded(dot_rows(jnp.concatenate([high, low], axis=0), wi_v[part]))
            return total

        total_inner = jnp.float32(0.0)
        for part in range(parts):
            total_inner = step(part, total_inner)
        stores = start_all([pltpu.make_async_copy(b_v, befores.at[micro], out_sem.at[0])])
        middle = g_v[...] + d_v[...]
        d_v[...] = middle
        high, low = split(middle * alphas[0, 0])
        f_v[0] = high
        f_v[1] = low
        stores += start_all([pltpu.make_async_copy(f_v, firsts.at[micro], out_sem.at[1])])
        wait_all(fetches)
        wait_all(later)
        grad_mixed = folded(dot_rows(jnp.concatenate([high, low], axis=0), wo_v[...]))
        do_v[...] = grad_mixed
        dt_v[...] = grad_mixed.T
        total_mixed = jnp.float32(0.0)
        for head in range(HEADS):
            hs = slice(head * HEAD_DIM, head * HEAD_DIM + HEAD_DIM)
            spread = jnp.sum(dt_v[hs, :] * o_v[hs, :], axis=0, keepdims=True)
            dl_v[head // 2, head % 2 : head % 2 + 1, :] = spread
            total_mixed = total_mixed + jnp.sum(spread)

        def pair_step(pair):
            lanes = pl.ds(pair * 128, 128)
            keys = k_v[:, lanes]
            keys_cat = three_lanes(keys)
            values_cat = three_lanes(v_v[:, lanes])
            queries_high, queries_low = split(q_v[:, lanes])
            do_high, do_low = split(do_v[:, lanes])
            turned_high, turned_low = split(keys.T)
            for qb in range(blocks - 1, -1, -1):
                qs = slice(qb * 128, qb * 128 + 128)
                ks = (qb + 1) * 128
                scores = pair_scores(keys_cat[:ks], queries_high[qs], queries_low[qs])
                slopes = pair_scores(values_cat[:ks], do_high[qs], do_low[qs])
                bias = bias_v[:ks, qs]
                sides = [halves_of(x[qs]) for x in (queries_high, queries_low, do_high, do_low)]
                key_part = jnp.zeros((ks, 128), jnp.float32)
                value_part = jnp.zeros((ks, 128), jnp.float32)
                for head in range(2):
                    own = slice(head * 128, head * 128 + 128)
                    at = slice(head, head + 1)
                    probs = jnp.exp((scores[:, own] + bias) - l_v[pair, at, qs])
                    grads = probs * (slopes[:, own] - dl_v[pair, at, qs])
                    q_high, q_low, d_high, d_low = [side[head] for side in sides]
                    none = jnp.zeros_like(q_high)

                    def product(left_high, left_low, right_high, right_low):
                        left_cat = jnp.concatenate([left_high, left_low], axis=1)
                        above = jnp.concatenate([right_high, right_low], axis=1)
                        below = jnp.concatenate([right_high, none], axis=1)
                        value = dot(left_cat, jnp.concatenate([above, below], axis=0))
                        return value[:, :128] + value[:, 128:]

                    value_part = value_part + product(*split(probs), d_high, d_low)
                    high, low = split(grads)
                    key_part = key_part + product(high, low, q_high, q_low)
                    hs = slice(head * HEAD_DIM, head * HEAD_DIM + HEAD_DIM)
                    both = jnp.concatenate([turned_high[hs, :ks], turned_low[hs, :ks]], axis=0)
                    turned = folded(dot(both, high)) + dot(turned_high[hs, :ks], low)
                    rows_at = pl.ds(pair * 128 + head * HEAD_DIM, HEAD_DIM)
                    qt_v[rows_at, qs] = turned * 0.125
                if qb == blocks - 1:
                    dk_v[:, lanes] = key_part
                    dv_v[:, lanes] = value_part
                else:
                    dk_v[:ks, lanes] += key_part
                    dv_v[:ks, lanes] += value_part

        for pair in range(HEADS // 2):
            pair_step(pair)
        result = d_v[...]
        for index, (source, weight) in enumerate(((qt_v, wq_v), (dk_v, wk_v), (dv_v, wv_v))):
            value = source[...].T if index == 0 else source[...]
            high, low = split(value)
            x_v[0, :, pl.ds(index * D, D)] = high
            x_v[1, :, pl.ds(index * D, D)] = low
            result = result + folded(dot_rows(jnp.concatenate([high, low], axis=0), weight[...]))
        y_v[...] = result
        t_v[...] = tile_of([total_mixed / alphas[0, 0], total_inner / alphas[0, 1]])
        stores += start_all(
            [
                pltpu.make_async_copy(y_v, sent, out_sem.at[2]),
                pltpu.make_async_copy(y_v, passed.at[micro], out_sem.at[3]),
                pltpu.make_async_copy(x_v, spreads.at[micro], out_sem.at[4]),
                pltpu.make_async_copy(t_v, small.at[micro], out_sem.at[5]),
            ]
        )
        wait_all(stores)


def rest_body(turn, counts, sizes, axes, extra, *refs):
    info, valids = refs[:2]
    saved_m, saved_s, saved_o, befores, spreads, firsts, sums, small = refs[2:10]
    refs = refs[11 + extra :]
    slots, refs = (refs[: counts[0]], refs[counts[0] : sum(counts)]), refs[sum(counts) + 1 :]
    (m_v, s_v, o_v, lt_v, r_v, w_v, n_v, t_v, in_sem, r_sem, out_sem, n_sem, t_sem) = refs
    rows = m_v.shape[1]

    @pl.when(info[0] == 1 - turn)
    def _():
        def loads(index):
            copies = []
            for micro in range(2):
                for half in range(2):
                    if index < 4:
                        source = befores.at[micro, half, :, pl.ds(index * 512, 512)]
                    elif index < 7:
                        source = spreads.at[micro, half, :, pl.ds((index - 4) * 512, 512)]
                    else:
                        source = firsts.at[micro, half]
                    target = r_v.at[index, half, pl.ds(micro * rows, rows)]
                    copies.append(pltpu.make_async_copy(source, target, r_sem.at[index, micro * 2 + half]))
            return copies

        lefts = [pltpu.make_async_copy(a, b, in_sem.at[i]) for i, (a, b) in enumerate(((saved_m, m_v), (saved_s, s_v), (saved_o, o_v)))]
        tiles = [
            pltpu.make_async_copy(sums, n_v.at[pl.ds(0, 2)], n_sem.at[0]),
            pltpu.make_async_copy(small, n_v.at[pl.ds(2, 2)], n_sem.at[1]),
        ]
        lefts[0].start()
        start_all(loads(0))
        start_all(lefts[1:])
        for index in range(1, 8):
            start_all(loads(index))
        start_all(tiles)

        def turn_left(index, source, transpose):
            for micro in range(2):
                high, low = split(source[micro].T if transpose else source[micro])
                lt_v[index, 0, :, pl.ds(micro * rows, rows)] = high
                lt_v[index, 1, :, pl.ds(micro * rows, rows)] = low

        stores = []
        for index in range(8):
            if index in (0, 4, 7):
                left = (0, 4, 7).index(index)
                lefts[left].wait()
                turn_left(left, (m_v, s_v, o_v)[left], left < 2)
            wait_all(loads(index))
            unit, part = w_v.at[index // 4], index % 4
            put_part(unit, part, three_dots(lt_v[left, 0], lt_v[left, 1], r_v[index, 0], r_v[index, 1]))
            own = index // 4
            stores += start_all(slot_copies(info, sizes, axes[own], unit, slots[own], out_sem.at[own], part))
        wait_all(tiles)
        lane = lax.broadcasted_iota(jnp.int32, (8, 256), 1)
        tile = jnp.where(lane == 3, jnp.sum(valids[...].astype(jnp.float32)), jnp.zeros((8, 256), jnp.float32))
        for index in range(3):
            tile = jnp.where(lane == index, n_v[0, 0, index] + n_v[1, 0, index], tile)
        for index in range(2):
            tile = jnp.where(lane == 4 + index, n_v[2, 0, index] + n_v[3, 0, index], tile)
        t_v[...] = tile
        axis, unit_rows = axes[1], w_v.shape[4]
        for by in range(counts[1]):

            @pl.when(lax.rem(info[1 + axis] + by, sizes[axis]) == 0)
            def _():
                target = slots[1][by].at[0, 0, 0, pl.ds(unit_rows, 8), pl.ds(0, 256)]
                copy = pltpu.make_async_copy(t_v, target, t_sem.at[0])
                copy.start()
                copy.wait()

        wait_all(stores)


def call(body, name, free, inputs, specs, outs, scratch, before, flops, limit):
    extra = list(before) if before is not None else []
    inputs = list(inputs[:free]) + in_hbm(list(inputs[free:])) + [TOKEN[0]]
    results = pl.pallas_call(
        functools.partial(body, len(extra)),
        out_shape=outs + [loose(8, 128)],
        in_specs=specs + [ANY] * (len(inputs) - len(specs) + len(extra)),
        out_specs=[ANY] * (len(outs) + 1),
        scratch_shapes=scratch,
        input_output_aliases={len(inputs) + i: i for i in range(len(extra))},
        compiler_params=pltpu.CompilerParams(vmem_limit_bytes=limit * 1024 * 1024),
        cost_estimate=pl.CostEstimate(flops=flops, bytes_accessed=2 * 10**7, transcendentals=10**6),
        name=name,
    )(*inputs, *in_hbm(extra))
    TOKEN[0] = results[-1]
    return results[:-1]


def backward_back(turn, info, alphas, upstreams, before, sizes, axis):
    micros, rows, inner = before.shape
    parts = inner // 512
    vmem, dma = pltpu.VMEM, pltpu.SemaphoreType.DMA
    f32, bf16 = jnp.float32, jnp.bfloat16
    slots = slot_structs(sizes, axis)
    scratch = [
        vmem((micros, rows, D), f32),
        vmem((2, micros * rows, D), bf16),
        vmem((parts, micros * rows, 512), f32),
        vmem(unit_shape(sizes), f32),
        dma((parts + 1, 2)),
        dma((parts, copy_count(sizes, axis))),
    ]

    def body(extra, *refs):
        back_body(turn, len(slots), sizes, axis, *refs)

    return call(
        body, "grad_back", 4, [info, alphas] + list(upstreams) + [before], [SCALARS, SCALARS], slots, scratch, None,
        5 * 10**9, 24,
    )


def backward_chain(turn, micro, info, alphas, segments, valids, upstream, before, saved, weights, previous):
    micros, rows, inner = before.shape
    parts = inner // 512
    vmem, dma = pltpu.VMEM, pltpu.SemaphoreType.DMA
    f32, bf16 = jnp.float32, jnp.bfloat16
    wq, wk, wv, wo, wi, wb = weights
    outs = [
        pltpu.HBM((micros, 2, rows, inner), bf16),
        pltpu.HBM((micros, 2, rows, 3 * D), bf16),
        pltpu.HBM((micros, 2, rows, D), bf16),
        struct(micros, rows, D),
        struct(micros, 8, 128),
        struct(rows, D),
    ]
    scratch = [
        vmem((rows, D), f32),
        vmem((parts, rows, 512), f32),
        vmem((parts, D, 512), bf16),
        vmem((parts, 512, D), bf16),
        vmem((2 * rows, D), bf16),
        vmem((rows, D), f32),
        vmem((2, rows, inner), bf16),
    ]
    scratch += [vmem(x.shape[1:], f32) for x in saved] + [vmem((D, D), bf16)] * 4
    scratch += [
        vmem((rows, rows), f32),
        vmem((rows, D), f32),
        vmem((D, rows), f32),
        vmem((HEADS // 2, 8, rows), f32),
        vmem((D, rows), f32),
        vmem((rows, D), f32),
        vmem((rows, D), f32),
        vmem((2, rows, 3 * D), bf16),
        vmem((2, rows, D), bf16),
        vmem((rows, D), f32),
        vmem((8, 128), f32),
        dma((6,)),
        dma((parts, 3)),
        dma((4,)),
        dma((6,)),
    ]

    def body(extra, *refs):
        chain_body(turn, micro, extra, *refs)

    inputs = [info, alphas, segments, valids, upstream, before] + list(saved) + [wi, wb, wq, wk, wv, wo]
    return call(
        body, "grad_chain", 5, inputs, [SCALARS, SCALARS, LOCAL, LOCAL], outs, scratch, previous, 2 * 10**10, 36
    )


def backward_rest(turn, info, valids, middle, stream, mixed, chain, sums, previous, sizes, axes):
    micros, rows, _ = middle.shape
    befores, spreads, firsts, _, small = chain
    vmem, dma = pltpu.VMEM, pltpu.SemaphoreType.DMA
    f32, bf16 = jnp.float32, jnp.bfloat16
    slots = [slot_structs(sizes, axes[0]), slot_structs(sizes, axes[1], 8)]
    scratch = [
        vmem(middle.shape, f32),
        vmem(stream.shape, f32),
        vmem(mixed.shape, f32),
        vmem((3, 2, D, micros * rows), bf16),
        vmem((8, 2, micros * rows, 512), bf16),
        vmem((2,) + unit_shape(sizes), f32),
        vmem((4, 8, 128), f32),
        vmem((8, 256), f32),
        dma((3,)),
        dma((8, 4)),
        dma((2, 4, max(copy_count(sizes, axis) for axis in axes))),
        dma((2,)),
        dma((1,)),
    ]

    def body(extra, *refs):
        rest_body(turn, [len(each) for each in slots], sizes, axes, extra, *refs)

    inputs = [info, valids, middle, stream, mixed, befores, spreads, firsts, sums, small]
    return call(body, "grad_rest", 2, inputs, [SCALARS, LOCAL], slots[0] + slots[1], scratch, previous, 10**10, 40)


def local_call(body, name, who, info, inputs, outs, scratch, previous=None, specs=None):
    extra = list(previous) if previous is not None else []
    inputs = [info, TOKEN[0]] + list(inputs)

    def guarded(*refs):
        def run():
            first = len(inputs) + len(extra)
            body(refs[0], refs[2 : len(inputs)], refs[first : first + len(outs)], refs[first + len(outs) + 1 :])

        if who is None:
            run()
        else:
            pl.when(refs[0][0] == who)(run)

    results = pl.pallas_call(
        guarded,
        out_shape=list(outs) + [loose(8, 128)],
        in_specs=[SCALARS] + [ANY] * (len(inputs) - 1 + len(extra)),
        out_specs=(specs or [ANY] * len(outs)) + [ANY],
        scratch_shapes=scratch,
        input_output_aliases={len(inputs) + i: i for i in range(len(extra))},
        compiler_params=pltpu.CompilerParams(vmem_limit_bytes=12 * 1024 * 1024),
        cost_estimate=pl.CostEstimate(flops=10**6, bytes_accessed=6 * 10**6, transcendentals=0),
        name=name,
    )(*inputs, *in_hbm(extra))
    TOKEN[0] = results[-1]
    return results[:-1]


def left_dims(done):
    return [axis for axis in (3, 2, 1, 0) if axis not in done]


def picked(ref, dims, axis, index):
    return ref.at[(slice(None),) * dims.index(axis) + (index,)]


def reduce_stage(sizes, order, step, who, info, arrays):
    shape = arrays[0].shape
    count = len(arrays)
    dims = left_dims(order[:step])
    if step < len(order):
        axis = order[step]
        at = dims.index(axis)
        outs = [loose(*shape[:at], *shape[at + 1 :])] * sizes[axis]
    else:
        outs = [loose(*shape)]

    def body(info, ins, outs, scratch):
        held, sem = scratch
        wait_all(start_all([pltpu.make_async_copy(ref, held.at[i], sem.at[i]) for i, ref in enumerate(ins)]))
        total = held[0]
        for i in range(1, count):
            total = total + held[i]
        held[0] = total
        stores = []
        for by in range(len(outs)):
            source = held.at[0]
            if step < len(order):
                source = picked(source, dims, axis, lax.rem(info[1 + axis] + by, sizes[axis]))
            stores.append(pltpu.make_async_copy(source, outs[by], sem.at[count + by]))
        wait_all(start_all(stores))

    scratch = [pltpu.VMEM((count,) + shape, jnp.float32), pltpu.SemaphoreType.DMA((count + len(outs),))]
    return local_call(body, "reduce_step", who, info, arrays, outs, scratch)


def place_stage(sizes, order, step, who, info, arrays):
    axis = order[step]
    dims = left_dims(order[:step])
    at = dims.index(axis)
    shape = arrays[0].shape
    count = sizes[axis]

    def body(info, ins, outs, scratch):
        copies = []
        for by in range(count):
            target = picked(outs[0], dims, axis, lax.rem(info[1 + axis] + count - by, count))
            copies.append(pltpu.make_async_copy(ins[by], target, scratch[0].at[by]))
        wait_all(start_all(copies))

    out = loose(*shape[:at], count, *shape[at:])
    return local_call(body, "place_step", who, info, arrays, [out], [pltpu.SemaphoreType.DMA((count,))])[0]


def last_stage(sizes, order, who, info, arrays, kind, previous):
    x, y, near, far = sizes
    rows = unit_shape(sizes)[3]
    depth = near * far // 4
    axis = order[0]
    count = sizes[axis]
    specs, scratch = None, [pltpu.SemaphoreType.DMA((near * far * count + 1,))]
    if kind == "rows":
        shapes = [struct(near * far, y, x, rows, D)]
    elif kind == "columns":
        shapes = [struct(depth, y, x, rows, 4 * D)]
    else:
        shapes = [struct(depth, y, x, rows, D)] * 4 + [loose(1, 2), loose(1, 3)]
        specs = [ANY] * 4 + [LOCAL] * 2
        scratch += [pltpu.VMEM((8, 256), jnp.float32)]

    def body(info, ins, outs, scratch):
        sem = scratch[0]
        copies = []

        def put(source, target):
            copies.append(pltpu.make_async_copy(source, target, sem.at[len(copies)]))

        for by in range(count):
            place = lax.rem(info[1 + axis] + count - by, count)
            if axis == 2:
                for at in range(far):
                    put(ins[by].at[at], outs[0].at[at * near + place])
                continue
            for at in range(near * far):
                source = ins[by].at[at // near, at % near, :, pl.ds(0, rows)]
                part, inside = at // depth, at % depth
                out = outs[part] if kind == "four" else outs[0]
                lanes = pl.ds(part * D if kind == "columns" else 0, D)
                inside = at if kind == "rows" else inside
                put(source, out.at[inside, :, place, :, lanes] if axis == 0 else out.at[inside, place, :, :, lanes])
        start_all(copies)
        if kind == "four":
            tile_v = scratch[1]
            for by in range(count):

                @pl.when(info[1 + axis] == by)
                def _():
                    source = ins[by].at[0, 0, 0, pl.ds(rows, 8), pl.ds(0, 256)]
                    copy = pltpu.make_async_copy(source, tile_v, sem.at[len(copies)])
                    copy.start()
                    copy.wait()

            tile = tile_v[0:1, 0:128]
            outs[-2][...] = tile[:, 4:6]
            outs[-1][...] = jnp.sqrt(tile[:, 0:3] / (jnp.maximum(tile[:, 3:4], 1.0) * D))
        wait_all(copies)

    return local_call(body, "place_last", who, info, arrays, shapes, scratch, previous, specs)


def extents(count):
    bits = count.bit_length() - 1
    if 1 << bits != count:
        return (1, 1, 1, count)
    side = 1 << (bits // 3)
    depth = count // (side * side)
    near = 2 if depth > 1 else 1
    return (side, side, near, depth // near)


def shifted(value, axis, by, sizes, who=None):
    count = math.prod(sizes)
    stride, length = math.prod(sizes[:axis]), sizes[axis]
    pairs = []
    for chip in range(count):
        along = (chip // stride) % length
        pairs.append((chip, chip + ((along + by) % length - along) * stride))
    if who is None:
        return lax.ppermute(value, "dp", pairs)
    return lax.ppermute(value, ("section", "dp"), [(who * count + a, who * count + b) for a, b in pairs])


def summing(slots, order, kind, sizes, info, who=None, previous=None):
    pieces = list(slots)
    for step in range(1, len(order) + 1):
        axis = order[step - 1]
        pieces = [pieces[0]] + [shifted(pieces[by], axis, by, sizes, who) for by in range(1, sizes[axis])]
        yield
        pieces = reduce_stage(sizes, order, step, who, info, pieces)
    whole = pieces[0]
    for step in range(len(order) - 1, -1, -1):
        axis = order[step]
        copies = [whole] + [shifted(whole, axis, by, sizes, who) for by in range(1, sizes[axis])]
        yield
        if step:
            whole = place_stage(sizes, order, step, who, info, copies)
    yield last_stage(sizes, order, who, info, copies, kind, previous() if previous else None)


def shards(stream_in, cotangent, segment_ids, pad_mask, w_query, w_key, w_value, w_out, w_in, w_back, alphas):
    weights = [weight[0] for weight in (w_query, w_key, w_value, w_out, w_in, w_back)]
    streams = stream_in[:, 0]
    sizes = extents(lax.axis_size("dp"))
    chip = lax.axis_index("dp")
    section = lax.axis_index("section")
    places, left = [], chip
    for size in sizes:
        places.append(lax.rem(left, size))
        left = lax.div(left, size)
    info = jnp.stack([section] + places).astype(jnp.int32)
    received, state = None, None
    for tick in range(3):
        sent, state = forward_tick(tick, info, alphas, segment_ids, pad_mask, streams, received, weights, state)
        if tick < 2:
            received = lax.ppermute(sent, "section", [(0, 1)])
    acts, saved_s, saved_q, saved_k, saved_v, saved_o, saved_l, saved_m, saved_p, sums = state
    saved = (saved_q, saved_k, saved_v, saved_o, saved_l)
    TOKEN[0] = jnp.zeros((8, 128), jnp.float32)

    def chain_step(turn, micro, upstream, previous):
        return backward_chain(
            turn, micro, info, alphas, segment_ids, pad_mask, upstream, saved_p, saved, weights, previous
        )

    orders = {"back": (2, 0, 1, 3), "inner": (0, 1, 2, 3), "attention": (1, 2, 0, 3)}
    first_axes = [orders["inner"][0], orders["attention"][0]]

    def back_step(turn, upstreams):
        return backward_back(turn, info, alphas, upstreams, saved_p, sizes, orders["back"][0])

    def rest_step(turn, chain, previous):
        return backward_rest(
            turn, info, pad_mask, saved_m, saved_s, saved_o, chain[:5], sums, previous, sizes, first_axes
        )

    late = {}
    early = summing(back_step(0, [cotangent, cotangent]), orders["back"], "rows", sizes, info, who=1)
    next(early)
    chain, upstreams = None, []
    for micro in range(2):
        chain = chain_step(0, micro, cotangent, chain)
        upstreams.append(lax.ppermute(chain[5], "section", [(1, 0)]))
        chain = chain[:5]
        next(early)
    slots = rest_step(0, chain, None)
    next(early)
    for micro in range(2):
        chain = chain_step(1, micro, upstreams[micro], chain)[:5]
    back = summing(
        back_step(1, upstreams), orders["back"], "rows", sizes, info, who=0, previous=lambda: late["back"]
    )
    next(back)
    slots = rest_step(1, chain, slots)
    split_at = sizes[first_axes[0]]
    inner = summing(slots[:split_at], orders["inner"], "columns", sizes, info)
    attention = summing(slots[split_at:], orders["attention"], "four", sizes, info)
    next(inner)
    next(attention)
    next(early)
    next(back)
    next(early)
    next(inner)
    next(attention)
    next(early)
    next(back)
    next(early)
    next(inner)
    next(attention)
    next(back)
    late["back"] = next(early)
    for _ in range(5):
        next(inner)
        next(attention)
        back_out = next(back)
    inner_out = next(inner)
    attention_out = next(attention)
    return (
        acts[None, :, None],
        chain[3][None, :, None],
        attention_out[0].reshape(1, D, D),
        attention_out[1].reshape(1, D, D),
        attention_out[2].reshape(1, D, D),
        attention_out[3].reshape(1, D, D),
        inner_out[0].reshape(1, D, -1),
        back_out[0].reshape(1, -1, D),
        attention_out[4],
        attention_out[5],
    )


def solution(mesh):
    in_specs = (
        P(None, "dp", None, None),
        P(None, "dp", None, None),
        P(None, "dp", None),
        P(None, "dp", None),
        P("section", None, None),
        P("section", None, None),
        P("section", None, None),
        P("section", None, None),
        P("section", None, None),
        P("section", None, None),
        P("section", None),
    )
    out_specs = (
        P("section", None, "dp", None, None),
        P("section", None, "dp", None, None),
        P("section", None, None),
        P("section", None, None),
        P("section", None, None),
        P("section", None, None),
        P("section", None, None),
        P("section", None, None),
        P("section", None),
        P("section", None),
    )
    return jax.shard_map(shards, mesh=mesh, in_specs=in_specs, out_specs=out_specs, check_vma=False)
```

```python
import functools
import math
import jax
import jax.numpy as jnp
from jax import lax
from jax.experimental import pallas as pl
from jax.experimental.pallas import tpu as pltpu
from jax.sharding import PartitionSpec as P

D = 512
HEADS = 8
HEAD_DIM = 64
GELU_A = math.sqrt(2.0 / math.pi)
GELU_B = 0.044715


def start_all(copies):
    for copy in copies:
        copy.start()
    return copies


def wait_all(copies):
    for copy in copies:
        copy.wait()


def split(value):
    high = value.astype(jnp.bfloat16)
    low = (value - high.astype(jnp.float32)).astype(jnp.bfloat16)
    return (high, low)


def stacked(value):
    return jnp.concatenate(split(value), axis=0)


def dot(left_side, right_side):
    return jnp.dot(left_side, right_side, preferred_element_type=jnp.float32)


def dot_rows(left_side, right_side):
    return lax.dot_general(
        left_side, right_side, (((1,), (1,)), ((), ())), preferred_element_type=jnp.float32
    )


def folded(product):
    half = product.shape[0] // 2
    return product[:half] + product[half:]


def put_split(target, value):
    high, low = split(value)
    target[0] = high
    target[1] = low


def two_dots(left_side, right_side):
    return dot(left_side[0], right_side) + dot(left_side[1], right_side)


def gelu_inner(value):
    return jnp.tanh(GELU_A * (value + GELU_B * (value * value * value)))


def tile_of(numbers):
    lane = lax.broadcasted_iota(jnp.int32, (8, 128), 1)
    tile = jnp.zeros((8, 128), jnp.float32)
    for index, number in enumerate(numbers):
        tile = jnp.where(lane == index, number, tile)
    return tile


def fill_bias(bias_ref, segment_row, valid_row):
    blocks = segment_row.shape[1] // 128
    segment_col = jnp.broadcast_to(segment_row, (128, segment_row.shape[1])).T
    valid_col = jnp.broadcast_to(valid_row, (128, valid_row.shape[1])).T
    for kb in range(blocks):
        ks = slice(kb * 128, kb * 128 + 128)
        for qb in range(kb, blocks):
            qs = slice(qb * 128, qb * 128 + 128)
            k_place = lax.broadcasted_iota(jnp.int32, (128, 128), 0) + kb * 128
            q_place = lax.broadcasted_iota(jnp.int32, (128, 128), 1) + qb * 128
            allowed = (segment_col[ks] == segment_row[:, qs]) & (k_place <= q_place)
            allowed = allowed & ((valid_col[ks] > 0) | (k_place == q_place))
            bias_ref[ks, qs] = jnp.where(allowed, 0.0, -1e30)


def halves_of(value):
    lane = lax.broadcasted_iota(jnp.int32, value.shape, 1)
    zero = jnp.zeros_like(value)
    return (jnp.where(lane < HEAD_DIM, value, zero), jnp.where(lane < HEAD_DIM, zero, value))


def pair_scores(keys_cat, queries_high, queries_low):
    sides = []
    for high, low in zip(halves_of(queries_high), halves_of(queries_low)):
        sides.append(jnp.concatenate([high, high, low], axis=1))
    return dot_rows(keys_cat, jnp.concatenate(sides, axis=0))


def three_lanes(value):
    high, low = split(value)
    return jnp.concatenate([high, low, high], axis=1)


def forward_body(tick, *refs):
    (info, alphas, segments, valids, streams, wq, wk, wv, wo, wi, wb) = refs[:11]
    received = streams.at[0] if tick == 0 else refs[11]
    refs = refs[11 + (0 if tick == 0 else 11) :]
    (acts, sent, saved_s, saved_q, saved_k, saved_v, saved_o, saved_l, saved_m, saved_p, sums) = refs[:11]
    (s_v, wq_v, wk_v, wv_v, wo_v, wi_v, wb_v, q_v, k_v, v_v, ot_v, l_v, m_v, p_v, a_v, t_v, bias_v, x_v, in_sem, out_sem) = refs[11:]
    section = info[0]
    micro = tick - section
    rows = s_v.shape[0]
    blocks = rows // 128

    @pl.when((micro >= 0) & (micro < 2))
    def _():
        pairs = [(wq, wq_v), (wk, wk_v), (wv, wv_v), (wo, wo_v), (wi, wi_v), (wb, wb_v)]
        loads = [pltpu.make_async_copy(a, b, in_sem.at[i]) for i, (a, b) in enumerate(pairs)]

        @pl.when(section == 0)
        def _():
            pltpu.make_async_copy(streams.at[micro], s_v, in_sem.at[6]).start()

        @pl.when(section != 0)
        def _():
            pltpu.make_async_copy(received, s_v, in_sem.at[6]).start()

        for load in loads:
            load.start()
        segment_row = segments[micro].astype(jnp.float32)
        valid_row = valids[micro].astype(jnp.float32)
        fill_bias(bias_v, segment_row, valid_row)
        pltpu.make_async_copy(received, s_v, in_sem.at[6]).wait()
        put_split(x_v, s_v[...])
        for index, (weight, target) in enumerate(((wq_v, q_v), (wk_v, k_v), (wv_v, v_v))):
            loads[index].wait()
            value = two_dots(x_v, weight[...])
            target[...] = value * 0.125 if index == 0 else value

        stores = []

        def store(index, source, target):
            copy = pltpu.make_async_copy(source, target, out_sem.at[index])
            copy.start()
            stores.append(copy)

        store(0, s_v, saved_s.at[micro])
        store(1, q_v, saved_q.at[micro])
        store(2, k_v, saved_k.at[micro])
        store(3, v_v, saved_v.at[micro])

        for pair in range(HEADS // 2):
            lanes = pl.ds(pair * 128, 128)
            keys_cat = three_lanes(k_v[:, lanes])
            queries_high, queries_low = split(q_v[:, lanes])
            values_high, values_low = split(v_v[:, lanes].T)
            for qb in range(blocks):
                qs = slice(qb * 128, qb * 128 + 128)
                ks = (qb + 1) * 128
                scores = pair_scores(keys_cat[:ks], queries_high[qs], queries_low[qs])
                bias = bias_v[:ks, qs]
                for head in range(2):
                    part = scores[:, head * 128 : head * 128 + 128] + bias
                    top = jnp.max(part, axis=0, keepdims=True)
                    probs = jnp.exp(part - top)
                    total = jnp.sum(probs, axis=0, keepdims=True)
                    high, low = split(probs)
                    hs = slice(head * HEAD_DIM, head * HEAD_DIM + HEAD_DIM)
                    both = jnp.concatenate([values_high[hs, :ks], values_low[hs, :ks]], axis=0)
                    mixed = folded(dot(both, high)) + dot(values_high[hs, :ks], low)
                    at = pl.ds(pair * 128 + head * HEAD_DIM, HEAD_DIM)
                    ot_v[at, qs] = mixed / total
                    l_v[pair, head : head + 1, qs] = top + jnp.log(total)

        store(4, ot_v, saved_o.at[micro])
        store(5, l_v, saved_l.at[micro])
        put_split(x_v, ot_v[...].T)
        loads[3].wait()
        attn = two_dots(x_v, wo_v[...]) * alphas[0, 0]
        valid_col = jnp.broadcast_to(valid_row, (128, rows)).T
        weighting = jnp.concatenate([valid_col] * (D // 128), axis=1)
        attn_sum = jnp.sum(attn * attn * weighting)
        middle = s_v[...] + attn
        m_v[...] = middle
        store(6, m_v, saved_m.at[micro])
        put_split(x_v, middle)
        a_v[...] = jnp.zeros_like(a_v)
        loads[4].wait()
        loads[5].wait()

        for part in range(wi_v.shape[1] // 512):
            cols = pl.ds(part * 512, 512)
            before = two_dots(x_v, wi_v[:, cols])
            p_v[:, cols] = before
            high, low = split(0.5 * before * (1.0 + gelu_inner(before)))
            a_v[...] += dot(high, wb_v[cols, :]) + dot(low, wb_v[cols, :])

        store(7, p_v, saved_p.at[micro])
        ffn = a_v[...] * alphas[0, 1]
        result = m_v[...] + ffn
        a_v[...] = result
        store(8, a_v, acts.at[micro])
        store(9, a_v, sent)
        t_v[...] = tile_of([jnp.sum(result * result * weighting), attn_sum, jnp.sum(ffn * ffn * weighting)])
        store(10, t_v, sums.at[micro])
        for copy in stores:
            copy.wait()


def struct(*shape):
    return pltpu.HBM(shape, jnp.float32)


def loose(*shape):
    return jax.ShapeDtypeStruct(shape, jnp.float32)


def in_hbm(arrays):
    return [pltpu.with_memory_space_constraint(array, pltpu.HBM) for array in arrays]


ANY = pl.BlockSpec(memory_space=pl.ANY)
SCALARS = pl.BlockSpec(memory_space=pltpu.SMEM)
LOCAL = pl.BlockSpec(memory_space=pltpu.VMEM)


def forward_tick(tick, info, alphas, segments, valids, streams, received, weights, state):
    micro_count, rows, width = streams.shape
    inner = weights[4].shape[1]
    whole = struct(micro_count, rows, width)
    shapes = [
        whole,
        struct(rows, width),
        whole,
        whole,
        whole,
        whole,
        struct(micro_count, width, rows),
        struct(micro_count, HEADS // 2, 8, rows),
        whole,
        struct(micro_count, rows, inner),
        struct(micro_count, 8, 128),
    ]
    kept = [0, 2, 3, 4, 5, 6, 7, 8, 9, 10]
    extra = [] if state is None else [received] + in_hbm(state)
    aliases = {} if state is None else {12 + i: out for i, out in enumerate(kept)}
    f32, bf16 = jnp.float32, jnp.bfloat16
    vmem = pltpu.VMEM
    scratch = [vmem((rows, width), f32)] + [vmem(w.shape, bf16) for w in weights]
    scratch += [vmem((rows, width), f32)] * 3 + [vmem((width, rows), f32), vmem((HEADS // 2, 8, rows), f32)]
    scratch += [vmem((rows, width), f32), vmem((rows, inner), f32), vmem((rows, width), f32)]
    scratch += [vmem((8, 128), f32), vmem((rows, rows), f32), vmem((2, rows, width), bf16)]
    scratch += [pltpu.SemaphoreType.DMA((7,)), pltpu.SemaphoreType.DMA((11,))]
    outs = pl.pallas_call(
        functools.partial(forward_body, tick),
        out_shape=shapes,
        in_specs=[SCALARS, SCALARS, LOCAL, LOCAL] + [ANY] * (7 + len(extra)),
        out_specs=[ANY] * len(shapes),
        scratch_shapes=scratch,
        input_output_aliases=aliases,
        compiler_params=pltpu.CompilerParams(vmem_limit_bytes=28 * 1024 * 1024),
        cost_estimate=pl.CostEstimate(flops=10**10, bytes_accessed=2 * 10**7, transcendentals=10**6),
        name="layer_forward",
    )(info, alphas, segments, valids, *in_hbm([streams, *weights]), *extra)
    return (outs[1], [outs[i] for i in kept])


TOKEN = [None]


def unit_shape(sizes):
    x, y, near, far = sizes
    return (near * far, y, x, 4 * D // (x * y * near * far), D)


def slot_structs(sizes, axis, more=0):
    x, y, near, far = sizes
    shape = [size for index, size in ((3, far), (2, near), (1, y), (0, x)) if index != axis]
    return [struct(*shape, unit_shape(sizes)[3] + more, D)] * sizes[axis]


def put_part(unit, part, value):
    depth = unit.shape[0] // 4
    unit[pl.ds(part * depth, depth)] = value.reshape((depth,) + unit.shape[1:])


def slot_copies(info, sizes, axis, unit, slots, sems, part):
    x, y, near, far = sizes
    depth, rows = near * far // 4, unit.shape[3]
    copies = []
    for by in range(sizes[axis]):
        place = lax.rem(info[1 + axis] + by, sizes[axis])
        if axis == 2:
            pairs = [(unit.at[at * near + place], slots[by].at[at]) for at in range(far) if part * depth < (at + 1) * near <= (part + 1) * depth]
        else:
            pairs = []
            for at in range(part * depth, (part + 1) * depth):
                source = unit.at[at, :, place] if axis == 0 else unit.at[at, place]
                pairs.append((source, slots[by].at[at // near, at % near, :, pl.ds(0, rows)]))
        for source, target in pairs:
            copies.append(pltpu.make_async_copy(source, target, sems.at[part, len(copies)]))
    return copies


def copy_count(sizes, axis):
    return sizes[axis] * max(1, sizes[2] * sizes[3] // 4)


def three_dots(left_high, left_low, right_high, right_low):
    return dot(left_high, right_high) + dot(left_low, right_high) + dot(left_high, right_low)


def back_body(count, sizes, axis, *refs):
    info, alphas = refs[:2]
    upstreams, targets, saved_p = refs[2:4], refs[4], refs[5]
    slots, refs = refs[7 : 7 + count], refs[8 + count :]
    g_v, gh_v, p_v, w_v, in_sem, out_sem = refs
    parts = p_v.shape[0]
    rows = g_v.shape[1]

    def load(part, micro):
        cols = pl.ds(part * 512, 512)
        return pltpu.make_async_copy(
            saved_p.at[micro, :, cols], p_v.at[part, pl.ds(micro * rows, rows)], in_sem.at[part, micro]
        )

    for micro in range(2):

        @pl.when(info[0] == 0)
        def _():
            pltpu.make_async_copy(upstreams[micro], g_v.at[micro], in_sem.at[parts, micro]).start()

        @pl.when(info[0] != 0)
        def _():
            pltpu.make_async_copy(targets.at[micro, 0], g_v.at[micro], in_sem.at[parts, micro]).start()

    for part in range(parts):
        for micro in range(2):
            load(part, micro).start()
    for micro in range(2):
        pltpu.make_async_copy(targets.at[micro, 0], g_v.at[micro], in_sem.at[parts, micro]).wait()
    high, low = split(jnp.concatenate([g_v[0], g_v[1]], axis=0) * alphas[0, 1])
    gh_v[0] = high
    gh_v[1] = low
    stores = []
    for part in range(parts):
        for micro in range(2):
            load(part, micro).wait()
        before = p_v[part].T
        high, low = split(0.5 * before * (1.0 + gelu_inner(before)))
        put_part(w_v, part, three_dots(high, low, gh_v[0], gh_v[1]))
        stores += start_all(slot_copies(info, sizes, axis, w_v, slots, out_sem, part))
    wait_all(stores)


def chain_body(turn, micro, extra, *refs):
    info, alphas, segments, valids, upstream = refs[:5]
    saved_p = refs[5]
    sources = refs[6:11]
    wi, wb = refs[11:13]
    weights = refs[13:17]
    refs = refs[18 + extra :]
    (befores, spreads, firsts, passed, small, sent, _) = refs[:7]
    (g_v, p_v, wi_v, wb_v, gs_v, d_v, b_v) = refs[7:14]
    held = refs[14:19]
    weights_v = refs[19:23]
    (bias_v, do_v, dt_v, dl_v, qt_v, dk_v, dv_v, x_v, f_v, y_v, t_v, in_sem, part_sem, w_sem, out_sem) = refs[23:]
    parts = p_v.shape[0]
    rows = bias_v.shape[0]
    blocks = rows // 128
    (q_v, k_v, v_v, o_v, l_v) = held
    (wq_v, wk_v, wv_v, wo_v) = weights_v

    @pl.when(info[0] == 1 - turn)
    def _():
        def loads(part):
            cols = pl.ds(part * 512, 512)
            return [
                pltpu.make_async_copy(wb.at[cols], wb_v.at[part], part_sem.at[part, 0]),
                pltpu.make_async_copy(saved_p.at[micro, :, cols], p_v.at[part], part_sem.at[part, 1]),
                pltpu.make_async_copy(wi.at[:, cols], wi_v.at[part], part_sem.at[part, 2]),
            ]

        source = upstream if turn else upstream.at[micro, 0]
        first = pltpu.make_async_copy(source, g_v, in_sem.at[5])
        first.start()
        for part in range(parts):
            start_all(loads(part))
        fetches = [pltpu.make_async_copy(a, b, w_sem.at[i]) for i, (a, b) in enumerate(zip(weights, weights_v))]
        start_all(fetches[::-1])
        later = start_all(
            [pltpu.make_async_copy(a.at[micro], b, in_sem.at[i]) for i, (a, b) in enumerate(zip(sources, held))]
        )
        segment_row = segments[micro].astype(jnp.float32)
        valid_row = valids[micro].astype(jnp.float32)
        fill_bias(bias_v, segment_row, valid_row)
        first.wait()
        gs_v[...] = stacked(g_v[...] * alphas[0, 1])
        d_v[...] = jnp.zeros_like(d_v)

        def step(part, total):
            wait_all(loads(part))
            cols = pl.ds(part * 512, 512)
            before = p_v[part]
            grad_hidden = folded(dot_rows(gs_v[...], wb_v[part]))
            inner = gelu_inner(before)
            above = 0.5 * (1.0 + inner)
            total = total + jnp.sum(grad_hidden * (before * above))
            slope = above + 0.5 * before * (1.0 - inner * inner) * (GELU_A * (1.0 + 3.0 * GELU_B * (before * before)))
            high, low = split(grad_hidden * slope)
            b_v[0, :, cols] = high
            b_v[1, :, cols] = low
            d_v[...] += folded(dot_rows(jnp.concatenate([high, low], axis=0), wi_v[part]))
            return total

        total_inner = jnp.float32(0.0)
        for part in range(parts):
            total_inner = step(part, total_inner)
        stores = start_all([pltpu.make_async_copy(b_v, befores.at[micro], out_sem.at[0])])
        middle = g_v[...] + d_v[...]
        d_v[...] = middle
        high, low = split(middle * alphas[0, 0])
        f_v[0] = high
        f_v[1] = low
        stores += start_all([pltpu.make_async_copy(f_v, firsts.at[micro], out_sem.at[1])])
        wait_all(fetches)
        wait_all(later)
        grad_mixed = folded(dot_rows(jnp.concatenate([high, low], axis=0), wo_v[...]))
        do_v[...] = grad_mixed
        dt_v[...] = grad_mixed.T
        total_mixed = jnp.float32(0.0)
        for head in range(HEADS):
            hs = slice(head * HEAD_DIM, head * HEAD_DIM + HEAD_DIM)
            spread = jnp.sum(dt_v[hs, :] * o_v[hs, :], axis=0, keepdims=True)
            dl_v[head // 2, head % 2 : head % 2 + 1, :] = spread
            total_mixed = total_mixed + jnp.sum(spread)

        def pair_step(pair):
            lanes = pl.ds(pair * 128, 128)
            keys = k_v[:, lanes]
            keys_cat = three_lanes(keys)
            values_cat = three_lanes(v_v[:, lanes])
            queries_high, queries_low = split(q_v[:, lanes])
            do_high, do_low = split(do_v[:, lanes])
            turned_high, turned_low = split(keys.T)
            for qb in range(blocks - 1, -1, -1):
                qs = slice(qb * 128, qb * 128 + 128)
                ks = (qb + 1) * 128
                scores = pair_scores(keys_cat[:ks], queries_high[qs], queries_low[qs])
                slopes = pair_scores(values_cat[:ks], do_high[qs], do_low[qs])
                bias = bias_v[:ks, qs]
                sides = [halves_of(x[qs]) for x in (queries_high, queries_low, do_high, do_low)]
                key_part = jnp.zeros((ks, 128), jnp.float32)
                value_part = jnp.zeros((ks, 128), jnp.float32)
                for head in range(2):
                    own = slice(head * 128, head * 128 + 128)
                    at = slice(head, head + 1)
                    probs = jnp.exp((scores[:, own] + bias) - l_v[pair, at, qs])
                    grads = probs * (slopes[:, own] - dl_v[pair, at, qs])
                    q_high, q_low, d_high, d_low = [side[head] for side in sides]
                    none = jnp.zeros_like(q_high)

                    def product(left_high, left_low, right_high, right_low):
                        left_cat = jnp.concatenate([left_high, left_low], axis=1)
                        above = jnp.concatenate([right_high, right_low], axis=1)
                        below = jnp.concatenate([right_high, none], axis=1)
                        value = dot(left_cat, jnp.concatenate([above, below], axis=0))
                        return value[:, :128] + value[:, 128:]

                    value_part = value_part + product(*split(probs), d_high, d_low)
                    high, low = split(grads)
                    key_part = key_part + product(high, low, q_high, q_low)
                    hs = slice(head * HEAD_DIM, head * HEAD_DIM + HEAD_DIM)
                    both = jnp.concatenate([turned_high[hs, :ks], turned_low[hs, :ks]], axis=0)
                    turned = folded(dot(both, high)) + dot(turned_high[hs, :ks], low)
                    rows_at = pl.ds(pair * 128 + head * HEAD_DIM, HEAD_DIM)
                    qt_v[rows_at, qs] = turned * 0.125
                if qb == blocks - 1:
                    dk_v[:, lanes] = key_part
                    dv_v[:, lanes] = value_part
                else:
                    dk_v[:ks, lanes] += key_part
                    dv_v[:ks, lanes] += value_part

        for pair in range(HEADS // 2):
            pair_step(pair)
        result = d_v[...]
        for index, (source, weight) in enumerate(((qt_v, wq_v), (dk_v, wk_v), (dv_v, wv_v))):
            value = source[...].T if index == 0 else source[...]
            high, low = split(value)
            x_v[0, :, pl.ds(index * D, D)] = high
            x_v[1, :, pl.ds(index * D, D)] = low
            result = result + folded(dot_rows(jnp.concatenate([high, low], axis=0), weight[...]))
        y_v[...] = result
        t_v[...] = tile_of([total_mixed / alphas[0, 0], total_inner / alphas[0, 1]])
        stores += start_all(
            [
                pltpu.make_async_copy(y_v, sent, out_sem.at[2]),
                pltpu.make_async_copy(y_v, passed.at[micro], out_sem.at[3]),
                pltpu.make_async_copy(x_v, spreads.at[micro], out_sem.at[4]),
                pltpu.make_async_copy(t_v, small.at[micro], out_sem.at[5]),
            ]
        )
        wait_all(stores)


def inner_body(count, sizes, axis, *refs):
    info, saved_m, befores = refs[:3]
    slots, refs = refs[4 : 4 + count], refs[5 + count :]
    m_v, lt_v, r_v, w_v, in_sem, r_sem, out_sem = refs
    rows = m_v.shape[1]

    def loads(part):
        copies = []
        for micro in range(2):
            for half in range(2):
                source = befores.at[micro, half, :, pl.ds(part * 512, 512)]
                target = r_v.at[part, half, pl.ds(micro * rows, rows)]
                copies.append(pltpu.make_async_copy(source, target, r_sem.at[part, micro * 2 + half]))
        return copies

    first = pltpu.make_async_copy(saved_m, m_v, in_sem.at[0])
    first.start()
    for part in range(4):
        start_all(loads(part))
    first.wait()
    turn_left(lt_v, m_v, True)
    stores = []
    for part in range(4):
        wait_all(loads(part))
        put_part(w_v, part, three_dots(lt_v[0], lt_v[1], r_v[part, 0], r_v[part, 1]))
        stores += start_all(slot_copies(info, sizes, axis, w_v, slots, out_sem, part))
    wait_all(stores)


def turn_left(target, source, transpose):
    rows = target.shape[2] // 2
    for micro in range(2):
        high, low = split(source[micro].T if transpose else source[micro])
        target[0, :, micro * rows : (micro + 1) * rows] = high
        target[1, :, micro * rows : (micro + 1) * rows] = low


def attention_body(count, sizes, axis, *refs):
    info, valids, saved_s, saved_o, spreads, firsts, sums, small = refs[:8]
    slots, refs = refs[9 : 9 + count], refs[10 + count :]
    (s_v, o_v, st_v, lo_v, r_v, w_v, n_v, t_v, in_sem, r_sem, out_sem) = refs
    rows = s_v.shape[1]

    def loads(part):
        copies = []
        for micro in range(2):
            for half in range(2):
                if part < 3:
                    source = spreads.at[micro, half, :, pl.ds(part * 512, 512)]
                else:
                    source = firsts.at[micro, half]
                target = r_v.at[part, half, pl.ds(micro * rows, rows)]
                copies.append(pltpu.make_async_copy(source, target, r_sem.at[part, micro * 2 + half]))
        return copies

    lefts = [pltpu.make_async_copy(saved_s, s_v, in_sem.at[0]), pltpu.make_async_copy(saved_o, o_v, in_sem.at[1])]
    tiles = [
        pltpu.make_async_copy(sums, n_v.at[pl.ds(0, 2)], in_sem.at[2]),
        pltpu.make_async_copy(small, n_v.at[pl.ds(2, 2)], in_sem.at[3]),
    ]
    start_all(lefts + tiles)
    for part in range(4):
        start_all(loads(part))
    lefts[0].wait()
    turn_left(st_v, s_v, True)
    stores = []
    for part in range(4):
        if part == 3:
            lefts[1].wait()
            turn_left(lo_v, o_v, False)
        left = lo_v if part == 3 else st_v
        wait_all(loads(part))
        put_part(w_v, part, three_dots(left[0], left[1], r_v[part, 0], r_v[part, 1]))
        stores += start_all(slot_copies(info, sizes, axis, w_v, slots, out_sem, part))
    wait_all(tiles)
    lane = lax.broadcasted_iota(jnp.int32, (8, 256), 1)
    tile = jnp.where(lane == 3, jnp.sum(valids[...].astype(jnp.float32)), jnp.zeros((8, 256), jnp.float32))
    for index in range(3):
        tile = jnp.where(lane == index, n_v[0, 0, index] + n_v[1, 0, index], tile)
    for index in range(2):
        tile = jnp.where(lane == 4 + index, n_v[2, 0, index] + n_v[3, 0, index], tile)
    t_v[...] = tile
    unit_rows = w_v.shape[3]
    for by in range(count):

        @pl.when(lax.rem(info[1 + axis] + by, sizes[axis]) == 0)
        def _():
            target = slots[by].at[0, 0, 0, pl.ds(unit_rows, 8), pl.ds(0, 256)]
            copy = pltpu.make_async_copy(t_v, target, in_sem.at[0])
            copy.start()
            copy.wait()

    wait_all(stores)


def call(body, name, free, inputs, specs, outs, scratch, before, flops, limit):
    extra = list(before) if before is not None else []
    inputs = list(inputs[:free]) + in_hbm(list(inputs[free:])) + [TOKEN[0]]
    results = pl.pallas_call(
        functools.partial(body, len(extra)),
        out_shape=outs + [loose(8, 128)],
        in_specs=specs + [ANY] * (len(inputs) - len(specs) + len(extra)),
        out_specs=[ANY] * (len(outs) + 1),
        scratch_shapes=scratch,
        input_output_aliases={len(inputs) + i: i for i in range(len(extra))},
        compiler_params=pltpu.CompilerParams(vmem_limit_bytes=limit * 1024 * 1024),
        cost_estimate=pl.CostEstimate(flops=flops, bytes_accessed=2 * 10**7, transcendentals=10**6),
        name=name,
    )(*inputs, *in_hbm(extra))
    TOKEN[0] = results[-1]
    return results[:-1]


def backward_back(info, alphas, upstreams, targets, before, sizes, axis):
    micros, rows, inner = before.shape
    parts = inner // 512
    vmem, dma = pltpu.VMEM, pltpu.SemaphoreType.DMA
    f32, bf16 = jnp.float32, jnp.bfloat16
    slots = slot_structs(sizes, axis)
    scratch = [
        vmem((micros, rows, D), f32),
        vmem((2, micros * rows, D), bf16),
        vmem((parts, micros * rows, 512), f32),
        vmem(unit_shape(sizes), f32),
        dma((parts + 1, 2)),
        dma((parts, copy_count(sizes, axis))),
    ]

    def body(extra, *refs):
        back_body(len(slots), sizes, axis, *refs)

    inputs = [info, alphas] + list(upstreams) + [targets, before]
    return call(body, "grad_back", 4, inputs, [SCALARS, SCALARS], slots, scratch, None, 5 * 10**9, 24)


def backward_inner(info, middle, befores, sizes, axis):
    micros, rows, _ = middle.shape
    vmem, dma = pltpu.VMEM, pltpu.SemaphoreType.DMA
    f32, bf16 = jnp.float32, jnp.bfloat16
    slots = slot_structs(sizes, axis)
    scratch = [
        vmem(middle.shape, f32),
        vmem((2, D, micros * rows), bf16),
        vmem((4, 2, micros * rows, 512), bf16),
        vmem(unit_shape(sizes), f32),
        dma((1,)),
        dma((4, 4)),
        dma((4, copy_count(sizes, axis))),
    ]

    def body(extra, *refs):
        inner_body(len(slots), sizes, axis, *refs)

    return call(body, "grad_inner", 1, [info, middle, befores], [SCALARS], slots, scratch, None, 5 * 10**9, 24)


def backward_attention(info, valids, stream, mixed, spreads, firsts, sums, small, sizes, axis):
    micros, rows, _ = stream.shape
    vmem, dma = pltpu.VMEM, pltpu.SemaphoreType.DMA
    f32, bf16 = jnp.float32, jnp.bfloat16
    slots = slot_structs(sizes, axis, 8)
    scratch = [
        vmem(stream.shape, f32),
        vmem(mixed.shape, f32),
        vmem((2, D, micros * rows), bf16),
        vmem((2, D, micros * rows), bf16),
        vmem((4, 2, micros * rows, 512), bf16),
        vmem(unit_shape(sizes), f32),
        vmem((4, 8, 128), f32),
        vmem((8, 256), f32),
        dma((4,)),
        dma((4, 4)),
        dma((4, copy_count(sizes, axis))),
    ]

    def body(extra, *refs):
        attention_body(len(slots), sizes, axis, *refs)

    inputs = [info, valids, stream, mixed, spreads, firsts, sums, small]
    return call(body, "grad_attention", 2, inputs, [SCALARS, LOCAL], slots, scratch, None, 5 * 10**9, 28)


def backward_chain(turn, micro, info, alphas, segments, valids, upstream, before, saved, weights, previous):
    micros, rows, inner = before.shape
    parts = inner // 512
    vmem, dma = pltpu.VMEM, pltpu.SemaphoreType.DMA
    f32, bf16 = jnp.float32, jnp.bfloat16
    wq, wk, wv, wo, wi, wb = weights
    outs = [
        pltpu.HBM((micros, 2, rows, inner), bf16),
        pltpu.HBM((micros, 2, rows, 3 * D), bf16),
        pltpu.HBM((micros, 2, rows, D), bf16),
        struct(micros, rows, D),
        struct(micros, 8, 128),
        struct(rows, D),
    ]
    scratch = [
        vmem((rows, D), f32),
        vmem((parts, rows, 512), f32),
        vmem((parts, D, 512), bf16),
        vmem((parts, 512, D), bf16),
        vmem((2 * rows, D), bf16),
        vmem((rows, D), f32),
        vmem((2, rows, inner), bf16),
    ]
    scratch += [vmem(x.shape[1:], f32) for x in saved] + [vmem((D, D), bf16)] * 4
    scratch += [
        vmem((rows, rows), f32),
        vmem((rows, D), f32),
        vmem((D, rows), f32),
        vmem((HEADS // 2, 8, rows), f32),
        vmem((D, rows), f32),
        vmem((rows, D), f32),
        vmem((rows, D), f32),
        vmem((2, rows, 3 * D), bf16),
        vmem((2, rows, D), bf16),
        vmem((rows, D), f32),
        vmem((8, 128), f32),
        dma((6,)),
        dma((parts, 3)),
        dma((4,)),
        dma((6,)),
    ]

    def body(extra, *refs):
        chain_body(turn, micro, extra, *refs)

    inputs = [info, alphas, segments, valids, upstream, before] + list(saved) + [wi, wb, wq, wk, wv, wo]
    return call(
        body, "grad_chain", 5, inputs, [SCALARS, SCALARS, LOCAL, LOCAL], outs, scratch, previous, 2 * 10**10, 36
    )


def local_call(body, name, info, inputs, outs, scratch, specs=None):
    inputs = [info, TOKEN[0]] + list(inputs)

    def parted(*refs):
        first = len(inputs)
        body(refs[0], refs[2:first], refs[first : first + len(outs)], refs[first + len(outs) + 1 :])

    results = pl.pallas_call(
        parted,
        out_shape=list(outs) + [loose(8, 128)],
        in_specs=[SCALARS] + [ANY] * (len(inputs) - 1),
        out_specs=(specs or [ANY] * len(outs)) + [ANY],
        scratch_shapes=scratch,
        compiler_params=pltpu.CompilerParams(vmem_limit_bytes=12 * 1024 * 1024),
        cost_estimate=pl.CostEstimate(flops=10**6, bytes_accessed=6 * 10**6, transcendentals=0),
        name=name,
    )(*inputs)
    TOKEN[0] = results[-1]
    return results[:-1]


def left_dims(done):
    return [axis for axis in (3, 2, 1, 0) if axis not in done]


def picked(ref, dims, axis, index):
    return ref.at[(slice(None),) * dims.index(axis) + (index,)]


def reduce_stage(sizes, order, step, info, arrays):
    shape = arrays[0].shape
    count = len(arrays)
    dims = left_dims(order[:step])
    parting = step < len(order) - 1
    if parting:
        axis = order[step]
        at = dims.index(axis)
        outs = [loose(*shape[:at], *shape[at + 1 :])] * sizes[axis]
    else:
        outs = [loose(*shape)]

    def body(info, ins, outs, scratch):
        held, sem = scratch
        wait_all(start_all([pltpu.make_async_copy(ref, held.at[i], sem.at[i]) for i, ref in enumerate(ins)]))
        total = held[0]
        for i in range(1, count):
            total = total + held[i]
        held[0] = total
        stores = []
        for by in range(len(outs)):
            source = held.at[0]
            if parting:
                source = picked(source, dims, axis, lax.rem(info[1 + axis] + by, sizes[axis]))
            stores.append(pltpu.make_async_copy(source, outs[by], sem.at[count + by]))
        wait_all(start_all(stores))

    scratch = [pltpu.VMEM((count,) + shape, jnp.float32), pltpu.SemaphoreType.DMA((count + len(outs),))]
    return local_call(body, "reduce_step", info, arrays, outs, scratch)


def place_stage(sizes, order, step, info, arrays):
    axis = order[step]
    dims = left_dims(order[:step])
    at = dims.index(axis)
    shape = arrays[0].shape
    count = sizes[axis]

    def body(info, ins, outs, scratch):
        copies = []
        for by in range(count):
            target = picked(outs[0], dims, axis, lax.rem(info[1 + axis] + count - by, count))
            copies.append(pltpu.make_async_copy(ins[by], target, scratch[0].at[by]))
        wait_all(start_all(copies))

    out = loose(*shape[:at], count, *shape[at:])
    return local_call(body, "place_step", info, arrays, [out], [pltpu.SemaphoreType.DMA((count,))])[0]


def last_stage(sizes, order, info, arrays, kind):
    x, y, near, far = sizes
    rows = unit_shape(sizes)[3]
    depth = near * far // 4
    axis = order[0]
    count = sizes[axis]
    specs, scratch = None, [pltpu.SemaphoreType.DMA((near * far * count + 1,))]
    if kind == "rows":
        shapes = [struct(near * far, y, x, rows, D)]
    elif kind == "columns":
        shapes = [struct(depth, y, x, rows, 4 * D)]
    else:
        shapes = [struct(depth, y, x, rows, D)] * 4 + [loose(1, 2), loose(1, 3)]
        specs = [ANY] * 4 + [LOCAL] * 2
        scratch += [pltpu.VMEM((8, 256), jnp.float32)]

    def body(info, ins, outs, scratch):
        sem = scratch[0]
        copies = []

        def put(source, target):
            copies.append(pltpu.make_async_copy(source, target, sem.at[len(copies)]))

        for by in range(count):
            place = lax.rem(info[1 + axis] + count - by, count)
            if axis == 2:
                for at in range(far):
                    put(ins[by].at[at], outs[0].at[at * near + place])
                continue
            for at in range(near * far):
                source = ins[by].at[at // near, at % near, :, pl.ds(0, rows)]
                part, inside = at // depth, at % depth
                out = outs[part] if kind == "four" else outs[0]
                lanes = pl.ds(part * D if kind == "columns" else 0, D)
                inside = at if kind == "rows" else inside
                put(source, out.at[inside, :, place, :, lanes] if axis == 0 else out.at[inside, place, :, :, lanes])
        start_all(copies)
        if kind == "four":
            tile_v = scratch[1]
            for by in range(count):

                @pl.when(info[1 + axis] == by)
                def _():
                    source = ins[by].at[0, 0, 0, pl.ds(rows, 8), pl.ds(0, 256)]
                    copy = pltpu.make_async_copy(source, tile_v, sem.at[len(copies)])
                    copy.start()
                    copy.wait()

            tile = tile_v[0:1, 0:128]
            outs[-2][...] = tile[:, 4:6]
            outs[-1][...] = jnp.sqrt(tile[:, 0:3] / (jnp.maximum(tile[:, 3:4], 1.0) * D))
        wait_all(copies)

    return local_call(body, "place_last", info, arrays, shapes, scratch, specs)


def extents(count):
    bits = count.bit_length() - 1
    if 1 << bits != count:
        return (1, 1, 1, count)
    side = 1 << (bits // 3)
    depth = count // (side * side)
    near = 2 if depth > 1 else 1
    return (side, side, near, depth // near)


def shifted(value, axis, by, sizes):
    count = math.prod(sizes)
    stride, length = math.prod(sizes[:axis]), sizes[axis]
    pairs = []
    for chip in range(count):
        along = (chip // stride) % length
        pairs.append((chip, chip + ((along + by) % length - along) * stride))
    return lax.ppermute(value, "dp", pairs)


def summing(slots, order, kind, sizes, info):
    pieces = list(slots)
    steps = len(order)
    for step in range(1, steps + 1):
        axis = order[step - 1]
        pieces = [pieces[0]] + [
            shifted(pieces[by if step < steps else 0], axis, by, sizes) for by in range(1, sizes[axis])
        ]
        yield
        pieces = reduce_stage(sizes, order, step, info, pieces)
    whole = pieces[0]
    for step in range(steps - 2, -1, -1):
        axis = order[step]
        copies = [whole] + [shifted(whole, axis, by, sizes) for by in range(1, sizes[axis])]
        yield
        if step:
            whole = place_stage(sizes, order, step, info, copies)
    yield last_stage(sizes, order, info, copies, kind)


def shards(stream_in, cotangent, segment_ids, pad_mask, w_query, w_key, w_value, w_out, w_in, w_back, alphas):
    weights = [weight[0] for weight in (w_query, w_key, w_value, w_out, w_in, w_back)]
    streams = stream_in[:, 0]
    sizes = extents(lax.axis_size("dp"))
    chip = lax.axis_index("dp")
    section = lax.axis_index("section")
    places, left = [], chip
    for size in sizes:
        places.append(lax.rem(left, size))
        left = lax.div(left, size)
    info = jnp.stack([section] + places).astype(jnp.int32)
    received, state = None, None
    for tick in range(3):
        sent, state = forward_tick(tick, info, alphas, segment_ids, pad_mask, streams, received, weights, state)
        if tick < 2:
            received = lax.ppermute(sent, "section", [(0, 1)])
    acts, saved_s, saved_q, saved_k, saved_v, saved_o, saved_l, saved_m, saved_p, sums = state
    saved = (saved_q, saved_k, saved_v, saved_o, saved_l)
    TOKEN[0] = jnp.zeros((8, 128), jnp.float32)

    def chain_step(turn, micro, upstream, previous):
        return backward_chain(
            turn, micro, info, alphas, segment_ids, pad_mask, upstream, saved_p, saved, weights, previous
        )

    orders = {"back": (2, 0, 1, 3), "inner": (0, 1, 2, 3), "attention": (1, 2, 0, 3)}
    chain, upstreams = None, []
    for micro in range(2):
        chain = chain_step(0, micro, cotangent, chain)
        upstreams.append(lax.ppermute(chain[5], "section", [(1, 0)]))
        chain = chain[:5]
    for micro in range(2):
        chain = chain_step(1, micro, upstreams[micro], chain)[:5]
    befores, spreads, firsts, passed, small = chain
    order = orders["back"]
    slots = backward_back(info, alphas, upstreams, cotangent, saved_p, sizes, order[0])
    back = summing(slots, order, "rows", sizes, info)
    next(back)
    order = orders["inner"]
    slots = backward_inner(info, saved_m, befores, sizes, order[0])
    inner = summing(slots, order, "columns", sizes, info)
    next(inner)
    order = orders["attention"]
    slots = backward_attention(info, pad_mask, saved_s, saved_o, spreads, firsts, sums, small, sizes, order[0])
    attention = summing(slots, order, "four", sizes, info)
    next(attention)
    for _ in range(7):
        back_out = next(back)
        inner_out = next(inner)
        attention_out = next(attention)
    return (
        acts[None, :, None],
        passed[None, :, None],
        attention_out[0].reshape(1, D, D),
        attention_out[1].reshape(1, D, D),
        attention_out[2].reshape(1, D, D),
        attention_out[3].reshape(1, D, D),
        inner_out[0].reshape(1, D, -1),
        back_out[0].reshape(1, -1, D),
        attention_out[4],
        attention_out[5],
    )


def solution(mesh):
    in_specs = (
        P(None, "dp", None, None),
        P(None, "dp", None, None),
        P(None, "dp", None),
        P(None, "dp", None),
        P("section", None, None),
        P("section", None, None),
        P("section", None, None),
        P("section", None, None),
        P("section", None, None),
        P("section", None, None),
        P("section", None),
    )
    out_specs = (
        P("section", None, "dp", None, None),
        P("section", None, "dp", None, None),
        P("section", None, None),
        P("section", None, None),
        P("section", None, None),
        P("section", None, None),
        P("section", None, None),
        P("section", None, None),
        P("section", None),
        P("section", None),
    )
    return jax.shard_map(shards, mesh=mesh, in_specs=in_specs, out_specs=out_specs, check_vma=False)
```

```python
import functools
import math
import jax
import jax.numpy as jnp
from jax import lax
from jax.experimental import pallas as pl
from jax.experimental.pallas import tpu as pltpu
from jax.sharding import PartitionSpec as P

D = 512
HEADS = 8
HEAD_DIM = 64
GELU_A = math.sqrt(2.0 / math.pi)
GELU_B = 0.044715
ORDERS = {"B": "nxyf", "b": "xnyf", "I": "yxnf", "i": "nyxf", "A": "xnyf", "a": "xynf"}
PROGRAM = "|Bb|Bb|IaibBbBAaIaBbiaIbABiIbaiAIAaBiIAaiAIBiAbaIiA"


TOKEN = [None]


def start_all(copies):
    for copy in copies:
        copy.start()
    return copies


def wait_all(copies):
    for copy in copies:
        copy.wait()


def split(value):
    high = value.astype(jnp.bfloat16)
    low = (value - high.astype(jnp.float32)).astype(jnp.bfloat16)
    return (high, low)


def stacked(value):
    return jnp.concatenate(split(value), axis=0)


def dot(left_side, right_side):
    return jnp.dot(left_side, right_side, preferred_element_type=jnp.float32)


def dot_rows(left_side, right_side):
    return lax.dot_general(
        left_side, right_side, (((1,), (1,)), ((), ())), preferred_element_type=jnp.float32
    )


def folded(product):
    half = product.shape[0] // 2
    return product[:half] + product[half:]


def put_split(target, value):
    high, low = split(value)
    target[0] = high
    target[1] = low


def two_dots(left_side, right_side):
    return dot(left_side[0], right_side) + dot(left_side[1], right_side)


def gelu_inner(value):
    return jnp.tanh(GELU_A * (value + GELU_B * (value * value * value)))


def tile_of(numbers):
    lane = lax.broadcasted_iota(jnp.int32, (8, 128), 1)
    tile = jnp.zeros((8, 128), jnp.float32)
    for index, number in enumerate(numbers):
        tile = jnp.where(lane == index, number, tile)
    return tile


def fill_bias(bias_ref, segment_row, valid_row):
    blocks = segment_row.shape[1] // 128
    segment_col = jnp.broadcast_to(segment_row, (128, segment_row.shape[1])).T
    valid_col = jnp.broadcast_to(valid_row, (128, valid_row.shape[1])).T
    for kb in range(blocks):
        ks = slice(kb * 128, kb * 128 + 128)
        for qb in range(kb, blocks):
            qs = slice(qb * 128, qb * 128 + 128)
            k_place = lax.broadcasted_iota(jnp.int32, (128, 128), 0) + kb * 128
            q_place = lax.broadcasted_iota(jnp.int32, (128, 128), 1) + qb * 128
            allowed = (segment_col[ks] == segment_row[:, qs]) & (k_place <= q_place)
            allowed = allowed & ((valid_col[ks] > 0) | (k_place == q_place))
            bias_ref[ks, qs] = jnp.where(allowed, 0.0, -1e30)


def halves_of(value):
    lane = lax.broadcasted_iota(jnp.int32, value.shape, 1)
    zero = jnp.zeros_like(value)
    return (jnp.where(lane < HEAD_DIM, value, zero), jnp.where(lane < HEAD_DIM, zero, value))


def pair_scores(keys_cat, queries_high, queries_low):
    sides = []
    for high, low in zip(halves_of(queries_high), halves_of(queries_low)):
        sides.append(jnp.concatenate([high, high, low], axis=1))
    return dot_rows(keys_cat, jnp.concatenate(sides, axis=0))


def three_lanes(value):
    high, low = split(value)
    return jnp.concatenate([high, low, high], axis=1)


def fetch_rows(alphas, segments, valids, alphas_s, rows_v, sem):
    return start_all(
        [
            pltpu.make_async_copy(alphas, alphas_s, sem.at[0]),
            pltpu.make_async_copy(segments, rows_v.at[0], sem.at[1]),
            pltpu.make_async_copy(valids, rows_v.at[1], sem.at[2]),
        ]
    )


def forward_body(tick, *refs):
    (info, alphas, segments, valids, streams, wq, wk, wv, wo, wi, wb) = refs[:11]
    received = streams.at[0, 0] if tick == 0 else refs[12]
    refs = refs[12 + (0 if tick == 0 else 11) :]
    (acts, sent, saved_s, saved_q, saved_k, saved_v, saved_o, saved_l, saved_m, saved_p, sums, _) = refs[:12]
    (s_v, wq_v, wk_v, wv_v, wo_v, wi_v, wb_v, q_v, k_v, v_v, ot_v, l_v, m_v, p_v, a_v, t_v, bias_v, x_v, alphas_s, rows_v, in_sem, out_sem, row_sem) = refs[12:]
    section = info[0]
    micro = tick - section
    rows = s_v.shape[0]
    blocks = rows // 128
    parts = wi_v.shape[1] // 512

    @pl.when((micro >= 0) & (micro < 2))
    def _():
        pairs = [(wq, wq_v), (wk, wk_v), (wv, wv_v), (wo, wo_v), (wi, wi_v), (wb, wb_v)]
        loads = [pltpu.make_async_copy(a, b, in_sem.at[i]) for i, (a, b) in enumerate(pairs)]

        @pl.when(section == 0)
        def _():
            pltpu.make_async_copy(streams.at[micro, 0], s_v, in_sem.at[6]).start()

        @pl.when(section != 0)
        def _():
            pltpu.make_async_copy(received, s_v, in_sem.at[6]).start()

        loads[0].start()
        small = fetch_rows(alphas, segments, valids, alphas_s, rows_v, row_sem)
        pltpu.make_async_copy(received, s_v, in_sem.at[6]).wait()
        start_all(loads[1:])
        put_split(x_v, s_v[...])
        for index, (weight, target) in enumerate(((wq_v, q_v), (wk_v, k_v), (wv_v, v_v))):
            loads[index].wait()
            value = two_dots(x_v, weight[...])
            target[...] = value * 0.125 if index == 0 else value
        wait_all(small)
        segment_row = rows_v[0, micro].astype(jnp.float32)
        valid_row = rows_v[1, micro].astype(jnp.float32)
        fill_bias(bias_v, segment_row, valid_row)

        stores = []

        def store(source, target):
            copy = pltpu.make_async_copy(source, target, out_sem.at[len(stores)])
            copy.start()
            stores.append(copy)

        store(s_v, saved_s.at[micro])
        store(q_v, saved_q.at[micro])
        store(k_v, saved_k.at[micro])
        store(v_v, saved_v.at[micro])
        made = {}

        def scores_of(pair, qb):
            lanes = pl.ds(pair * 128, 128)
            if pair not in made:
                made.clear()
                made[pair] = (three_lanes(k_v[:, lanes]), split(q_v[:, lanes]), split(v_v[:, lanes].T))
            keys_cat, queries, values = made[pair]
            qs = slice(qb * 128, qb * 128 + 128)
            return pair_scores(keys_cat[: (qb + 1) * 128], queries[0][qs], queries[1][qs]), values

        units = [(pair, qb) for pair in range(HEADS // 2) for qb in range(blocks)]
        ahead = scores_of(*units[0])
        for index, (pair, qb) in enumerate(units):
            scores, (values_high, values_low) = ahead
            if index + 1 < len(units):
                ahead = scores_of(*units[index + 1])
            qs = slice(qb * 128, qb * 128 + 128)
            ks = (qb + 1) * 128
            bias = bias_v[:ks, qs]
            for head in range(2):
                part = scores[:, head * 128 : head * 128 + 128] + bias
                top = jnp.max(part, axis=0, keepdims=True)
                probs = jnp.exp(part - top)
                total = jnp.sum(probs, axis=0, keepdims=True)
                high, low = split(probs)
                hs = slice(head * HEAD_DIM, head * HEAD_DIM + HEAD_DIM)
                both = jnp.concatenate([values_high[hs, :ks], values_low[hs, :ks]], axis=0)
                mixed = folded(dot(both, high)) + dot(values_high[hs, :ks], low)
                at = slice(pair * 128 + head * HEAD_DIM, pair * 128 + head * HEAD_DIM + HEAD_DIM)
                ot_v[at, qs] = mixed / total
                l_v[pair, head : head + 1, qs] = top + jnp.log(total)
        store(ot_v, saved_o.at[micro])
        store(l_v, saved_l.at[micro])
        put_split(x_v, ot_v[...].T)
        loads[3].wait()
        attn = two_dots(x_v, wo_v[...]) * alphas_s[0, 0]
        valid_col = jnp.broadcast_to(valid_row, (128, rows)).T
        weighting = jnp.concatenate([valid_col] * (D // 128), axis=1)
        attn_sum = jnp.sum(attn * attn * weighting)
        middle = s_v[...] + attn
        m_v[...] = middle
        store(m_v, saved_m.at[micro])
        put_split(x_v, middle)
        loads[4].wait()

        def before_of(part):
            return two_dots(x_v, wi_v[:, part * 512 : part * 512 + 512])

        ahead = before_of(0)
        loads[5].wait()
        for part in range(parts):
            cols = slice(part * 512, part * 512 + 512)
            before = ahead
            p_v[:, cols] = before
            store(p_v.at[:, pl.ds(part * 512, 512)], saved_p.at[micro, :, pl.ds(part * 512, 512)])
            if part + 1 < parts:
                ahead = before_of(part + 1)
            high, low = split(0.5 * before * (1.0 + gelu_inner(before)))
            more = dot(high, wb_v[cols, :]) + dot(low, wb_v[cols, :])
            a_v[...] = a_v[...] + more if part else more
        ffn = a_v[...] * alphas_s[0, 1]
        result = m_v[...] + ffn
        a_v[...] = result
        store(a_v, sent)
        store(a_v, acts.at[micro])
        t_v[...] = tile_of([jnp.sum(result * result * weighting), attn_sum, jnp.sum(ffn * ffn * weighting)])
        store(t_v, sums.at[micro])
        wait_all(stores)


def struct(*shape):
    return pltpu.HBM(shape, jnp.float32)


def loose(*shape):
    return jax.ShapeDtypeStruct(shape, jnp.float32)


def in_hbm(arrays):
    return [pltpu.with_memory_space_constraint(array, pltpu.HBM) for array in arrays]


ANY = pl.BlockSpec(memory_space=pl.ANY)
SCALARS = pl.BlockSpec(memory_space=pltpu.SMEM)
LOCAL = pl.BlockSpec(memory_space=pltpu.VMEM)


def forward_tick(tick, info, alphas, segments, valids, streams, received, weights, state):
    micro_count, _, rows, width = streams.shape
    inner = weights[4].shape[1]
    whole = struct(micro_count, rows, width)
    shapes = [
        whole,
        struct(rows, width),
        whole,
        whole,
        whole,
        whole,
        struct(micro_count, width, rows),
        struct(micro_count, HEADS // 2, 8, rows),
        whole,
        struct(micro_count, rows, inner),
        struct(micro_count, 8, 128),
        loose(8, 128),
    ]
    kept = [0, 2, 3, 4, 5, 6, 7, 8, 9, 10]
    extra = [] if state is None else [received] + in_hbm(state)
    aliases = {} if state is None else {13 + i: out for i, out in enumerate(kept)}
    f32, bf16 = jnp.float32, jnp.bfloat16
    vmem, dma = pltpu.VMEM, pltpu.SemaphoreType.DMA
    scratch = [vmem((rows, width), f32)] + [vmem(w.shape, bf16) for w in weights]
    scratch += [vmem((rows, width), f32)] * 3 + [vmem((width, rows), f32), vmem((HEADS // 2, 8, rows), f32)]
    scratch += [vmem((rows, width), f32), vmem((rows, inner), f32), vmem((rows, width), f32)]
    scratch += [vmem((8, 128), f32), vmem((rows, rows), f32), vmem((2, rows, width), bf16)]
    scratch += [pltpu.SMEM(alphas.shape, f32), vmem((2,) + segments.shape, jnp.int32)]
    scratch += [dma((7,)), dma((10 + inner // 512,)), dma((3,))]
    outs = pl.pallas_call(
        functools.partial(forward_body, tick),
        out_shape=shapes,
        in_specs=[SCALARS] + [ANY] * (11 + len(extra)),
        out_specs=[ANY] * len(shapes),
        scratch_shapes=scratch,
        input_output_aliases=aliases,
        compiler_params=pltpu.CompilerParams(vmem_limit_bytes=28 * 1024 * 1024),
        cost_estimate=pl.CostEstimate(flops=10**10, bytes_accessed=2 * 10**7, transcendentals=10**6),
        name="layer_forward",
    )(info, *in_hbm([alphas, segments, valids, streams, *weights]), TOKEN[0], *extra)
    TOKEN[0] = outs[-1]
    return (outs[1], [outs[i] for i in kept])


def unit_shape(sizes):
    x, y, near, far = sizes
    return (near * far, y, x, 4 * D // (x * y * near * far), D)


def slot_structs(sizes, axes, more=0):
    x, y, near, far = sizes
    structs = []
    for axis in axes:
        shape = [size for index, size in ((3, far), (2, near), (1, y), (0, x)) if index != axis]
        structs += [struct(*shape, unit_shape(sizes)[3] + (0 if structs else more), D // len(axes))] * sizes[axis]
    return structs


def put_part(unit, part, value):
    depth = unit.shape[0] // 4
    unit[pl.ds(part * depth, depth)] = value.reshape((depth,) + unit.shape[1:])


def slot_copies(info, sizes, axes, unit, slots, sems, part):
    x, y, near, far = sizes
    depth, rows = near * far // 4, unit.shape[3]
    copies, first = [], 0
    for half, axis in enumerate(axes):
        lanes = pl.ds(half * (D // len(axes)), D // len(axes))
        for by in range(sizes[axis]):
            place = lax.rem(info[1 + axis] + by, sizes[axis])
            slot = slots[first + by]
            if axis == 2:
                pairs = [
                    (unit.at[at * near + place, :, :, :, lanes], slot.at[at, :, :, pl.ds(0, rows)])
                    for at in range(far)
                    if part * depth < (at + 1) * near <= (part + 1) * depth
                ]
            else:
                pairs = []
                for at in range(part * depth, (part + 1) * depth):
                    source = unit.at[at, :, place, :, lanes] if axis == 0 else unit.at[at, place, :, :, lanes]
                    pairs.append((source, slot.at[at // near, at % near, :, pl.ds(0, rows)]))
            for source, target in pairs:
                copies.append(pltpu.make_async_copy(source, target, sems.at[part, len(copies)]))
        first += sizes[axis]
    return copies


def copy_count(sizes, axes):
    return sum(sizes[axis] for axis in axes) * max(1, sizes[2] * sizes[3] // 4)


def three_dots(left_high, left_low, right_high, right_low):
    return dot(left_high, right_high) + dot(left_low, right_high) + dot(left_high, right_low)


def back_body(count, sizes, axes, *refs):
    info, alphas = refs[:2]
    upstreams, targets, saved_p = refs[2:4], refs[4], refs[5]
    slots, refs = refs[7 : 7 + count], refs[8 + count :]
    g_v, gh_v, p_v, w_v, in_sem, out_sem = refs
    parts = p_v.shape[0]
    rows = g_v.shape[1]

    def load(part, micro):
        cols = pl.ds(part * 512, 512)
        return pltpu.make_async_copy(
            saved_p.at[micro, :, cols], p_v.at[part, pl.ds(micro * rows, rows)], in_sem.at[part, micro]
        )

    for micro in range(2):

        @pl.when(info[0] == 0)
        def _():
            pltpu.make_async_copy(upstreams[micro], g_v.at[micro], in_sem.at[parts, micro]).start()

        @pl.when(info[0] != 0)
        def _():
            pltpu.make_async_copy(targets.at[micro, 0], g_v.at[micro], in_sem.at[parts, micro]).start()

    start_all([load(0, micro) for micro in range(2)])
    for micro in range(2):
        pltpu.make_async_copy(targets.at[micro, 0], g_v.at[micro], in_sem.at[parts, micro]).wait()
    for part in range(1, parts):
        start_all([load(part, micro) for micro in range(2)])
    high, low = split(jnp.concatenate([g_v[0], g_v[1]], axis=0) * alphas[0, 1])
    gh_v[0] = high
    gh_v[1] = low

    def left_of(part):
        for micro in range(2):
            load(part, micro).wait()
        before = p_v[part].T
        return split(0.5 * before * (1.0 + gelu_inner(before)))

    stores = []
    ahead = left_of(0)
    for part in range(parts):
        high, low = ahead
        if part + 1 < parts:
            ahead = left_of(part + 1)
        put_part(w_v, part, three_dots(high, low, gh_v[0], gh_v[1]))
        stores += start_all(slot_copies(info, sizes, axes, w_v, slots, out_sem, part))
    wait_all(stores)


def chain_body(tick, extra, *refs):
    info, received = refs[:2]
    alphas, segments, valids, targets, saved_p = refs[2:7]
    sources = refs[7:12]
    wi, wb = refs[12:14]
    weights = refs[14:18]
    refs = refs[19 + extra :]
    (befores, spreads, firsts, passed, small, sent, _) = refs[:7]
    (g_v, p_v, wi_v, wb_v, gs_v, d_v, b_v) = refs[7:14]
    held = refs[14:19]
    weights_v = refs[19:23]
    (bias_v, do_v, dt_v, dl_v, qt_v, dk_v, dv_v, x_v, f_v, y_v, t_v, alphas_s, rows_v, in_sem, part_sem, w_sem, out_sem, row_sem) = refs[23:]
    parts = p_v.shape[0]
    rows = bias_v.shape[0]
    blocks = rows // 128
    (q_v, k_v, v_v, o_v, l_v) = held
    (wq_v, wk_v, wv_v, wo_v) = weights_v
    section = info[0]
    micro = tick - (1 - section)

    @pl.when((micro >= 0) & (micro < 2))
    def _():
        def loads(part):
            cols = pl.ds(part * 512, 512)
            return [
                pltpu.make_async_copy(wb.at[cols], wb_v.at[part], part_sem.at[part, 0]),
                pltpu.make_async_copy(saved_p.at[micro, :, cols], p_v.at[part], part_sem.at[part, 1]),
                pltpu.make_async_copy(wi.at[:, cols], wi_v.at[part], part_sem.at[part, 2]),
            ]

        @pl.when(section == 0)
        def _():
            pltpu.make_async_copy(received if tick else targets.at[micro, 0], g_v, in_sem.at[5]).start()

        @pl.when(section != 0)
        def _():
            pltpu.make_async_copy(targets.at[micro, 0], g_v, in_sem.at[5]).start()

        rows_in = fetch_rows(alphas, segments, valids, alphas_s, rows_v, row_sem)
        start_all(loads(0))
        fetches = [pltpu.make_async_copy(a, b, w_sem.at[i]) for i, (a, b) in enumerate(zip(weights, weights_v))]
        later = [pltpu.make_async_copy(a.at[micro], b, in_sem.at[i]) for i, (a, b) in enumerate(zip(sources, held))]
        wait_all(rows_in)
        segment_row = rows_v[0, micro].astype(jnp.float32)
        valid_row = rows_v[1, micro].astype(jnp.float32)
        fill_bias(bias_v, segment_row, valid_row)
        pltpu.make_async_copy(targets.at[micro, 0], g_v, in_sem.at[5]).wait()
        for part in range(1, parts):
            start_all(loads(part))
        start_all(fetches[::-1])
        start_all(later)
        gs_v[...] = stacked(g_v[...] * alphas_s[0, 1])

        def hidden_of(part):
            wait_all(loads(part))
            return folded(dot_rows(gs_v[...], wb_v[part]))

        total_inner = jnp.float32(0.0)
        ahead = hidden_of(0)
        for part in range(parts):
            cols = slice(part * 512, part * 512 + 512)
            grad_hidden = ahead
            if part + 1 < parts:
                ahead = hidden_of(part + 1)
            before = p_v[part]
            inner = gelu_inner(before)
            above = 0.5 * (1.0 + inner)
            total_inner = total_inner + jnp.sum(grad_hidden * (before * above))
            slope = above + 0.5 * before * (1.0 - inner * inner) * (GELU_A * (1.0 + 3.0 * GELU_B * (before * before)))
            high, low = split(grad_hidden * slope)
            b_v[0, :, cols] = high
            b_v[1, :, cols] = low
            more = folded(dot_rows(jnp.concatenate([high, low], axis=0), wi_v[part]))
            d_v[...] = d_v[...] + more if part else more
        stores = start_all([pltpu.make_async_copy(b_v, befores.at[micro], out_sem.at[0])])
        middle = g_v[...] + d_v[...]
        d_v[...] = middle
        high, low = split(middle * alphas_s[0, 0])
        f_v[0] = high
        f_v[1] = low
        stores += start_all([pltpu.make_async_copy(f_v, firsts.at[micro], out_sem.at[1])])
        wait_all(fetches)
        wait_all(later)
        grad_mixed = folded(dot_rows(jnp.concatenate([high, low], axis=0), wo_v[...]))
        do_v[...] = grad_mixed
        dt_v[...] = grad_mixed.T
        total_mixed = jnp.float32(0.0)
        for head in range(HEADS):
            hs = slice(head * HEAD_DIM, head * HEAD_DIM + HEAD_DIM)
            spread = jnp.sum(dt_v[hs, :] * o_v[hs, :], axis=0, keepdims=True)
            dl_v[head // 2, head % 2 : head % 2 + 1, :] = spread
            total_mixed = total_mixed + jnp.sum(spread)

        made = {}

        def products_of(pair, qb):
            lanes = slice(pair * 128, pair * 128 + 128)
            if pair not in made:
                made.clear()
                keys = k_v[:, lanes]
                made[pair] = (
                    three_lanes(keys),
                    three_lanes(v_v[:, lanes]),
                    split(q_v[:, lanes]),
                    split(do_v[:, lanes]),
                    split(keys.T),
                )
            keys_cat, values_cat, queries, mixed, turned = made[pair]
            qs = slice(qb * 128, qb * 128 + 128)
            ks = (qb + 1) * 128
            scores = pair_scores(keys_cat[:ks], queries[0][qs], queries[1][qs])
            slopes = pair_scores(values_cat[:ks], mixed[0][qs], mixed[1][qs])
            return scores, slopes, queries, mixed, turned

        def product(left_high, left_low, right_high, right_low):
            left_cat = jnp.concatenate([left_high, left_low], axis=1)
            above = jnp.concatenate([right_high, right_low], axis=1)
            below = jnp.concatenate([right_high, jnp.zeros_like(right_high)], axis=1)
            value = dot(left_cat, jnp.concatenate([above, below], axis=0))
            return value[:, :128] + value[:, 128:]

        units = [(pair, qb) for pair in range(HEADS // 2) for qb in range(blocks - 1, -1, -1)]
        for pair, qb in units:
            scores, slopes, queries, mixed, turned = products_of(pair, qb)
            lanes = slice(pair * 128, pair * 128 + 128)
            qs = slice(qb * 128, qb * 128 + 128)
            ks = (qb + 1) * 128
            bias = bias_v[:ks, qs]
            sides = [halves_of(x[qs]) for x in queries + mixed]
            key_part, value_part = None, None
            for head in range(2):
                own = slice(head * 128, head * 128 + 128)
                at = slice(head, head + 1)
                probs = jnp.exp((scores[:, own] + bias) - l_v[pair, at, qs])
                grads = probs * (slopes[:, own] - dl_v[pair, at, qs])
                q_high, q_low, d_high, d_low = [side[head] for side in sides]
                from_values = product(*split(probs), d_high, d_low)
                high, low = split(grads)
                from_keys = product(high, low, q_high, q_low)
                value_part = from_values if head == 0 else value_part + from_values
                key_part = from_keys if head == 0 else key_part + from_keys
                hs = slice(head * HEAD_DIM, head * HEAD_DIM + HEAD_DIM)
                both = jnp.concatenate([turned[0][hs, :ks], turned[1][hs, :ks]], axis=0)
                back = folded(dot(both, high)) + dot(turned[0][hs, :ks], low)
                qt_v[pair * 128 + head * HEAD_DIM : pair * 128 + head * HEAD_DIM + HEAD_DIM, qs] = back * 0.125
            if qb == blocks - 1:
                dk_v[:, lanes] = key_part
                dv_v[:, lanes] = value_part
            else:
                dk_v[:ks, lanes] += key_part
                dv_v[:ks, lanes] += value_part
        result = d_v[...]
        for index, (source, weight) in enumerate(((qt_v, wq_v), (dk_v, wk_v), (dv_v, wv_v))):
            value = source[...].T if index == 0 else source[...]
            high, low = split(value)
            x_v[0, :, pl.ds(index * D, D)] = high
            x_v[1, :, pl.ds(index * D, D)] = low
            result = result + folded(dot_rows(jnp.concatenate([high, low], axis=0), weight[...]))
        y_v[...] = result
        t_v[...] = tile_of([total_mixed / alphas_s[0, 0], total_inner / alphas_s[0, 1]])
        stores += start_all(
            [
                pltpu.make_async_copy(y_v, sent, out_sem.at[2]),
                pltpu.make_async_copy(y_v, passed.at[micro], out_sem.at[3]),
                pltpu.make_async_copy(x_v, spreads.at[micro], out_sem.at[4]),
                pltpu.make_async_copy(t_v, small.at[micro], out_sem.at[5]),
            ]
        )
        wait_all(stores)


def inner_body(count, sizes, axes, *refs):
    info, saved_m, befores = refs[:3]
    slots, refs = refs[4 : 4 + count], refs[5 + count :]
    m_v, lt_v, r_v, w_v, in_sem, r_sem, out_sem = refs
    rows = m_v.shape[1]

    def loads(part):
        copies = []
        for micro in range(2):
            for half in range(2):
                source = befores.at[micro, half, :, pl.ds(part * 512, 512)]
                target = r_v.at[part, half, pl.ds(micro * rows, rows)]
                copies.append(pltpu.make_async_copy(source, target, r_sem.at[part, len(copies)]))
        return copies

    first = pltpu.make_async_copy(saved_m, m_v, in_sem.at[0])
    first.start()
    start_all(loads(0))
    first.wait()
    for part in range(1, 4):
        start_all(loads(part))
    turn_left(lt_v, m_v, True)
    stores = []
    for part in range(4):
        wait_all(loads(part))
        put_part(w_v, part, three_dots(lt_v[0], lt_v[1], r_v[part, 0], r_v[part, 1]))
        stores += start_all(slot_copies(info, sizes, axes, w_v, slots, out_sem, part))
    wait_all(stores)


def turn_left(target, source, transpose):
    rows = target.shape[2] // 2
    for micro in range(2):
        high, low = split(source[micro].T if transpose else source[micro])
        target[0, :, micro * rows : (micro + 1) * rows] = high
        target[1, :, micro * rows : (micro + 1) * rows] = low


def attention_body(count, sizes, axes, *refs):
    info, valids, saved_s, saved_o, spreads, firsts, sums, small = refs[:8]
    slots, refs = refs[9 : 9 + count], refs[10 + count :]
    (s_v, o_v, st_v, lo_v, r_v, w_v, n_v, t_v, in_sem, r_sem, out_sem) = refs
    rows = s_v.shape[1]

    def loads(part):
        copies = []
        for micro in range(2):
            for half in range(2):
                if part < 3:
                    source = spreads.at[micro, half, :, pl.ds(part * 512, 512)]
                else:
                    source = firsts.at[micro, half]
                target = r_v.at[part, half, pl.ds(micro * rows, rows)]
                copies.append(pltpu.make_async_copy(source, target, r_sem.at[part, micro * 2 + half]))
        return copies

    lefts = [pltpu.make_async_copy(saved_s, s_v, in_sem.at[0]), pltpu.make_async_copy(saved_o, o_v, in_sem.at[1])]
    tiles = [
        pltpu.make_async_copy(sums, n_v.at[pl.ds(0, 2)], in_sem.at[2]),
        pltpu.make_async_copy(small, n_v.at[pl.ds(2, 2)], in_sem.at[3]),
    ]
    lefts[0].start()
    start_all(loads(0))
    lefts[0].wait()
    for part in range(1, 4):
        start_all(loads(part))
    start_all(lefts[1:] + tiles)
    turn_left(st_v, s_v, True)
    stores = []
    for part in range(4):
        if part == 3:
            lefts[1].wait()
            turn_left(lo_v, o_v, False)
        left = lo_v if part == 3 else st_v
        wait_all(loads(part))
        put_part(w_v, part, three_dots(left[0], left[1], r_v[part, 0], r_v[part, 1]))
        stores += start_all(slot_copies(info, sizes, axes, w_v, slots, out_sem, part))
    wait_all(tiles)
    lane = lax.broadcasted_iota(jnp.int32, (8, 256), 1)
    tile = jnp.where(lane == 3, jnp.sum(valids[...].astype(jnp.float32)), jnp.zeros((8, 256), jnp.float32))
    for index in range(3):
        tile = jnp.where(lane == index, n_v[0, 0, index] + n_v[1, 0, index], tile)
    for index in range(2):
        tile = jnp.where(lane == 4 + index, n_v[2, 0, index] + n_v[3, 0, index], tile)
    t_v[...] = tile
    unit_rows = w_v.shape[3]
    axis = axes[0]
    for by in range(sizes[axis]):

        @pl.when(lax.rem(info[1 + axis] + by, sizes[axis]) == 0)
        def _():
            target = slots[by].at[0, 0, 0, pl.ds(unit_rows, 8), pl.ds(0, 256)]
            copy = pltpu.make_async_copy(t_v, target, in_sem.at[0])
            copy.start()
            copy.wait()

    wait_all(stores)


def call(body, name, free, inputs, specs, outs, scratch, before, flops, limit):
    extra = list(before) if before is not None else []
    inputs = list(inputs[:free]) + in_hbm(list(inputs[free:])) + [TOKEN[0]]
    results = pl.pallas_call(
        functools.partial(body, len(extra)),
        out_shape=outs + [loose(8, 128)],
        in_specs=specs + [ANY] * (len(inputs) - len(specs) + len(extra)),
        out_specs=[ANY] * (len(outs) + 1),
        scratch_shapes=scratch,
        input_output_aliases={len(inputs) + i: i for i in range(len(extra))},
        compiler_params=pltpu.CompilerParams(vmem_limit_bytes=limit * 1024 * 1024),
        cost_estimate=pl.CostEstimate(flops=flops, bytes_accessed=2 * 10**7, transcendentals=10**6),
        name=name,
    )(*inputs, *in_hbm(extra))
    TOKEN[0] = results[-1]
    return results[:-1]


def backward_back(info, alphas, upstreams, targets, before, sizes, axes):
    micros, rows, inner = before.shape
    parts = inner // 512
    vmem, dma = pltpu.VMEM, pltpu.SemaphoreType.DMA
    f32, bf16 = jnp.float32, jnp.bfloat16
    slots = slot_structs(sizes, axes)
    scratch = [
        vmem((micros, rows, D), f32),
        vmem((2, micros * rows, D), bf16),
        vmem((parts, micros * rows, 512), f32),
        vmem(unit_shape(sizes), f32),
        dma((parts + 1, 2)),
        dma((parts, copy_count(sizes, axes))),
    ]

    def body(extra, *refs):
        back_body(len(slots), sizes, axes, *refs)

    inputs = [info, alphas] + list(upstreams) + [targets, before]
    return call(body, "grad_back", 4, inputs, [SCALARS, SCALARS], slots, scratch, None, 5 * 10**9, 24)


def backward_inner(info, middle, befores, sizes, axes):
    micros, rows, _ = middle.shape
    vmem, dma = pltpu.VMEM, pltpu.SemaphoreType.DMA
    f32, bf16 = jnp.float32, jnp.bfloat16
    slots = slot_structs(sizes, axes)
    scratch = [
        vmem(middle.shape, f32),
        vmem((2, D, micros * rows), bf16),
        vmem((4, 2, micros * rows, 512), bf16),
        vmem(unit_shape(sizes), f32),
        dma((1,)),
        dma((4, 4)),
        dma((4, copy_count(sizes, axes))),
    ]

    def body(extra, *refs):
        inner_body(len(slots), sizes, axes, *refs)

    return call(body, "grad_inner", 1, [info, middle, befores], [SCALARS], slots, scratch, None, 5 * 10**9, 24)


def backward_attention(info, valids, stream, mixed, spreads, firsts, sums, small, sizes, axes):
    micros, rows, _ = stream.shape
    vmem, dma = pltpu.VMEM, pltpu.SemaphoreType.DMA
    f32, bf16 = jnp.float32, jnp.bfloat16
    slots = slot_structs(sizes, axes, 8)
    scratch = [
        vmem(stream.shape, f32),
        vmem(mixed.shape, f32),
        vmem((2, D, micros * rows), bf16),
        vmem((2, D, micros * rows), bf16),
        vmem((4, 2, micros * rows, 512), bf16),
        vmem(unit_shape(sizes), f32),
        vmem((4, 8, 128), f32),
        vmem((8, 256), f32),
        dma((4,)),
        dma((4, 4)),
        dma((4, copy_count(sizes, axes))),
    ]

    def body(extra, *refs):
        attention_body(len(slots), sizes, axes, *refs)

    inputs = [info, valids, stream, mixed, spreads, firsts, sums, small]
    return call(body, "grad_attention", 2, inputs, [SCALARS, LOCAL], slots, scratch, None, 5 * 10**9, 28)


def backward_chain(tick, info, alphas, segments, valids, targets, received, before, saved, weights, previous):
    micros, rows, inner = before.shape
    parts = inner // 512
    vmem, dma = pltpu.VMEM, pltpu.SemaphoreType.DMA
    f32, bf16 = jnp.float32, jnp.bfloat16
    wq, wk, wv, wo, wi, wb = weights
    outs = [
        pltpu.HBM((micros, 2, rows, inner), bf16),
        pltpu.HBM((micros, 2, rows, 3 * D), bf16),
        pltpu.HBM((micros, 2, rows, D), bf16),
        struct(micros, rows, D),
        struct(micros, 8, 128),
        struct(rows, D),
    ]
    scratch = [
        vmem((rows, D), f32),
        vmem((parts, rows, 512), f32),
        vmem((parts, D, 512), bf16),
        vmem((parts, 512, D), bf16),
        vmem((2 * rows, D), bf16),
        vmem((rows, D), f32),
        vmem((2, rows, inner), bf16),
    ]
    scratch += [vmem(x.shape[1:], f32) for x in saved] + [vmem((D, D), bf16)] * 4
    scratch += [
        vmem((rows, rows), f32),
        vmem((rows, D), f32),
        vmem((D, rows), f32),
        vmem((HEADS // 2, 8, rows), f32),
        vmem((D, rows), f32),
        vmem((rows, D), f32),
        vmem((rows, D), f32),
        vmem((2, rows, 3 * D), bf16),
        vmem((2, rows, D), bf16),
        vmem((rows, D), f32),
        vmem((8, 128), f32),
        pltpu.SMEM(alphas.shape, f32),
        vmem((2,) + segments.shape, jnp.int32),
        dma((6,)),
        dma((parts, 3)),
        dma((4,)),
        dma((6,)),
        dma((3,)),
    ]

    def body(extra, *refs):
        chain_body(tick, extra, *refs)

    inputs = [info, TOKEN[0] if received is None else received, alphas, segments, valids, targets, before]
    inputs += list(saved) + [wi, wb, wq, wk, wv, wo]
    return call(body, "grad_chain", 2, inputs, [SCALARS], outs, scratch, previous, 2 * 10**10, 36)


def local_call(body, name, info, inputs, outs, scratch, specs=None, placed=()):
    inputs = [info, TOKEN[0]] + list(inputs)

    def parted(*refs):
        refs = refs[: len(inputs)] + refs[len(inputs) + len(placed) :]
        first = len(inputs)
        body(refs[0], refs[2:first], refs[first : first + len(outs)], refs[first + len(outs) + 1 :])

    results = pl.pallas_call(
        parted,
        out_shape=list(outs) + [loose(8, 128)],
        in_specs=[SCALARS] + [ANY] * (len(inputs) - 1 + len(placed)),
        out_specs=(specs or [ANY] * len(outs)) + [ANY],
        scratch_shapes=scratch,
        input_output_aliases={len(inputs) + i: i for i in range(len(placed))},
        compiler_params=pltpu.CompilerParams(vmem_limit_bytes=12 * 1024 * 1024),
        cost_estimate=pl.CostEstimate(flops=10**6, bytes_accessed=6 * 10**6, transcendentals=0),
        name=name,
    )(*inputs, *in_hbm(placed))
    TOKEN[0] = results[-1]
    return results[:-1]


def left_dims(done):
    return [axis for axis in (3, 2, 1, 0) if axis not in done]


def picked(ref, dims, axis, index):
    return ref.at[(slice(None),) * dims.index(axis) + (index,)]


def reduce_stage(sizes, order, step, info, arrays):
    shape = arrays[0].shape
    count = len(arrays)
    dims = left_dims(order[:step])
    parting = step < len(order) - 1
    if parting:
        axis = order[step]
        at = dims.index(axis)
        outs = [loose(*shape[:at], *shape[at + 1 :])] * sizes[axis]
    else:
        outs = [loose(*shape)]

    def body(info, ins, outs, scratch):
        held, sem = scratch
        wait_all(start_all([pltpu.make_async_copy(ref, held.at[i], sem.at[i]) for i, ref in enumerate(ins)]))
        total = held[0]
        for i in range(1, count):
            total = total + held[i]
        held[0] = total
        stores = []
        for by in range(len(outs)):
            source = held.at[0]
            if parting:
                source = picked(source, dims, axis, lax.rem(info[1 + axis] + by, sizes[axis]))
            stores.append(pltpu.make_async_copy(source, outs[by], sem.at[count + by]))
        wait_all(start_all(stores))

    scratch = [pltpu.VMEM((count,) + shape, jnp.float32), pltpu.SemaphoreType.DMA((count + len(outs),))]
    return local_call(body, "reduce_step", info, arrays, outs, scratch)


def place_stage(sizes, order, step, info, arrays):
    axis = order[step]
    dims = left_dims(order[:step])
    at = dims.index(axis)
    shape = arrays[0].shape
    count = sizes[axis]

    def body(info, ins, outs, scratch):
        copies = []
        for by in range(count):
            target = picked(outs[0], dims, axis, lax.rem(info[1 + axis] + count - by, count))
            copies.append(pltpu.make_async_copy(ins[by], target, scratch[0].at[by]))
        wait_all(start_all(copies))

    out = loose(*shape[:at], count, *shape[at:])
    return local_call(body, "place_step", info, arrays, [out], [pltpu.SemaphoreType.DMA((count,))])[0]


def out_copies(sizes, axis, info, kind, half, sources, outs, sem):
    x, y, near, far = sizes
    rows = unit_shape(sizes)[3]
    depth = near * far // 4
    count = sizes[axis]
    copies = []

    def put(source, target):
        copies.append(pltpu.make_async_copy(source, target, sem.at[len(copies)]))

    for by, piece in sources:
        place = lax.rem(info[1 + axis] + count - by, count)
        for at in range(near * far if axis < 2 else far):
            if axis == 2:
                source = piece.at[at, :, :, pl.ds(0, rows)]
                z = at * near + place
            else:
                source = piece.at[at // near, at % near, :, pl.ds(0, rows)]
                z = at
            width = piece.shape[-1]
            first = half * width
            if kind == "rows":
                out, inside = outs[0], z
            elif kind == "columns":
                part = lax.div(z, depth) if axis == 2 else z // depth
                first = pl.multiple_of(part * D + first, 128) if axis == 2 else part * D + first
                out, inside = outs[0], lax.rem(z, depth) if axis == 2 else z % depth
            else:
                out, inside = outs[z // depth], z % depth
            lanes = pl.ds(first, width)
            if axis == 0:
                put(source, out.at[inside, :, place, :, lanes])
            elif axis == 1:
                put(source, out.at[inside, place, :, :, lanes])
            else:
                put(source, out.at[inside, :, :, :, lanes])
    return copies


def out_shapes(sizes, kind):
    x, y, near, far = sizes
    rows = unit_shape(sizes)[3]
    depth = near * far // 4
    if kind == "rows":
        return [struct(near * far, y, x, rows, D)]
    if kind == "columns":
        return [struct(depth, y, x, rows, 4 * D)]
    return [struct(depth, y, x, rows, D)] * 4


def own_stage(sizes, axis, info, whole, kind, half, placed):
    def body(info, ins, outs, scratch):
        wait_all(start_all(out_copies(sizes, axis, info, kind, half, [(0, ins[0])], outs, scratch[0])))

    scratch = [pltpu.SemaphoreType.DMA((sizes[2] * sizes[3],))]
    return local_call(body, "place_own", info, [whole], out_shapes(sizes, kind), scratch, None, placed)


def last_stage(sizes, axis, info, arrays, kind, half, placed):
    rows = unit_shape(sizes)[3]
    count = sizes[axis]
    shapes, specs = out_shapes(sizes, kind), None
    scratch = [pltpu.SemaphoreType.DMA((sizes[2] * sizes[3] * count + 1,))]
    has_small = arrays[0].shape[3] > rows
    if has_small:
        specs = [ANY] * len(shapes) + [LOCAL] * 2
        shapes += [loose(1, 2), loose(1, 3)]
        scratch += [pltpu.VMEM((8, 256), jnp.float32)]

    def body(info, ins, outs, scratch):
        sem = scratch[0]
        sources = [(by, ins[by]) for by in range(1, count)]
        copies = start_all(out_copies(sizes, axis, info, kind, half, sources, outs, sem))
        if has_small:
            tile_v = scratch[1]
            for by in range(count):

                @pl.when(info[1 + axis] == by)
                def _():
                    source = ins[by].at[0, 0, 0, pl.ds(rows, 8), pl.ds(0, 256)]
                    copy = pltpu.make_async_copy(source, tile_v, sem.at[len(copies)])
                    copy.start()
                    copy.wait()

            tile = tile_v[0:1, 0:128]
            outs[-2][...] = tile[:, 4:6]
            outs[-1][...] = jnp.sqrt(tile[:, 0:3] / (jnp.maximum(tile[:, 3:4], 1.0) * D))
        wait_all(copies)

    return local_call(body, "place_last", info, arrays, shapes, scratch, specs, placed)


def extents(count):
    bits = count.bit_length() - 1
    if 1 << bits != count:
        return (1, 1, 1, count)
    side = 1 << (bits // 3)
    depth = count // (side * side)
    near = 2 if depth > 1 else 1
    return (side, side, near, depth // near)


def shifted(value, axis, by, sizes):
    count = math.prod(sizes)
    stride, length = math.prod(sizes[:axis]), sizes[axis]
    pairs = []
    for chip in range(count):
        along = (chip // stride) % length
        pairs.append((chip, chip + ((along + by) % length - along) * stride))
    return lax.ppermute(value, "dp", pairs)


def summing(slots, order, kind, half, results, sizes, info):
    pieces = list(slots)
    steps = len(order)
    for step in range(1, steps + 1):
        axis = order[step - 1]
        pieces = [pieces[0]] + [
            shifted(pieces[by if step < steps else 0], axis, by, sizes) for by in range(1, sizes[axis])
        ]
        yield pieces[-1]
        pieces = reduce_stage(sizes, order, step, info, pieces)
    whole = pieces[0]
    for step in range(steps - 2, -1, -1):
        axis = order[step]
        copies = [whole] + [shifted(whole, axis, by, sizes) for by in range(1, sizes[axis])]
        yield copies[-1]
        if step:
            whole = place_stage(sizes, order, step, info, copies)
    placed = results.get(kind, ())
    results[kind] = own_stage(sizes, order[0], info, whole, kind, half, placed)
    yield
    outs = last_stage(sizes, order[0], info, copies, kind, half, results[kind])
    results[kind] = outs[: len(out_shapes(sizes, kind))]
    results["small"] = outs[len(results[kind]) :] or results.get("small")
    yield


def shards(stream_in, cotangent, segment_ids, pad_mask, w_query, w_key, w_value, w_out, w_in, w_back, alphas):
    weights = [weight[0] for weight in (w_query, w_key, w_value, w_out, w_in, w_back)]
    sizes = extents(lax.axis_size("dp"))
    chip = lax.axis_index("dp")
    section = lax.axis_index("section")
    places, left = [], chip
    for size in sizes:
        places.append(lax.rem(left, size))
        left = lax.div(left, size)
    info = jnp.stack([section] + places).astype(jnp.int32)
    TOKEN[0] = jnp.zeros((8, 128), jnp.float32)
    state, chain = None, None

    def forward_step(tick, received):
        return forward_tick(tick, info, alphas, segment_ids, pad_mask, stream_in, received, weights, state)

    def chain_step(tick, received):
        saved = state[2:7]
        return backward_chain(
            tick, info, alphas, segment_ids, pad_mask, cotangent, received, state[8], saved, weights, chain
        )

    received, upstreams = [None], [None]
    for tick in range(2):
        sent, state = forward_step(tick, received[tick])
        received.append(lax.ppermute(sent, "section", [(0, 1)]))
    for tick in range(3):
        *chain, sent = chain_step(tick, upstreams[tick])
        if tick < 2:
            upstreams.append(lax.ppermute(sent, "section", [(1, 0)]))
        if tick == 0:
            _, state = forward_step(2, received[2])
    acts, saved_s, _, _, _, saved_o, _, saved_m, saved_p, sums = state
    befores, spreads, firsts, passed, small = chain
    orders = {key: tuple("xynf".index(axis) for axis in order) for key, order in ORDERS.items()}
    results, streams = {}, {}

    def gradients(index):
        pair, kind = ("Bb", "Ii", "Aa")[index], ("rows", "columns", "four")[index]
        pair = [key for key in pair if key in orders]
        axes = [orders[key][0] for key in pair]
        if index == 0:
            slots = backward_back(info, alphas, upstreams[1:], cotangent, saved_p, sizes, axes)
        elif index == 1:
            slots = backward_inner(info, saved_m, befores, sizes, axes)
        else:
            slots = backward_attention(info, pad_mask, saved_s, saved_o, spreads, firsts, sums, small, sizes, axes)
        for half, key in enumerate(pair):
            count = sizes[axes[half]]
            streams[key] = summing(slots[:count], orders[key], kind, half, results, sizes, info)
            slots = slots[count:]

    made, steps, owned = 0, {}, set()
    for item in PROGRAM:
        if item == "|":
            gradients(made)
            made += 1
            continue
        steps[item] = steps.get(item, 0) + 1
        if steps[item] == 8:
            for key in [key for key in steps if steps[key] in (7, 8) and key not in owned]:
                owned.add(key)
                next(streams[key])
        next(streams[item])
    attention, inner, back = results["four"], results["columns"], results["rows"]
    return (
        acts[None, :, None],
        passed[None, :, None],
        attention[0].reshape(1, D, D),
        attention[1].reshape(1, D, D),
        attention[2].reshape(1, D, D),
        attention[3].reshape(1, D, D),
        inner[0].reshape(1, D, -1),
        back[0].reshape(1, -1, D),
        results["small"][0],
        results["small"][1],
    )


def solution(mesh):
    in_specs = (
        P(None, "dp", None, None),
        P(None, "dp", None, None),
        P(None, "dp", None),
        P(None, "dp", None),
        P("section", None, None),
        P("section", None, None),
        P("section", None, None),
        P("section", None, None),
        P("section", None, None),
        P("section", None, None),
        P("section", None),
    )
    out_specs = (
        P("section", None, "dp", None, None),
        P("section", None, "dp", None, None),
        P("section", None, None),
        P("section", None, None),
        P("section", None, None),
        P("section", None, None),
        P("section", None, None),
        P("section", None, None),
        P("section", None),
        P("section", None),
    )
    return jax.shard_map(shards, mesh=mesh, in_specs=in_specs, out_specs=out_specs, check_vma=False)
```

```python
import functools
import math
import jax
import jax.numpy as jnp
from jax import lax
from jax.experimental import pallas as pl
from jax.experimental.pallas import tpu as pltpu
from jax.sharding import PartitionSpec as P

D = 512
HEADS = 8
HEAD_DIM = 64
GELU_A = math.sqrt(2.0 / math.pi)
GELU_B = 0.044715
ORDERS = {"B": "nxyf", "b": "xnyf", "I": "yxnf", "i": "nyxf", "A": "xnyf", "a": "xynf"}
PROGRAM = "|Bb|Bb|IaibBbBAaIaBbiaIbABiIbaiAIAaBiIAaiAIBiAbaIiA"


TOKEN = [None]


def start_all(copies):
    for copy in copies:
        copy.start()
    return copies


def wait_all(copies):
    for copy in copies:
        copy.wait()


def split(value):
    high = value.astype(jnp.bfloat16)
    low = (value - high.astype(jnp.float32)).astype(jnp.bfloat16)
    return (high, low)


def stacked(value):
    return jnp.concatenate(split(value), axis=0)


def dot(left_side, right_side):
    return jnp.dot(left_side, right_side, preferred_element_type=jnp.float32)


def dot_rows(left_side, right_side):
    return lax.dot_general(
        left_side, right_side, (((1,), (1,)), ((), ())), preferred_element_type=jnp.float32
    )


def folded(product):
    half = product.shape[0] // 2
    return product[:half] + product[half:]


def bands(rows, step=32):
    return [slice(at, at + step) for at in range(0, rows, step)]


def put_split(target, source, factor=None):
    for band in bands(source.shape[0]):
        high, low = split(source[band, :] if factor is None else source[band, :] * factor)
        target[0, band, :] = high
        target[1, band, :] = low


def turned(target, source):
    rows, cols = source.shape
    for row in bands(rows, 128):
        for col in bands(cols, 128):
            target[col, row] = source[row, col].T


def two_dots(left_side, right_side):
    return dot(left_side[0], right_side) + dot(left_side[1], right_side)


def gelu_inner(value):
    return jnp.tanh(value * (GELU_A + (GELU_A * GELU_B) * (value * value)))


def tile_of(numbers):
    lane = lax.broadcasted_iota(jnp.int32, (8, 128), 1)
    tile = jnp.zeros((8, 128), jnp.float32)
    for index, number in enumerate(numbers):
        tile = jnp.where(lane == index, number, tile)
    return tile


def fill_bias(bias_ref, segment_row, valid_row):
    blocks = segment_row.shape[1] // 128
    segment_col = jnp.broadcast_to(segment_row, (128, segment_row.shape[1])).T
    valid_col = jnp.broadcast_to(valid_row, (128, valid_row.shape[1])).T
    for kb in range(blocks):
        ks = slice(kb * 128, kb * 128 + 128)
        for qb in range(kb, blocks):
            qs = slice(qb * 128, qb * 128 + 128)
            k_place = lax.broadcasted_iota(jnp.int32, (128, 128), 0) + kb * 128
            q_place = lax.broadcasted_iota(jnp.int32, (128, 128), 1) + qb * 128
            allowed = (segment_col[ks] == segment_row[:, qs]) & (k_place <= q_place)
            allowed = allowed & ((valid_col[ks] > 0) | (k_place == q_place))
            bias_ref[ks, qs] = jnp.where(allowed, 0.0, -1e30)


def halves_of(value):
    lane = lax.broadcasted_iota(jnp.int32, value.shape, 1)
    zero = jnp.zeros_like(value)
    return (jnp.where(lane < HEAD_DIM, value, zero), jnp.where(lane < HEAD_DIM, zero, value))


def pair_scores(keys_cat, queries_high, queries_low):
    sides = []
    for high, low in zip(halves_of(queries_high), halves_of(queries_low)):
        sides.append(jnp.concatenate([high, high, low], axis=1))
    return dot_rows(keys_cat, jnp.concatenate(sides, axis=0))


def three_lanes(value):
    high, low = split(value)
    return jnp.concatenate([high, low, high], axis=1)


def fetch_rows(alphas, segments, valids, alphas_s, rows_v, sem):
    return start_all(
        [
            pltpu.make_async_copy(alphas, alphas_s, sem.at[0]),
            pltpu.make_async_copy(segments, rows_v.at[0], sem.at[1]),
            pltpu.make_async_copy(valids, rows_v.at[1], sem.at[2]),
        ]
    )


def forward_body(tick, *refs):
    (info, alphas, segments, valids, streams, wq, wk, wv, wo, wi, wb) = refs[:11]
    received = streams.at[0, 0] if tick == 0 else refs[12]
    refs = refs[12 + (0 if tick == 0 else 11) :]
    (acts, sent, saved_s, saved_q, saved_k, saved_v, saved_o, saved_l, saved_m, saved_p, sums, _) = refs[:12]
    (s_v, wq_v, wk_v, wv_v, wo_v, wi_v, wb_v, q_v, k_v, v_v, ot_v, l_v, m_v, p_v, a_v, t_v, bias_v, x_v, w_v, c_v, h_v, alphas_s, rows_v, in_sem, out_sem, row_sem) = refs[12:]
    section = info[0]
    micro = tick - section
    rows = s_v.shape[0]
    blocks = rows // 128
    parts = wi_v.shape[1] // 512

    @pl.when((micro >= 0) & (micro < 2))
    def _():
        pairs = [(wq, wq_v), (wk, wk_v), (wv, wv_v), (wo, wo_v), (wi, wi_v), (wb, wb_v)]
        loads = [pltpu.make_async_copy(a, b, in_sem.at[i]) for i, (a, b) in enumerate(pairs)]

        @pl.when(section == 0)
        def _():
            pltpu.make_async_copy(streams.at[micro, 0], s_v, in_sem.at[6]).start()

        @pl.when(section != 0)
        def _():
            pltpu.make_async_copy(received, s_v, in_sem.at[6]).start()

        loads[0].start()
        small = fetch_rows(alphas, segments, valids, alphas_s, rows_v, row_sem)
        pltpu.make_async_copy(received, s_v, in_sem.at[6]).wait()
        start_all(loads[1:])
        put_split(x_v, s_v)
        for index, (weight, target) in enumerate(((wq_v, q_v), (wk_v, k_v), (wv_v, v_v))):
            loads[index].wait()
            value = two_dots(x_v, weight[...])
            target[...] = value * 0.125 if index == 0 else value
        wait_all(small)
        segment_row = rows_v[0, micro].astype(jnp.float32)
        valid_row = rows_v[1, micro].astype(jnp.float32)
        fill_bias(bias_v, segment_row, valid_row)

        stores = []

        def store(source, target):
            copy = pltpu.make_async_copy(source, target, out_sem.at[len(stores)])
            copy.start()
            stores.append(copy)

        store(s_v, saved_s.at[micro])
        store(q_v, saved_q.at[micro])
        store(k_v, saved_k.at[micro])
        store(v_v, saved_v.at[micro])
        made = {}

        def put_scores(index):
            pair, qb = units[index]
            lanes = slice(pair * 128, pair * 128 + 128)
            if pair not in made:
                made[pair] = (three_lanes(k_v[:, lanes]), split(q_v[:, lanes]), split(v_v[:, lanes].T))
            keys_cat, queries, _ = made[pair]
            qs = slice(qb * 128, qb * 128 + 128)
            ks = (qb + 1) * 128
            w_v[index % 2, :ks, :] = pair_scores(keys_cat[:ks], queries[0][qs], queries[1][qs])

        units = [(pair, qb) for pair in range(HEADS // 2) for qb in range(blocks)]
        put_scores(0)
        for index, (pair, qb) in enumerate(units):
            if index + 1 < len(units):
                put_scores(index + 1)
            values_high, values_low = made[pair][2]
            qs = slice(qb * 128, qb * 128 + 128)
            ks = (qb + 1) * 128
            for head in range(2):
                own = slice(head * 128, head * 128 + 128)
                top = None
                for band in bands(ks, 128):
                    part = w_v[index % 2, band, own] + bias_v[band, qs]
                    w_v[index % 2, band, own] = part
                    most = jnp.max(part, axis=0, keepdims=True)
                    top = most if top is None else jnp.maximum(top, most)
                total = None
                for band in bands(ks, 128):
                    probs = jnp.exp(w_v[index % 2, band, own] - top)
                    more = jnp.sum(probs, axis=0, keepdims=True)
                    total = more if total is None else total + more
                    high, low = split(probs)
                    c_v[head, band, :128] = high
                    c_v[head, band, 128:] = low
                hs = slice(head * HEAD_DIM, head * HEAD_DIM + HEAD_DIM)
                both = jnp.concatenate([values_high[hs, :ks], values_low[hs, :ks]], axis=0)
                mixed = folded(dot(both, c_v[head, :ks, :128])) + dot(values_high[hs, :ks], c_v[head, :ks, 128:])
                at = slice(pair * 128 + head * HEAD_DIM, pair * 128 + head * HEAD_DIM + HEAD_DIM)
                ot_v[at, qs] = mixed / total
                l_v[pair, head : head + 1, qs] = top + jnp.log(total)
        store(ot_v, saved_o.at[micro])
        store(l_v, saved_l.at[micro])
        turned(m_v, ot_v)
        put_split(x_v, m_v)
        loads[3].wait()
        a_v[...] = two_dots(x_v, wo_v[...])
        valid_col = jnp.broadcast_to(valid_row, (128, rows)).T
        attn_sum = jnp.zeros((32, D), jnp.float32)
        for band in bands(rows):
            attn = a_v[band, :] * alphas_s[0, 0]
            attn_sum = attn_sum + attn * attn * jnp.concatenate([valid_col[band]] * (D // 128), axis=1)
            middle = s_v[band, :] + attn
            m_v[band, :] = middle
            high, low = split(middle)
            x_v[0, band, :] = high
            x_v[1, band, :] = low
        store(m_v, saved_m.at[micro])
        loads[4].wait()

        def put_before(part):
            p_v[:, part * 512 : part * 512 + 512] = two_dots(x_v, wi_v[:, part * 512 : part * 512 + 512])

        put_before(0)
        loads[5].wait()
        for part in range(parts):
            cols = slice(part * 512, part * 512 + 512)
            store(p_v.at[:, pl.ds(part * 512, 512)], saved_p.at[micro, :, pl.ds(part * 512, 512)])
            if part + 1 < parts:
                put_before(part + 1)
            for band in bands(rows):
                before = p_v[band, cols]
                high, low = split(0.5 * before * (1.0 + gelu_inner(before)))
                h_v[part % 2, 0, band, :] = high
                h_v[part % 2, 1, band, :] = low
            more = two_dots(h_v.at[part % 2], wb_v[cols, :])
            a_v[...] = a_v[...] + more if part else more
        result_sum = jnp.zeros((32, D), jnp.float32)
        ffn_sum = jnp.zeros((32, D), jnp.float32)
        for band in bands(rows):
            weighting = jnp.concatenate([valid_col[band]] * (D // 128), axis=1)
            ffn = a_v[band, :] * alphas_s[0, 1]
            result = m_v[band, :] + ffn
            a_v[band, :] = result
            result_sum = result_sum + result * result * weighting
            ffn_sum = ffn_sum + ffn * ffn * weighting
        store(a_v, sent)
        store(a_v, acts.at[micro])
        t_v[...] = tile_of([jnp.sum(result_sum), jnp.sum(attn_sum), jnp.sum(ffn_sum)])
        store(t_v, sums.at[micro])
        wait_all(stores)


def struct(*shape):
    return pltpu.HBM(shape, jnp.float32)


def loose(*shape):
    return jax.ShapeDtypeStruct(shape, jnp.float32)


def in_hbm(arrays):
    return [pltpu.with_memory_space_constraint(array, pltpu.HBM) for array in arrays]


ANY = pl.BlockSpec(memory_space=pl.ANY)
SCALARS = pl.BlockSpec(memory_space=pltpu.SMEM)
LOCAL = pl.BlockSpec(memory_space=pltpu.VMEM)


def forward_tick(tick, info, alphas, segments, valids, streams, received, weights, state):
    micro_count, _, rows, width = streams.shape
    inner = weights[4].shape[1]
    whole = struct(micro_count, rows, width)
    shapes = [
        whole,
        struct(rows, width),
        whole,
        whole,
        whole,
        whole,
        struct(micro_count, width, rows),
        struct(micro_count, HEADS // 2, 8, rows),
        whole,
        struct(micro_count, rows, inner),
        struct(micro_count, 8, 128),
        loose(8, 128),
    ]
    kept = [0, 2, 3, 4, 5, 6, 7, 8, 9, 10]
    extra = [] if state is None else [received] + in_hbm(state)
    aliases = {} if state is None else {13 + i: out for i, out in enumerate(kept)}
    f32, bf16 = jnp.float32, jnp.bfloat16
    vmem, dma = pltpu.VMEM, pltpu.SemaphoreType.DMA
    scratch = [vmem((rows, width), f32)] + [vmem(w.shape, bf16) for w in weights]
    scratch += [vmem((rows, width), f32)] * 3 + [vmem((width, rows), f32), vmem((HEADS // 2, 8, rows), f32)]
    scratch += [vmem((rows, width), f32), vmem((rows, inner), f32), vmem((rows, width), f32)]
    scratch += [vmem((8, 128), f32), vmem((rows, rows), f32), vmem((2, rows, width), bf16)]
    scratch += [vmem((2, rows, 256), f32), vmem((2, rows, 256), bf16), vmem((2, 2, rows, 512), bf16)]
    scratch += [pltpu.SMEM(alphas.shape, f32), vmem((2,) + segments.shape, jnp.int32)]
    scratch += [dma((7,)), dma((10 + inner // 512,)), dma((3,))]
    outs = pl.pallas_call(
        functools.partial(forward_body, tick),
        out_shape=shapes,
        in_specs=[SCALARS] + [ANY] * (11 + len(extra)),
        out_specs=[ANY] * len(shapes),
        scratch_shapes=scratch,
        input_output_aliases=aliases,
        compiler_params=pltpu.CompilerParams(vmem_limit_bytes=28 * 1024 * 1024),
        cost_estimate=pl.CostEstimate(flops=10**10, bytes_accessed=2 * 10**7, transcendentals=10**6),
        name="layer_forward",
    )(info, *in_hbm([alphas, segments, valids, streams, *weights]), TOKEN[0], *extra)
    TOKEN[0] = outs[-1]
    return (outs[1], [outs[i] for i in kept])


def unit_shape(sizes):
    x, y, near, far = sizes
    return (near * far, y, x, 4 * D // (x * y * near * far), D)


def slot_structs(sizes, axes, more=0):
    x, y, near, far = sizes
    structs = []
    for axis in axes:
        shape = [size for index, size in ((3, far), (2, near), (1, y), (0, x)) if index != axis]
        structs += [struct(*shape, unit_shape(sizes)[3] + (0 if structs else more), D // len(axes))] * sizes[axis]
    return structs


def put_part(unit, part, value):
    depth = unit.shape[0] // 4
    unit[pl.ds(part * depth, depth)] = value.reshape((depth,) + unit.shape[1:])


def slot_copies(info, sizes, axes, unit, slots, sems, part):
    x, y, near, far = sizes
    depth, rows = near * far // 4, unit.shape[3]
    copies, first = [], 0
    for half, axis in enumerate(axes):
        lanes = pl.ds(half * (D // len(axes)), D // len(axes))
        for by in range(sizes[axis]):
            place = lax.rem(info[1 + axis] + by, sizes[axis])
            slot = slots[first + by]
            if axis == 2:
                pairs = [
                    (unit.at[at * near + place, :, :, :, lanes], slot.at[at, :, :, pl.ds(0, rows)])
                    for at in range(far)
                    if part * depth < (at + 1) * near <= (part + 1) * depth
                ]
            else:
                pairs = []
                for at in range(part * depth, (part + 1) * depth):
                    source = unit.at[at, :, place, :, lanes] if axis == 0 else unit.at[at, place, :, :, lanes]
                    pairs.append((source, slot.at[at // near, at % near, :, pl.ds(0, rows)]))
            for source, target in pairs:
                copies.append(pltpu.make_async_copy(source, target, sems.at[part, len(copies)]))
        first += sizes[axis]
    return copies


def copy_count(sizes, axes):
    return sum(sizes[axis] for axis in axes) * max(1, sizes[2] * sizes[3] // 4)


def three_dots(left_high, left_low, right_high, right_low):
    return dot(left_high, right_high) + dot(left_low, right_high) + dot(left_high, right_low)


def back_body(count, sizes, axes, *refs):
    info, alphas = refs[:2]
    upstreams, targets, saved_p = refs[2:4], refs[4], refs[5]
    slots, refs = refs[7 : 7 + count], refs[8 + count :]
    g_v, gh_v, p_v, h_v, w_v, in_sem, out_sem = refs
    parts = p_v.shape[0]
    rows = g_v.shape[1]

    def load(part, micro):
        cols = pl.ds(part * 512, 512)
        return pltpu.make_async_copy(
            saved_p.at[micro, :, cols], p_v.at[part, pl.ds(micro * rows, rows)], in_sem.at[part, micro]
        )

    for micro in range(2):

        @pl.when(info[0] == 0)
        def _():
            pltpu.make_async_copy(upstreams[micro], g_v.at[micro], in_sem.at[parts, micro]).start()

        @pl.when(info[0] != 0)
        def _():
            pltpu.make_async_copy(targets.at[micro, 0], g_v.at[micro], in_sem.at[parts, micro]).start()

    start_all([load(0, micro) for micro in range(2)])
    for micro in range(2):
        pltpu.make_async_copy(targets.at[micro, 0], g_v.at[micro], in_sem.at[parts, micro]).wait()
    for part in range(1, parts):
        start_all([load(part, micro) for micro in range(2)])
    for micro in range(2):
        put_split(gh_v.at[:, pl.ds(micro * rows, rows)], g_v.at[micro], alphas[0, 1])

    def put_left(part):
        for micro in range(2):
            load(part, micro).wait()
        for row in bands(2 * rows, 128):
            for col in bands(512, 128):
                before = p_v[part, row, col].T
                high, low = split(0.5 * before * (1.0 + gelu_inner(before)))
                h_v[part % 2, 0, col, row] = high
                h_v[part % 2, 1, col, row] = low

    stores = []
    put_left(0)
    for part in range(parts):
        if part + 1 < parts:
            put_left(part + 1)
        left = h_v.at[part % 2]
        put_part(w_v, part, three_dots(left[0], left[1], gh_v[0], gh_v[1]))
        stores += start_all(slot_copies(info, sizes, axes, w_v, slots, out_sem, part))
    wait_all(stores)


def chain_body(tick, extra, *refs):
    info, received = refs[:2]
    alphas, segments, valids, targets, saved_p = refs[2:7]
    sources = refs[7:12]
    wi, wb = refs[12:14]
    weights = refs[14:18]
    refs = refs[19 + extra :]
    (befores, spreads, firsts, passed, small, sent, _) = refs[:7]
    (g_v, p_v, wi_v, wb_v, gs_v, d_v, b_v) = refs[7:14]
    held = refs[14:19]
    weights_v = refs[19:23]
    (bias_v, do_v, dt_v, dl_v, qt_v, dk_v, dv_v, x_v, f_v, y_v, t_v, h_v, s_v, c_v, alphas_s, rows_v, in_sem, part_sem, w_sem, out_sem, row_sem) = refs[23:]
    parts = p_v.shape[0]
    rows = bias_v.shape[0]
    blocks = rows // 128
    (q_v, k_v, v_v, o_v, l_v) = held
    (wq_v, wk_v, wv_v, wo_v) = weights_v
    section = info[0]
    micro = tick - (1 - section)

    @pl.when((micro >= 0) & (micro < 2))
    def _():
        def loads(part):
            cols = pl.ds(part * 512, 512)
            return [
                pltpu.make_async_copy(wb.at[cols], wb_v.at[part], part_sem.at[part, 0]),
                pltpu.make_async_copy(saved_p.at[micro, :, cols], p_v.at[part], part_sem.at[part, 1]),
                pltpu.make_async_copy(wi.at[:, cols], wi_v.at[part], part_sem.at[part, 2]),
            ]

        @pl.when(section == 0)
        def _():
            pltpu.make_async_copy(received if tick else targets.at[micro, 0], g_v, in_sem.at[5]).start()

        @pl.when(section != 0)
        def _():
            pltpu.make_async_copy(targets.at[micro, 0], g_v, in_sem.at[5]).start()

        rows_in = fetch_rows(alphas, segments, valids, alphas_s, rows_v, row_sem)
        start_all(loads(0))
        fetches = [pltpu.make_async_copy(a, b, w_sem.at[i]) for i, (a, b) in enumerate(zip(weights, weights_v))]
        later = [pltpu.make_async_copy(a.at[micro], b, in_sem.at[i]) for i, (a, b) in enumerate(zip(sources, held))]
        wait_all(rows_in)
        segment_row = rows_v[0, micro].astype(jnp.float32)
        valid_row = rows_v[1, micro].astype(jnp.float32)
        fill_bias(bias_v, segment_row, valid_row)
        pltpu.make_async_copy(targets.at[micro, 0], g_v, in_sem.at[5]).wait()
        for part in range(1, parts):
            start_all(loads(part))
        start_all(fetches[::-1])
        start_all(later)
        put_split(gs_v, g_v, alphas_s[0, 1])

        def put_hidden(part):
            wait_all(loads(part))
            h_v[part % 2] = dot_rows(gs_v[0], wb_v[part]) + dot_rows(gs_v[1], wb_v[part])

        inner_sum = jnp.zeros((32, 512), jnp.float32)
        put_hidden(0)
        for part in range(parts):
            cols = slice(part * 512, part * 512 + 512)
            if part + 1 < parts:
                put_hidden(part + 1)
            for band in bands(rows):
                grad_hidden = h_v[part % 2, band, :]
                before = p_v[part, band, :]
                square = before * before
                inner = jnp.tanh(before * (GELU_A + (GELU_A * GELU_B) * square))
                above = 0.5 + 0.5 * inner
                inner_sum = inner_sum + grad_hidden * (before * above)
                slope = above + before * (1.0 - inner * inner) * (0.5 * GELU_A + (1.5 * GELU_A * GELU_B) * square)
                high, low = split(grad_hidden * slope)
                b_v[0, band, cols] = high
                b_v[1, band, cols] = low
            more = dot_rows(b_v[0, :, cols], wi_v[part]) + dot_rows(b_v[1, :, cols], wi_v[part])
            d_v[...] = d_v[...] + more if part else more
        total_inner = jnp.sum(inner_sum)
        stores = start_all([pltpu.make_async_copy(b_v, befores.at[micro], out_sem.at[0])])
        for band in bands(rows):
            middle = g_v[band, :] + d_v[band, :]
            d_v[band, :] = middle
            high, low = split(middle * alphas_s[0, 0])
            f_v[0, band, :] = high
            f_v[1, band, :] = low
        stores += start_all([pltpu.make_async_copy(f_v, firsts.at[micro], out_sem.at[1])])
        wait_all(fetches)
        wait_all(later)
        do_v[...] = dot_rows(f_v[0], wo_v[...]) + dot_rows(f_v[1], wo_v[...])
        turned(dt_v, do_v)
        total_mixed = jnp.float32(0.0)
        for head in range(HEADS):
            hs = slice(head * HEAD_DIM, head * HEAD_DIM + HEAD_DIM)
            spread = jnp.sum(dt_v[hs, :] * o_v[hs, :], axis=0, keepdims=True)
            dl_v[head // 2, head % 2 : head % 2 + 1, :] = spread
            total_mixed = total_mixed + jnp.sum(spread)
        made = {}

        def put_products(index):
            pair, qb = units[index]
            lanes = slice(pair * 128, pair * 128 + 128)
            if pair not in made:
                keys = k_v[:, lanes]
                made[pair] = (
                    three_lanes(keys),
                    three_lanes(v_v[:, lanes]),
                    split(q_v[:, lanes]),
                    split(do_v[:, lanes]),
                    split(keys.T),
                )
            keys_cat, values_cat, queries, mixed, _ = made[pair]
            qs = slice(qb * 128, qb * 128 + 128)
            ks = (qb + 1) * 128
            s_v[index % 2, 0, :ks, :] = pair_scores(keys_cat[:ks], queries[0][qs], queries[1][qs])
            s_v[index % 2, 1, :ks, :] = pair_scores(values_cat[:ks], mixed[0][qs], mixed[1][qs])

        def product(left_cat, right_high, right_low):
            above = jnp.concatenate([right_high, right_low], axis=1)
            below = jnp.concatenate([right_high, jnp.zeros_like(right_high)], axis=1)
            value = dot(left_cat, jnp.concatenate([above, below], axis=0))
            return value[:, :128] + value[:, 128:]

        units = [(pair, qb) for pair in range(HEADS // 2) for qb in range(blocks - 1, -1, -1)]
        put_products(0)
        for index, (pair, qb) in enumerate(units):
            if index + 1 < len(units):
                put_products(index + 1)
            _, _, queries, mixed, keys_turned = made[pair]
            lanes = slice(pair * 128, pair * 128 + 128)
            qs = slice(qb * 128, qb * 128 + 128)
            ks = (qb + 1) * 128
            sides = [halves_of(x[qs]) for x in queries + mixed]
            for head in range(2):
                own = slice(head * 128, head * 128 + 128)
                at = slice(head, head + 1)
                for band in bands(ks, 128):
                    probs = jnp.exp((s_v[index % 2, 0, band, own] + bias_v[band, qs]) - l_v[pair, at, qs])
                    grads = probs * (s_v[index % 2, 1, band, own] - dl_v[pair, at, qs])
                    for place, value in enumerate((probs, grads)):
                        high, low = split(value)
                        c_v[head, place, band, :128] = high
                        c_v[head, place, band, 128:] = low
                q_high, q_low, d_high, d_low = [side[head] for side in sides]
                from_values = product(c_v[head, 0, :ks, :], d_high, d_low)
                from_keys = product(c_v[head, 1, :ks, :], q_high, q_low)
                if qb == blocks - 1 and head == 0:
                    dv_v[:, lanes] = from_values
                    dk_v[:, lanes] = from_keys
                else:
                    dv_v[:ks, lanes] += from_values
                    dk_v[:ks, lanes] += from_keys
                hs = slice(head * HEAD_DIM, head * HEAD_DIM + HEAD_DIM)
                both = jnp.concatenate([keys_turned[0][hs, :ks], keys_turned[1][hs, :ks]], axis=0)
                back = folded(dot(both, c_v[head, 1, :ks, :128])) + dot(keys_turned[0][hs, :ks], c_v[head, 1, :ks, 128:])
                qt_v[pair * 128 + head * HEAD_DIM : pair * 128 + head * HEAD_DIM + HEAD_DIM, qs] = back * 0.125

        turned(do_v, qt_v)
        result = d_v[...]
        for index, (source, weight) in enumerate(((do_v, wq_v), (dk_v, wk_v), (dv_v, wv_v))):
            cols = pl.ds(index * D, D)
            put_split(x_v.at[:, :, cols], source)
            result = result + dot_rows(x_v[0, :, cols], weight[...]) + dot_rows(x_v[1, :, cols], weight[...])
        y_v[...] = result
        t_v[...] = tile_of([total_mixed / alphas_s[0, 0], total_inner / alphas_s[0, 1]])
        stores += start_all(
            [
                pltpu.make_async_copy(y_v, sent, out_sem.at[2]),
                pltpu.make_async_copy(y_v, passed.at[micro], out_sem.at[3]),
                pltpu.make_async_copy(x_v, spreads.at[micro], out_sem.at[4]),
                pltpu.make_async_copy(t_v, small.at[micro], out_sem.at[5]),
            ]
        )
        wait_all(stores)


def inner_body(count, sizes, axes, *refs):
    info, saved_m, befores = refs[:3]
    slots, refs = refs[4 : 4 + count], refs[5 + count :]
    m_v, lt_v, r_v, w_v, in_sem, r_sem, out_sem = refs
    rows = m_v.shape[1]

    def loads(part):
        copies = []
        for micro in range(2):
            for half in range(2):
                source = befores.at[micro, half, :, pl.ds(part * 512, 512)]
                target = r_v.at[part, half, pl.ds(micro * rows, rows)]
                copies.append(pltpu.make_async_copy(source, target, r_sem.at[part, len(copies)]))
        return copies

    first = pltpu.make_async_copy(saved_m, m_v, in_sem.at[0])
    first.start()
    start_all(loads(0))
    first.wait()
    for part in range(1, 4):
        start_all(loads(part))
    turn_left(lt_v, m_v, True)
    stores = []
    for part in range(4):
        wait_all(loads(part))
        put_part(w_v, part, three_dots(lt_v[0], lt_v[1], r_v[part, 0], r_v[part, 1]))
        stores += start_all(slot_copies(info, sizes, axes, w_v, slots, out_sem, part))
    wait_all(stores)


def turn_left(target, source, transpose):
    rows = target.shape[2] // 2
    for micro in range(2):
        for row in bands(source.shape[1], 128):
            for col in bands(source.shape[2], 128):
                value = source[micro, row, col]
                high, low = split(value.T if transpose else value)
                lines, lanes = (col, row) if transpose else (row, col)
                lanes = slice(micro * rows + lanes.start, micro * rows + lanes.stop)
                target[0, lines, lanes] = high
                target[1, lines, lanes] = low


def attention_body(count, sizes, axes, *refs):
    info, valids, saved_s, saved_o, spreads, firsts, sums, small = refs[:8]
    slots, refs = refs[9 : 9 + count], refs[10 + count :]
    (s_v, o_v, st_v, lo_v, r_v, w_v, n_v, t_v, in_sem, r_sem, out_sem) = refs
    rows = s_v.shape[1]

    def loads(part):
        copies = []
        for micro in range(2):
            for half in range(2):
                if part < 3:
                    source = spreads.at[micro, half, :, pl.ds(part * 512, 512)]
                else:
                    source = firsts.at[micro, half]
                target = r_v.at[part, half, pl.ds(micro * rows, rows)]
                copies.append(pltpu.make_async_copy(source, target, r_sem.at[part, micro * 2 + half]))
        return copies

    lefts = [pltpu.make_async_copy(saved_s, s_v, in_sem.at[0]), pltpu.make_async_copy(saved_o, o_v, in_sem.at[1])]
    tiles = [
        pltpu.make_async_copy(sums, n_v.at[pl.ds(0, 2)], in_sem.at[2]),
        pltpu.make_async_copy(small, n_v.at[pl.ds(2, 2)], in_sem.at[3]),
    ]
    lefts[0].start()
    start_all(loads(0))
    lefts[0].wait()
    for part in range(1, 4):
        start_all(loads(part))
    start_all(lefts[1:] + tiles)
    turn_left(st_v, s_v, True)
    stores = []
    for part in range(4):
        if part == 3:
            lefts[1].wait()
            turn_left(lo_v, o_v, False)
        left = lo_v if part == 3 else st_v
        wait_all(loads(part))
        put_part(w_v, part, three_dots(left[0], left[1], r_v[part, 0], r_v[part, 1]))
        stores += start_all(slot_copies(info, sizes, axes, w_v, slots, out_sem, part))
    wait_all(tiles)
    lane = lax.broadcasted_iota(jnp.int32, (8, 256), 1)
    tile = jnp.where(lane == 3, jnp.sum(valids[...].astype(jnp.float32)), jnp.zeros((8, 256), jnp.float32))
    for index in range(3):
        tile = jnp.where(lane == index, n_v[0, 0, index] + n_v[1, 0, index], tile)
    for index in range(2):
        tile = jnp.where(lane == 4 + index, n_v[2, 0, index] + n_v[3, 0, index], tile)
    t_v[...] = tile
    unit_rows = w_v.shape[3]
    axis = axes[0]
    for by in range(sizes[axis]):

        @pl.when(lax.rem(info[1 + axis] + by, sizes[axis]) == 0)
        def _():
            target = slots[by].at[0, 0, 0, pl.ds(unit_rows, 8), pl.ds(0, 256)]
            copy = pltpu.make_async_copy(t_v, target, in_sem.at[0])
            copy.start()
            copy.wait()

    wait_all(stores)


def call(body, name, free, inputs, specs, outs, scratch, before, flops, limit):
    extra = list(before) if before is not None else []
    inputs = list(inputs[:free]) + in_hbm(list(inputs[free:])) + [TOKEN[0]]
    results = pl.pallas_call(
        functools.partial(body, len(extra)),
        out_shape=outs + [loose(8, 128)],
        in_specs=specs + [ANY] * (len(inputs) - len(specs) + len(extra)),
        out_specs=[ANY] * (len(outs) + 1),
        scratch_shapes=scratch,
        input_output_aliases={len(inputs) + i: i for i in range(len(extra))},
        compiler_params=pltpu.CompilerParams(vmem_limit_bytes=limit * 1024 * 1024),
        cost_estimate=pl.CostEstimate(flops=flops, bytes_accessed=2 * 10**7, transcendentals=10**6),
        name=name,
    )(*inputs, *in_hbm(extra))
    TOKEN[0] = results[-1]
    return results[:-1]


def backward_back(info, alphas, upstreams, targets, before, sizes, axes):
    micros, rows, inner = before.shape
    parts = inner // 512
    vmem, dma = pltpu.VMEM, pltpu.SemaphoreType.DMA
    f32, bf16 = jnp.float32, jnp.bfloat16
    slots = slot_structs(sizes, axes)
    scratch = [
        vmem((micros, rows, D), f32),
        vmem((2, micros * rows, D), bf16),
        vmem((parts, micros * rows, 512), f32),
        vmem((2, 2, 512, micros * rows), bf16),
        vmem(unit_shape(sizes), f32),
        dma((parts + 1, 2)),
        dma((parts, copy_count(sizes, axes))),
    ]

    def body(extra, *refs):
        back_body(len(slots), sizes, axes, *refs)

    inputs = [info, alphas] + list(upstreams) + [targets, before]
    return call(body, "grad_back", 4, inputs, [SCALARS, SCALARS], slots, scratch, None, 5 * 10**9, 24)


def backward_inner(info, middle, befores, sizes, axes):
    micros, rows, _ = middle.shape
    vmem, dma = pltpu.VMEM, pltpu.SemaphoreType.DMA
    f32, bf16 = jnp.float32, jnp.bfloat16
    slots = slot_structs(sizes, axes)
    scratch = [
        vmem(middle.shape, f32),
        vmem((2, D, micros * rows), bf16),
        vmem((4, 2, micros * rows, 512), bf16),
        vmem(unit_shape(sizes), f32),
        dma((1,)),
        dma((4, 4)),
        dma((4, copy_count(sizes, axes))),
    ]

    def body(extra, *refs):
        inner_body(len(slots), sizes, axes, *refs)

    return call(body, "grad_inner", 1, [info, middle, befores], [SCALARS], slots, scratch, None, 5 * 10**9, 24)


def backward_attention(info, valids, stream, mixed, spreads, firsts, sums, small, sizes, axes):
    micros, rows, _ = stream.shape
    vmem, dma = pltpu.VMEM, pltpu.SemaphoreType.DMA
    f32, bf16 = jnp.float32, jnp.bfloat16
    slots = slot_structs(sizes, axes, 8)
    scratch = [
        vmem(stream.shape, f32),
        vmem(mixed.shape, f32),
        vmem((2, D, micros * rows), bf16),
        vmem((2, D, micros * rows), bf16),
        vmem((4, 2, micros * rows, 512), bf16),
        vmem(unit_shape(sizes), f32),
        vmem((4, 8, 128), f32),
        vmem((8, 256), f32),
        dma((4,)),
        dma((4, 4)),
        dma((4, copy_count(sizes, axes))),
    ]

    def body(extra, *refs):
        attention_body(len(slots), sizes, axes, *refs)

    inputs = [info, valids, stream, mixed, spreads, firsts, sums, small]
    return call(body, "grad_attention", 2, inputs, [SCALARS, LOCAL], slots, scratch, None, 5 * 10**9, 28)


def backward_chain(tick, info, alphas, segments, valids, targets, received, before, saved, weights, previous):
    micros, rows, inner = before.shape
    parts = inner // 512
    vmem, dma = pltpu.VMEM, pltpu.SemaphoreType.DMA
    f32, bf16 = jnp.float32, jnp.bfloat16
    wq, wk, wv, wo, wi, wb = weights
    outs = [
        pltpu.HBM((micros, 2, rows, inner), bf16),
        pltpu.HBM((micros, 2, rows, 3 * D), bf16),
        pltpu.HBM((micros, 2, rows, D), bf16),
        struct(micros, rows, D),
        struct(micros, 8, 128),
        struct(rows, D),
    ]
    scratch = [
        vmem((rows, D), f32),
        vmem((parts, rows, 512), f32),
        vmem((parts, D, 512), bf16),
        vmem((parts, 512, D), bf16),
        vmem((2, rows, D), bf16),
        vmem((rows, D), f32),
        vmem((2, rows, inner), bf16),
    ]
    scratch += [vmem(x.shape[1:], f32) for x in saved] + [vmem((D, D), bf16)] * 4
    scratch += [
        vmem((rows, rows), f32),
        vmem((rows, D), f32),
        vmem((D, rows), f32),
        vmem((HEADS // 2, 8, rows), f32),
        vmem((D, rows), f32),
        vmem((rows, D), f32),
        vmem((rows, D), f32),
        vmem((2, rows, 3 * D), bf16),
        vmem((2, rows, D), bf16),
        vmem((rows, D), f32),
        vmem((8, 128), f32),
        vmem((2, rows, 512), f32),
        vmem((2, 2, rows, 256), f32),
        vmem((2, 2, rows, 256), bf16),
        pltpu.SMEM(alphas.shape, f32),
        vmem((2,) + segments.shape, jnp.int32),
        dma((6,)),
        dma((parts, 3)),
        dma((4,)),
        dma((6,)),
        dma((3,)),
    ]

    def body(extra, *refs):
        chain_body(tick, extra, *refs)

    inputs = [info, TOKEN[0] if received is None else received, alphas, segments, valids, targets, before]
    inputs += list(saved) + [wi, wb, wq, wk, wv, wo]
    return call(body, "grad_chain", 2, inputs, [SCALARS], outs, scratch, previous, 2 * 10**10, 36)


def local_call(body, name, info, inputs, outs, scratch, specs=None, placed=()):
    inputs = [info, TOKEN[0]] + list(inputs)

    def parted(*refs):
        refs = refs[: len(inputs)] + refs[len(inputs) + len(placed) :]
        first = len(inputs)
        body(refs[0], refs[2:first], refs[first : first + len(outs)], refs[first + len(outs) + 1 :])

    results = pl.pallas_call(
        parted,
        out_shape=list(outs) + [loose(8, 128)],
        in_specs=[SCALARS] + [ANY] * (len(inputs) - 1 + len(placed)),
        out_specs=(specs or [ANY] * len(outs)) + [ANY],
        scratch_shapes=scratch,
        input_output_aliases={len(inputs) + i: i for i in range(len(placed))},
        compiler_params=pltpu.CompilerParams(vmem_limit_bytes=12 * 1024 * 1024),
        cost_estimate=pl.CostEstimate(flops=10**10, bytes_accessed=10**8, transcendentals=0),
        name=name,
    )(*inputs, *in_hbm(placed))
    TOKEN[0] = results[-1]
    return results[:-1]


def left_dims(done):
    return [axis for axis in (3, 2, 1, 0) if axis not in done]


def picked(ref, dims, axis, index):
    return ref.at[(slice(None),) * dims.index(axis) + (index,)]


def reduce_stage(sizes, order, step, info, arrays):
    shape = arrays[0].shape
    count = len(arrays)
    dims = left_dims(order[:step])
    parting = step < len(order) - 1
    if parting:
        axis = order[step]
        at = dims.index(axis)
        outs = [loose(*shape[:at], *shape[at + 1 :])] * sizes[axis]
    else:
        outs = [loose(*shape)]

    def body(info, ins, outs, scratch):
        held, sem = scratch
        wait_all(start_all([pltpu.make_async_copy(ref, held.at[i], sem.at[i]) for i, ref in enumerate(ins)]))
        total = held[0]
        for i in range(1, count):
            total = total + held[i]
        held[0] = total
        stores = []
        for by in range(len(outs)):
            source = held.at[0]
            if parting:
                source = picked(source, dims, axis, lax.rem(info[1 + axis] + by, sizes[axis]))
            stores.append(pltpu.make_async_copy(source, outs[by], sem.at[count + by]))
        wait_all(start_all(stores))

    scratch = [pltpu.VMEM((count,) + shape, jnp.float32), pltpu.SemaphoreType.DMA((count + len(outs),))]
    return local_call(body, "reduce_step", info, arrays, outs, scratch)


def place_stage(sizes, order, step, info, arrays):
    axis = order[step]
    dims = left_dims(order[:step])
    at = dims.index(axis)
    shape = arrays[0].shape
    count = sizes[axis]

    def body(info, ins, outs, scratch):
        copies = []
        for by in range(count):
            target = picked(outs[0], dims, axis, lax.rem(info[1 + axis] + count - by, count))
            copies.append(pltpu.make_async_copy(ins[by], target, scratch[0].at[by]))
        wait_all(start_all(copies))

    out = loose(*shape[:at], count, *shape[at:])
    return local_call(body, "place_step", info, arrays, [out], [pltpu.SemaphoreType.DMA((count,))])[0]


def out_copies(sizes, axis, info, kind, half, sources, outs, stage, sem):
    x, y, near, far = sizes
    rows = unit_shape(sizes)[3]
    depth = near * far // 4
    count = sizes[axis]
    copies = []

    def put(source, target):
        at = len(copies)
        load = pltpu.make_async_copy(source, stage.at[at], sem.at[0, at])
        copies.append((load, pltpu.make_async_copy(stage.at[at], target, sem.at[1, at])))

    for by, piece in sources:
        place = lax.rem(info[1 + axis] + count - by, count)
        for at in range(near * far if axis < 2 else far):
            if axis == 2:
                source = piece.at[at, :, :, pl.ds(0, rows)]
                z = at * near + place
            else:
                source = piece.at[at // near, at % near, :, pl.ds(0, rows)]
                z = at
            width = piece.shape[-1]
            first = half * width
            if kind == "rows":
                out, inside = outs[0], z
            elif kind == "columns":
                part = lax.div(z, depth) if axis == 2 else z // depth
                first = pl.multiple_of(part * D + first, 128) if axis == 2 else part * D + first
                out, inside = outs[0], lax.rem(z, depth) if axis == 2 else z % depth
            else:
                out, inside = outs[z // depth], z % depth
            lanes = pl.ds(first, width)
            if axis == 0:
                put(source, out.at[inside, :, place, :, lanes])
            elif axis == 1:
                put(source, out.at[inside, place, :, :, lanes])
            else:
                put(source, out.at[inside, :, :, :, lanes])
    start_all([load for load, _ in copies])
    for load, store in copies:
        load.wait()
        store.start()
    return [store for _, store in copies]


def out_scratch(sizes, axis, shape, pieces):
    rows, count = unit_shape(sizes)[3], pieces * (sizes[3] if axis == 2 else sizes[2] * sizes[3])
    inner = shape[1:3] if axis == 2 else shape[2:3]
    return [pltpu.VMEM((count, *inner, rows, shape[-1]), jnp.float32), pltpu.SemaphoreType.DMA((2, count))]


def out_shapes(sizes, kind):
    x, y, near, far = sizes
    rows = unit_shape(sizes)[3]
    depth = near * far // 4
    if kind == "rows":
        return [struct(near * far, y, x, rows, D)]
    if kind == "columns":
        return [struct(depth, y, x, rows, 4 * D)]
    return [struct(depth, y, x, rows, D)] * 4


def own_stage(sizes, axis, info, whole, kind, half, placed):
    def body(info, ins, outs, scratch):
        wait_all(out_copies(sizes, axis, info, kind, half, [(0, ins[0])], outs, *scratch))

    scratch = out_scratch(sizes, axis, whole.shape, 1)
    return local_call(body, "place_own", info, [whole], out_shapes(sizes, kind), scratch, None, placed)


def last_stage(sizes, axis, info, arrays, kind, half, placed):
    rows = unit_shape(sizes)[3]
    count = sizes[axis]
    shapes, specs = out_shapes(sizes, kind), None
    scratch = out_scratch(sizes, axis, arrays[0].shape, count - 1)
    has_small = arrays[0].shape[3] > rows
    if has_small:
        specs = [ANY] * len(shapes) + [LOCAL] * 2
        shapes += [loose(1, 2), loose(1, 3)]
        scratch += [pltpu.VMEM((8, 256), jnp.float32), pltpu.SemaphoreType.DMA((1,))]

    def body(info, ins, outs, scratch):
        sources = [(by, ins[by]) for by in range(1, count)]
        copies = out_copies(sizes, axis, info, kind, half, sources, outs, *scratch[:2])
        if has_small:
            tile_v, sem = scratch[2:]
            for by in range(count):

                @pl.when(info[1 + axis] == by)
                def _():
                    source = ins[by].at[0, 0, 0, pl.ds(rows, 8), pl.ds(0, 256)]
                    copy = pltpu.make_async_copy(source, tile_v, sem.at[0])
                    copy.start()
                    copy.wait()

            tile = tile_v[0:1, 0:128]
            outs[-2][...] = tile[:, 4:6]
            outs[-1][...] = jnp.sqrt(tile[:, 0:3] / (jnp.maximum(tile[:, 3:4], 1.0) * D))
        wait_all(copies)

    return local_call(body, "place_last", info, arrays, shapes, scratch, specs, placed)


def extents(count):
    bits = count.bit_length() - 1
    if 1 << bits != count:
        return (1, 1, 1, count)
    side = 1 << (bits // 3)
    depth = count // (side * side)
    near = 2 if depth > 1 else 1
    return (side, side, near, depth // near)


def shifted(value, axis, by, sizes):
    count = math.prod(sizes)
    stride, length = math.prod(sizes[:axis]), sizes[axis]
    pairs = []
    for chip in range(count):
        along = (chip // stride) % length
        pairs.append((chip, chip + ((along + by) % length - along) * stride))
    return lax.ppermute(value, "dp", pairs)


def summing(slots, order, kind, half, results, sizes, info):
    pieces = list(slots)
    steps = len(order)
    for step in range(1, steps + 1):
        axis = order[step - 1]
        pieces = [pieces[0]] + [
            shifted(pieces[by if step < steps else 0], axis, by, sizes) for by in range(1, sizes[axis])
        ]
        yield pieces[-1]
        pieces = reduce_stage(sizes, order, step, info, pieces)
    whole = pieces[0]
    for step in range(steps - 2, -1, -1):
        axis = order[step]
        copies = [whole] + [shifted(whole, axis, by, sizes) for by in range(1, sizes[axis])]
        yield copies[-1]
        if step:
            whole = place_stage(sizes, order, step, info, copies)
    placed = results.get(kind, ())
    results[kind] = own_stage(sizes, order[0], info, whole, kind, half, placed)
    yield
    outs = last_stage(sizes, order[0], info, copies, kind, half, results[kind])
    results[kind] = outs[: len(out_shapes(sizes, kind))]
    results["small"] = outs[len(results[kind]) :] or results.get("small")
    yield


def shards(stream_in, cotangent, segment_ids, pad_mask, w_query, w_key, w_value, w_out, w_in, w_back, alphas):
    weights = [weight[0] for weight in (w_query, w_key, w_value, w_out, w_in, w_back)]
    sizes = extents(lax.axis_size("dp"))
    chip = lax.axis_index("dp")
    section = lax.axis_index("section")
    places, left = [], chip
    for size in sizes:
        places.append(lax.rem(left, size))
        left = lax.div(left, size)
    info = jnp.stack([section] + places).astype(jnp.int32)
    TOKEN[0] = jnp.zeros((8, 128), jnp.float32)
    state, chain = None, None

    def forward_step(tick, received):
        return forward_tick(tick, info, alphas, segment_ids, pad_mask, stream_in, received, weights, state)

    def chain_step(tick, received):
        saved = state[2:7]
        return backward_chain(
            tick, info, alphas, segment_ids, pad_mask, cotangent, received, state[8], saved, weights, chain
        )

    received, upstreams = [None], [None]
    for tick in range(2):
        sent, state = forward_step(tick, received[tick])
        received.append(lax.ppermute(sent, "section", [(0, 1)]))
    for tick in range(3):
        *chain, sent = chain_step(tick, upstreams[tick])
        if tick < 2:
            upstreams.append(lax.ppermute(sent, "section", [(1, 0)]))
        if tick == 0:
            _, state = forward_step(2, received[2])
    acts, saved_s, _, _, _, saved_o, _, saved_m, saved_p, sums = state
    befores, spreads, firsts, passed, small = chain
    orders = {key: tuple("xynf".index(axis) for axis in order) for key, order in ORDERS.items()}
    results, streams = {}, {}

    def gradients(index):
        pair, kind = ("Bb", "Ii", "Aa")[index], ("rows", "columns", "four")[index]
        pair = [key for key in pair if key in orders]
        axes = [orders[key][0] for key in pair]
        if index == 0:
            slots = backward_back(info, alphas, upstreams[1:], cotangent, saved_p, sizes, axes)
        elif index == 1:
            slots = backward_inner(info, saved_m, befores, sizes, axes)
        else:
            slots = backward_attention(info, pad_mask, saved_s, saved_o, spreads, firsts, sums, small, sizes, axes)
        for half, key in enumerate(pair):
            count = sizes[axes[half]]
            streams[key] = summing(slots[:count], orders[key], kind, half, results, sizes, info)
            slots = slots[count:]

    made, steps, owned = 0, {}, set()
    for item in PROGRAM:
        if item == "|":
            gradients(made)
            made += 1
            continue
        steps[item] = steps.get(item, 0) + 1
        if steps[item] == 8:
            for key in [key for key in steps if steps[key] in (7, 8) and key not in owned]:
                owned.add(key)
                next(streams[key])
        next(streams[item])
    attention, inner, back = results["four"], results["columns"], results["rows"]
    return (
        acts[None, :, None],
        passed[None, :, None],
        attention[0].reshape(1, D, D),
        attention[1].reshape(1, D, D),
        attention[2].reshape(1, D, D),
        attention[3].reshape(1, D, D),
        inner[0].reshape(1, D, -1),
        back[0].reshape(1, -1, D),
        results["small"][0],
        results["small"][1],
    )


def solution(mesh):
    in_specs = (
        P(None, "dp", None, None),
        P(None, "dp", None, None),
        P(None, "dp", None),
        P(None, "dp", None),
        P("section", None, None),
        P("section", None, None),
        P("section", None, None),
        P("section", None, None),
        P("section", None, None),
        P("section", None, None),
        P("section", None),
    )
    out_specs = (
        P("section", None, "dp", None, None),
        P("section", None, "dp", None, None),
        P("section", None, None),
        P("section", None, None),
        P("section", None, None),
        P("section", None, None),
        P("section", None, None),
        P("section", None, None),
        P("section", None),
        P("section", None),
    )
    return jax.shard_map(shards, mesh=mesh, in_specs=in_specs, out_specs=out_specs, check_vma=False)
```

```python
import functools
import math
import jax
import jax.numpy as jnp
from jax import lax
from jax.experimental import pallas as pl
from jax.experimental.pallas import tpu as pltpu
from jax.sharding import PartitionSpec as P

D = 512
HEADS = 8
HEAD_DIM = 64
GELU_A = math.sqrt(2.0 / math.pi)
GELU_B = 0.044715
ORDERS = {"B": "nxyf", "b": "xynf", "I": "yxnf", "i": "nyxf", "A": "xnyf", "a": "xynf"}
PROGRAM = "|Bb|Bb|IbaiIBbBAaaBbiaIbABiIbaiAIAaBiIAaiAIBiAbaIiA"


TOKEN = [None]


def start_all(copies):
    for copy in copies:
        copy.start()
    return copies


def wait_all(copies):
    for copy in copies:
        copy.wait()


def split(value):
    high = value.astype(jnp.bfloat16)
    low = (value - high.astype(jnp.float32)).astype(jnp.bfloat16)
    return (high, low)


def stacked(value):
    return jnp.concatenate(split(value), axis=0)


def dot(left_side, right_side):
    return jnp.dot(left_side, right_side, preferred_element_type=jnp.float32)


def dot_rows(left_side, right_side):
    return lax.dot_general(
        left_side, right_side, (((1,), (1,)), ((), ())), preferred_element_type=jnp.float32
    )


def folded(product):
    half = product.shape[0] // 2
    return product[:half] + product[half:]


def bands(rows, step=32):
    return [slice(at, at + step) for at in range(0, rows, step)]


def put_split(target, source, factor=None):
    for band in bands(source.shape[0]):
        high, low = split(source[band, :] if factor is None else source[band, :] * factor)
        target[0, band, :] = high
        target[1, band, :] = low


def turned(target, source):
    rows, cols = source.shape
    for row in bands(rows, 128):
        for col in bands(cols, 128):
            target[col, row] = source[row, col].T


def two_dots(left_side, right_side):
    return dot(left_side[0], right_side) + dot(left_side[1], right_side)


def gelu_inner(value):
    return jnp.tanh(value * (GELU_A + (GELU_A * GELU_B) * (value * value)))


def tile_of(numbers):
    lane = lax.broadcasted_iota(jnp.int32, (8, 128), 1)
    tile = jnp.zeros((8, 128), jnp.float32)
    for index, number in enumerate(numbers):
        tile = jnp.where(lane == index, number, tile)
    return tile


def fill_bias(bias_ref, segment_row, valid_row):
    blocks = segment_row.shape[1] // 128
    segment_col = jnp.broadcast_to(segment_row, (128, segment_row.shape[1])).T
    valid_col = jnp.broadcast_to(valid_row, (128, valid_row.shape[1])).T
    for kb in range(blocks):
        ks = slice(kb * 128, kb * 128 + 128)
        for qb in range(kb, blocks):
            qs = slice(qb * 128, qb * 128 + 128)
            k_place = lax.broadcasted_iota(jnp.int32, (128, 128), 0) + kb * 128
            q_place = lax.broadcasted_iota(jnp.int32, (128, 128), 1) + qb * 128
            allowed = (segment_col[ks] == segment_row[:, qs]) & (k_place <= q_place)
            allowed = allowed & ((valid_col[ks] > 0) | (k_place == q_place))
            bias_ref[ks, qs] = jnp.where(allowed, 0.0, -1e30)


def halves_of(value):
    lane = lax.broadcasted_iota(jnp.int32, value.shape, 1)
    zero = jnp.zeros_like(value)
    return (jnp.where(lane < HEAD_DIM, value, zero), jnp.where(lane < HEAD_DIM, zero, value))


def pair_scores(keys_cat, queries_high, queries_low):
    sides = []
    for high, low in zip(halves_of(queries_high), halves_of(queries_low)):
        sides.append(jnp.concatenate([high, high, low], axis=1))
    return dot_rows(keys_cat, jnp.concatenate(sides, axis=0))


def three_lanes(value):
    high, low = split(value)
    return jnp.concatenate([high, low, high], axis=1)


def fetch_rows(alphas, segments, valids, alphas_s, rows_v, sem):
    return start_all(
        [
            pltpu.make_async_copy(alphas, alphas_s, sem.at[0]),
            pltpu.make_async_copy(segments, rows_v.at[0], sem.at[1]),
            pltpu.make_async_copy(valids, rows_v.at[1], sem.at[2]),
        ]
    )


def forward_body(tick, *refs):
    (info, alphas, segments, valids, streams, wq, wk, wv, wo, wi, wb) = refs[:11]
    received = streams.at[0, 0] if tick == 0 else refs[12]
    refs = refs[12 + (0 if tick == 0 else 11) :]
    (acts, sent, saved_s, saved_q, saved_k, saved_v, saved_o, saved_l, saved_m, saved_p, sums, _) = refs[:12]
    (s_v, wq_v, wk_v, wv_v, wo_v, wi_v, wb_v, q_v, k_v, v_v, ot_v, l_v, m_v, p_v, a_v, t_v, bias_v, x_v, w_v, c_v, h_v, alphas_s, rows_v, in_sem, out_sem, row_sem) = refs[12:]
    section = info[0]
    micro = tick - section
    rows = s_v.shape[0]
    blocks = rows // 128
    parts = wi_v.shape[1] // 512

    @pl.when((micro >= 0) & (micro < 2))
    def _():
        pairs = [(wq, wq_v), (wk, wk_v), (wv, wv_v), (wo, wo_v), (wi, wi_v), (wb, wb_v)]
        loads = [pltpu.make_async_copy(a, b, in_sem.at[i]) for i, (a, b) in enumerate(pairs)]

        @pl.when(section == 0)
        def _():
            pltpu.make_async_copy(streams.at[micro, 0], s_v, in_sem.at[6]).start()

        @pl.when(section != 0)
        def _():
            pltpu.make_async_copy(received, s_v, in_sem.at[6]).start()

        loads[0].start()
        small = fetch_rows(alphas, segments, valids, alphas_s, rows_v, row_sem)
        pltpu.make_async_copy(received, s_v, in_sem.at[6]).wait()
        start_all(loads[1:])
        put_split(x_v, s_v)
        for index, (weight, target) in enumerate(((wq_v, q_v), (wk_v, k_v), (wv_v, v_v))):
            loads[index].wait()
            value = two_dots(x_v, weight[...])
            target[...] = value * 0.125 if index == 0 else value
        wait_all(small)
        segment_row = rows_v[0, micro].astype(jnp.float32)
        valid_row = rows_v[1, micro].astype(jnp.float32)
        fill_bias(bias_v, segment_row, valid_row)

        stores = []

        def store(source, target):
            copy = pltpu.make_async_copy(source, target, out_sem.at[len(stores)])
            copy.start()
            stores.append(copy)

        store(s_v, saved_s.at[micro])
        store(q_v, saved_q.at[micro])
        store(k_v, saved_k.at[micro])
        store(v_v, saved_v.at[micro])
        made = {}

        def put_scores(index):
            pair, qb = units[index]
            lanes = slice(pair * 128, pair * 128 + 128)
            if pair not in made:
                made[pair] = (three_lanes(k_v[:, lanes]), split(q_v[:, lanes]), split(v_v[:, lanes].T))
            keys_cat, queries, _ = made[pair]
            qs = slice(qb * 128, qb * 128 + 128)
            ks = (qb + 1) * 128
            w_v[index % 2, :ks, :] = pair_scores(keys_cat[:ks], queries[0][qs], queries[1][qs])

        units = [(pair, qb) for pair in range(HEADS // 2) for qb in range(blocks)]
        put_scores(0)
        for index, (pair, qb) in enumerate(units):
            if index + 1 < len(units):
                put_scores(index + 1)
            values_high, values_low = made[pair][2]
            qs = slice(qb * 128, qb * 128 + 128)
            ks = (qb + 1) * 128
            for head in range(2):
                own = slice(head * 128, head * 128 + 128)
                top = None
                for band in bands(ks, 128):
                    part = w_v[index % 2, band, own] + bias_v[band, qs]
                    w_v[index % 2, band, own] = part
                    most = jnp.max(part, axis=0, keepdims=True)
                    top = most if top is None else jnp.maximum(top, most)
                total = None
                for band in bands(ks, 128):
                    probs = jnp.exp(w_v[index % 2, band, own] - top)
                    more = jnp.sum(probs, axis=0, keepdims=True)
                    total = more if total is None else total + more
                    high, low = split(probs)
                    c_v[head, band, :128] = high
                    c_v[head, band, 128:] = low
                hs = slice(head * HEAD_DIM, head * HEAD_DIM + HEAD_DIM)
                both = jnp.concatenate([values_high[hs, :ks], values_low[hs, :ks]], axis=0)
                mixed = folded(dot(both, c_v[head, :ks, :128])) + dot(values_high[hs, :ks], c_v[head, :ks, 128:])
                at = slice(pair * 128 + head * HEAD_DIM, pair * 128 + head * HEAD_DIM + HEAD_DIM)
                ot_v[at, qs] = mixed / total
                l_v[pair, head : head + 1, qs] = top + jnp.log(total)
        store(ot_v, saved_o.at[micro])
        store(l_v, saved_l.at[micro])
        turned(m_v, ot_v)
        put_split(x_v, m_v)
        loads[3].wait()
        a_v[...] = two_dots(x_v, wo_v[...])
        valid_col = jnp.broadcast_to(valid_row, (128, rows)).T
        attn_sum = jnp.zeros((32, D), jnp.float32)
        for band in bands(rows):
            attn = a_v[band, :] * alphas_s[0, 0]
            attn_sum = attn_sum + attn * attn * jnp.concatenate([valid_col[band]] * (D // 128), axis=1)
            middle = s_v[band, :] + attn
            m_v[band, :] = middle
            high, low = split(middle)
            x_v[0, band, :] = high
            x_v[1, band, :] = low
        store(m_v, saved_m.at[micro])
        loads[4].wait()

        def put_before(part):
            p_v[:, part * 512 : part * 512 + 512] = two_dots(x_v, wi_v[:, part * 512 : part * 512 + 512])

        put_before(0)
        loads[5].wait()
        for part in range(parts):
            cols = slice(part * 512, part * 512 + 512)
            store(p_v.at[:, pl.ds(part * 512, 512)], saved_p.at[micro, :, pl.ds(part * 512, 512)])
            if part + 1 < parts:
                put_before(part + 1)
            for band in bands(rows):
                before = p_v[band, cols]
                high, low = split(0.5 * before * (1.0 + gelu_inner(before)))
                h_v[part % 2, 0, band, :] = high
                h_v[part % 2, 1, band, :] = low
            more = two_dots(h_v.at[part % 2], wb_v[cols, :])
            a_v[...] = a_v[...] + more if part else more
        result_sum = jnp.zeros((32, D), jnp.float32)
        ffn_sum = jnp.zeros((32, D), jnp.float32)
        for band in bands(rows):
            weighting = jnp.concatenate([valid_col[band]] * (D // 128), axis=1)
            ffn = a_v[band, :] * alphas_s[0, 1]
            result = m_v[band, :] + ffn
            a_v[band, :] = result
            result_sum = result_sum + result * result * weighting
            ffn_sum = ffn_sum + ffn * ffn * weighting
        store(a_v, sent)
        store(a_v, acts.at[micro])
        t_v[...] = tile_of([jnp.sum(result_sum), jnp.sum(attn_sum), jnp.sum(ffn_sum)])
        store(t_v, sums.at[micro])
        wait_all(stores)


def struct(*shape):
    return pltpu.HBM(shape, jnp.float32)


def loose(*shape):
    return jax.ShapeDtypeStruct(shape, jnp.float32)


def in_hbm(arrays):
    return [pltpu.with_memory_space_constraint(array, pltpu.HBM) for array in arrays]


ANY = pl.BlockSpec(memory_space=pl.ANY)
SCALARS = pl.BlockSpec(memory_space=pltpu.SMEM)
LOCAL = pl.BlockSpec(memory_space=pltpu.VMEM)


def forward_tick(tick, info, alphas, segments, valids, streams, received, weights, state):
    micro_count, _, rows, width = streams.shape
    inner = weights[4].shape[1]
    whole = struct(micro_count, rows, width)
    shapes = [
        whole,
        struct(rows, width),
        whole,
        whole,
        whole,
        whole,
        struct(micro_count, width, rows),
        struct(micro_count, HEADS // 2, 8, rows),
        whole,
        struct(micro_count, rows, inner),
        struct(micro_count, 8, 128),
        loose(8, 128),
    ]
    kept = [0, 2, 3, 4, 5, 6, 7, 8, 9, 10]
    extra = [] if state is None else [received] + in_hbm(state)
    aliases = {} if state is None else {13 + i: out for i, out in enumerate(kept)}
    f32, bf16 = jnp.float32, jnp.bfloat16
    vmem, dma = pltpu.VMEM, pltpu.SemaphoreType.DMA
    scratch = [vmem((rows, width), f32)] + [vmem(w.shape, bf16) for w in weights]
    scratch += [vmem((rows, width), f32)] * 3 + [vmem((width, rows), f32), vmem((HEADS // 2, 8, rows), f32)]
    scratch += [vmem((rows, width), f32), vmem((rows, inner), f32), vmem((rows, width), f32)]
    scratch += [vmem((8, 128), f32), vmem((rows, rows), f32), vmem((2, rows, width), bf16)]
    scratch += [vmem((2, rows, 256), f32), vmem((2, rows, 256), bf16), vmem((2, 2, rows, 512), bf16)]
    scratch += [pltpu.SMEM(alphas.shape, f32), vmem((2,) + segments.shape, jnp.int32)]
    scratch += [dma((7,)), dma((10 + inner // 512,)), dma((3,))]
    outs = pl.pallas_call(
        functools.partial(forward_body, tick),
        out_shape=shapes,
        in_specs=[SCALARS] + [ANY] * (11 + len(extra)),
        out_specs=[ANY] * len(shapes),
        scratch_shapes=scratch,
        input_output_aliases=aliases,
        compiler_params=pltpu.CompilerParams(vmem_limit_bytes=28 * 1024 * 1024),
        cost_estimate=pl.CostEstimate(flops=10**10, bytes_accessed=2 * 10**7, transcendentals=10**6),
        name="layer_forward",
    )(info, *in_hbm([alphas, segments, valids, streams, *weights]), TOKEN[0], *extra)
    TOKEN[0] = outs[-1]
    return (outs[1], [outs[i] for i in kept])


def unit_shape(sizes):
    x, y, near, far = sizes
    return (near * far, y, x, 4 * D // (x * y * near * far), D)


def slot_structs(sizes, axes, more=0):
    x, y, near, far = sizes
    structs = []
    for axis in axes:
        shape = [size for index, size in ((3, far), (2, near), (1, y), (0, x)) if index != axis]
        structs += [struct(*shape, unit_shape(sizes)[3] + (0 if structs else more), D // len(axes))] * sizes[axis]
    return structs


def put_part(unit, part, value):
    depth = unit.shape[0] // 4
    unit[pl.ds(part * depth, depth)] = value.reshape((depth,) + unit.shape[1:])


def slot_copies(info, sizes, axes, unit, slots, sems, part):
    x, y, near, far = sizes
    depth, rows = near * far // 4, unit.shape[3]
    copies, first = [], 0
    for half, axis in enumerate(axes):
        lanes = pl.ds(half * (D // len(axes)), D // len(axes))
        for by in range(sizes[axis]):
            place = lax.rem(info[1 + axis] + by, sizes[axis])
            slot = slots[first + by]
            if axis == 2:
                pairs = [
                    (unit.at[at * near + place, :, :, :, lanes], slot.at[at, :, :, pl.ds(0, rows)])
                    for at in range(far)
                    if part * depth < (at + 1) * near <= (part + 1) * depth
                ]
            else:
                pairs = []
                for at in range(part * depth, (part + 1) * depth):
                    source = unit.at[at, :, place, :, lanes] if axis == 0 else unit.at[at, place, :, :, lanes]
                    pairs.append((source, slot.at[at // near, at % near, :, pl.ds(0, rows)]))
            for source, target in pairs:
                copies.append(pltpu.make_async_copy(source, target, sems.at[part, len(copies)]))
        first += sizes[axis]
    return copies


def copy_count(sizes, axes):
    return sum(sizes[axis] for axis in axes) * max(1, sizes[2] * sizes[3] // 4)


def three_dots(left_high, left_low, right_high, right_low):
    return dot(left_high, right_high) + dot(left_low, right_high) + dot(left_high, right_low)


def back_body(count, sizes, axes, *refs):
    info, alphas = refs[:2]
    upstreams, targets, saved_p = refs[2:4], refs[4], refs[5]
    slots, refs = refs[7 : 7 + count], refs[8 + count :]
    g_v, gh_v, p_v, h_v, w_v, in_sem, out_sem = refs
    parts = p_v.shape[0]
    rows = g_v.shape[1]

    def load(part, micro):
        cols = pl.ds(part * 512, 512)
        return pltpu.make_async_copy(
            saved_p.at[micro, :, cols], p_v.at[part, pl.ds(micro * rows, rows)], in_sem.at[part, micro]
        )

    for micro in range(2):

        @pl.when(info[0] == 0)
        def _():
            pltpu.make_async_copy(upstreams[micro], g_v.at[micro], in_sem.at[parts, micro]).start()

        @pl.when(info[0] != 0)
        def _():
            pltpu.make_async_copy(targets.at[micro, 0], g_v.at[micro], in_sem.at[parts, micro]).start()

    start_all([load(0, micro) for micro in range(2)])
    for micro in range(2):
        pltpu.make_async_copy(targets.at[micro, 0], g_v.at[micro], in_sem.at[parts, micro]).wait()
    for part in range(1, parts):
        start_all([load(part, micro) for micro in range(2)])
    for micro in range(2):
        put_split(gh_v.at[:, pl.ds(micro * rows, rows)], g_v.at[micro], alphas[0, 1])

    def put_left(part):
        for micro in range(2):
            load(part, micro).wait()
        for row in bands(2 * rows, 128):
            for col in bands(512, 128):
                before = p_v[part, row, col].T
                high, low = split(0.5 * before * (1.0 + gelu_inner(before)))
                h_v[part % 2, 0, col, row] = high
                h_v[part % 2, 1, col, row] = low

    stores = []
    put_left(0)
    for part in range(parts):
        if part + 1 < parts:
            put_left(part + 1)
        left = h_v.at[part % 2]
        put_part(w_v, part, three_dots(left[0], left[1], gh_v[0], gh_v[1]))
        stores += start_all(slot_copies(info, sizes, axes, w_v, slots, out_sem, part))
    wait_all(stores)


def chain_body(tick, extra, *refs):
    info, received = refs[:2]
    alphas, segments, valids, targets, saved_p = refs[2:7]
    sources = refs[7:12]
    wi, wb = refs[12:14]
    weights = refs[14:18]
    refs = refs[19 + extra :]
    (befores, spreads, firsts, passed, small, sent, _) = refs[:7]
    (g_v, p_v, wi_v, wb_v, gs_v, d_v, b_v) = refs[7:14]
    held = refs[14:19]
    weights_v = refs[19:23]
    (bias_v, do_v, dt_v, dl_v, qt_v, dk_v, dv_v, x_v, f_v, y_v, t_v, h_v, s_v, c_v, alphas_s, rows_v, in_sem, part_sem, w_sem, out_sem, row_sem) = refs[23:]
    parts = p_v.shape[0]
    rows = bias_v.shape[0]
    blocks = rows // 128
    (q_v, k_v, v_v, o_v, l_v) = held
    (wq_v, wk_v, wv_v, wo_v) = weights_v
    section = info[0]
    micro = tick - (1 - section)

    @pl.when((micro >= 0) & (micro < 2))
    def _():
        def loads(part):
            cols = pl.ds(part * 512, 512)
            return [
                pltpu.make_async_copy(wb.at[cols], wb_v.at[part], part_sem.at[part, 0]),
                pltpu.make_async_copy(saved_p.at[micro, :, cols], p_v.at[part], part_sem.at[part, 1]),
                pltpu.make_async_copy(wi.at[:, cols], wi_v.at[part], part_sem.at[part, 2]),
            ]

        @pl.when(section == 0)
        def _():
            pltpu.make_async_copy(received if tick else targets.at[micro, 0], g_v, in_sem.at[5]).start()

        @pl.when(section != 0)
        def _():
            pltpu.make_async_copy(targets.at[micro, 0], g_v, in_sem.at[5]).start()

        rows_in = fetch_rows(alphas, segments, valids, alphas_s, rows_v, row_sem)
        start_all(loads(0))
        fetches = [pltpu.make_async_copy(a, b, w_sem.at[i]) for i, (a, b) in enumerate(zip(weights, weights_v))]
        later = [pltpu.make_async_copy(a.at[micro], b, in_sem.at[i]) for i, (a, b) in enumerate(zip(sources, held))]
        wait_all(rows_in)
        segment_row = rows_v[0, micro].astype(jnp.float32)
        valid_row = rows_v[1, micro].astype(jnp.float32)
        fill_bias(bias_v, segment_row, valid_row)
        pltpu.make_async_copy(targets.at[micro, 0], g_v, in_sem.at[5]).wait()
        for part in range(1, parts):
            start_all(loads(part))
        start_all(fetches[::-1])
        start_all(later)
        put_split(gs_v, g_v, alphas_s[0, 1])

        def put_hidden(part):
            wait_all(loads(part))
            h_v[part % 2] = dot_rows(gs_v[0], wb_v[part]) + dot_rows(gs_v[1], wb_v[part])

        inner_sum = jnp.zeros((32, 512), jnp.float32)
        put_hidden(0)
        for part in range(parts):
            cols = slice(part * 512, part * 512 + 512)
            if part + 1 < parts:
                put_hidden(part + 1)
            for band in bands(rows):
                grad_hidden = h_v[part % 2, band, :]
                before = p_v[part, band, :]
                square = before * before
                inner = jnp.tanh(before * (GELU_A + (GELU_A * GELU_B) * square))
                above = 0.5 + 0.5 * inner
                inner_sum = inner_sum + grad_hidden * (before * above)
                slope = above + before * (1.0 - inner * inner) * (0.5 * GELU_A + (1.5 * GELU_A * GELU_B) * square)
                high, low = split(grad_hidden * slope)
                b_v[0, band, cols] = high
                b_v[1, band, cols] = low
            more = dot_rows(b_v[0, :, cols], wi_v[part]) + dot_rows(b_v[1, :, cols], wi_v[part])
            d_v[...] = d_v[...] + more if part else more
        total_inner = jnp.sum(inner_sum)
        stores = start_all([pltpu.make_async_copy(b_v, befores.at[micro], out_sem.at[0])])
        for band in bands(rows):
            middle = g_v[band, :] + d_v[band, :]
            d_v[band, :] = middle
            high, low = split(middle * alphas_s[0, 0])
            f_v[0, band, :] = high
            f_v[1, band, :] = low
        stores += start_all([pltpu.make_async_copy(f_v, firsts.at[micro], out_sem.at[1])])
        wait_all(fetches)
        wait_all(later)
        do_v[...] = dot_rows(f_v[0], wo_v[...]) + dot_rows(f_v[1], wo_v[...])
        turned(dt_v, do_v)
        total_mixed = jnp.float32(0.0)
        for head in range(HEADS):
            hs = slice(head * HEAD_DIM, head * HEAD_DIM + HEAD_DIM)
            spread = jnp.sum(dt_v[hs, :] * o_v[hs, :], axis=0, keepdims=True)
            dl_v[head // 2, head % 2 : head % 2 + 1, :] = spread
            total_mixed = total_mixed + jnp.sum(spread)
        made = {}

        def put_products(index):
            pair, qb = units[index]
            lanes = slice(pair * 128, pair * 128 + 128)
            if pair not in made:
                keys = k_v[:, lanes]
                made[pair] = (
                    three_lanes(keys),
                    three_lanes(v_v[:, lanes]),
                    split(q_v[:, lanes]),
                    split(do_v[:, lanes]),
                    split(keys.T),
                )
            keys_cat, values_cat, queries, mixed, _ = made[pair]
            qs = slice(qb * 128, qb * 128 + 128)
            ks = (qb + 1) * 128
            s_v[index % 2, 0, :ks, :] = pair_scores(keys_cat[:ks], queries[0][qs], queries[1][qs])
            s_v[index % 2, 1, :ks, :] = pair_scores(values_cat[:ks], mixed[0][qs], mixed[1][qs])

        def product(left_cat, right_high, right_low):
            above = jnp.concatenate([right_high, right_low], axis=1)
            below = jnp.concatenate([right_high, jnp.zeros_like(right_high)], axis=1)
            value = dot(left_cat, jnp.concatenate([above, below], axis=0))
            return value[:, :128] + value[:, 128:]

        units = [(pair, qb) for pair in range(HEADS // 2) for qb in range(blocks - 1, -1, -1)]
        put_products(0)
        for index, (pair, qb) in enumerate(units):
            if index + 1 < len(units):
                put_products(index + 1)
            _, _, queries, mixed, keys_turned = made[pair]
            lanes = slice(pair * 128, pair * 128 + 128)
            qs = slice(qb * 128, qb * 128 + 128)
            ks = (qb + 1) * 128
            sides = [halves_of(x[qs]) for x in queries + mixed]
            for head in range(2):
                own = slice(head * 128, head * 128 + 128)
                at = slice(head, head + 1)
                for band in bands(ks, 128):
                    probs = jnp.exp((s_v[index % 2, 0, band, own] + bias_v[band, qs]) - l_v[pair, at, qs])
                    grads = probs * (s_v[index % 2, 1, band, own] - dl_v[pair, at, qs])
                    for place, value in enumerate((probs, grads)):
                        high, low = split(value)
                        c_v[head, place, band, :128] = high
                        c_v[head, place, band, 128:] = low
                q_high, q_low, d_high, d_low = [side[head] for side in sides]
                from_values = product(c_v[head, 0, :ks, :], d_high, d_low)
                from_keys = product(c_v[head, 1, :ks, :], q_high, q_low)
                if qb == blocks - 1 and head == 0:
                    dv_v[:, lanes] = from_values
                    dk_v[:, lanes] = from_keys
                else:
                    dv_v[:ks, lanes] += from_values
                    dk_v[:ks, lanes] += from_keys
                hs = slice(head * HEAD_DIM, head * HEAD_DIM + HEAD_DIM)
                both = jnp.concatenate([keys_turned[0][hs, :ks], keys_turned[1][hs, :ks]], axis=0)
                back = folded(dot(both, c_v[head, 1, :ks, :128])) + dot(keys_turned[0][hs, :ks], c_v[head, 1, :ks, 128:])
                qt_v[pair * 128 + head * HEAD_DIM : pair * 128 + head * HEAD_DIM + HEAD_DIM, qs] = back * 0.125

        turned(do_v, qt_v)
        result = d_v[...]
        for index, (source, weight) in enumerate(((do_v, wq_v), (dk_v, wk_v), (dv_v, wv_v))):
            cols = pl.ds(index * D, D)
            put_split(x_v.at[:, :, cols], source)
            result = result + dot_rows(x_v[0, :, cols], weight[...]) + dot_rows(x_v[1, :, cols], weight[...])
        y_v[...] = result
        t_v[...] = tile_of([total_mixed / alphas_s[0, 0], total_inner / alphas_s[0, 1]])
        stores += start_all(
            [
                pltpu.make_async_copy(y_v, sent, out_sem.at[2]),
                pltpu.make_async_copy(y_v, passed.at[micro], out_sem.at[3]),
                pltpu.make_async_copy(x_v, spreads.at[micro], out_sem.at[4]),
                pltpu.make_async_copy(t_v, small.at[micro], out_sem.at[5]),
            ]
        )
        wait_all(stores)


def inner_body(count, sizes, axes, *refs):
    info, saved_m, befores = refs[:3]
    slots, refs = refs[4 : 4 + count], refs[5 + count :]
    m_v, lt_v, r_v, w_v, in_sem, r_sem, out_sem = refs
    rows = m_v.shape[1]

    def loads(part):
        copies = []
        for micro in range(2):
            for half in range(2):
                source = befores.at[micro, half, :, pl.ds(part * 512, 512)]
                target = r_v.at[part, half, pl.ds(micro * rows, rows)]
                copies.append(pltpu.make_async_copy(source, target, r_sem.at[part, len(copies)]))
        return copies

    first = pltpu.make_async_copy(saved_m, m_v, in_sem.at[0])
    first.start()
    start_all(loads(0))
    first.wait()
    for part in range(1, 4):
        start_all(loads(part))
    turn_left(lt_v, m_v, True)
    stores = []
    for part in range(4):
        wait_all(loads(part))
        put_part(w_v, part, three_dots(lt_v[0], lt_v[1], r_v[part, 0], r_v[part, 1]))
        stores += start_all(slot_copies(info, sizes, axes, w_v, slots, out_sem, part))
    wait_all(stores)


def turn_left(target, source, transpose):
    rows = target.shape[2] // 2
    for micro in range(2):
        for row in bands(source.shape[1], 128):
            for col in bands(source.shape[2], 128):
                value = source[micro, row, col]
                high, low = split(value.T if transpose else value)
                lines, lanes = (col, row) if transpose else (row, col)
                lanes = slice(micro * rows + lanes.start, micro * rows + lanes.stop)
                target[0, lines, lanes] = high
                target[1, lines, lanes] = low


def attention_body(count, sizes, axes, *refs):
    info, valids, saved_s, saved_o, spreads, firsts, sums, small = refs[:8]
    slots, refs = refs[9 : 9 + count], refs[10 + count :]
    (s_v, o_v, st_v, lo_v, r_v, w_v, n_v, t_v, in_sem, r_sem, out_sem) = refs
    rows = s_v.shape[1]

    def loads(part):
        copies = []
        for micro in range(2):
            for half in range(2):
                if part < 3:
                    source = spreads.at[micro, half, :, pl.ds(part * 512, 512)]
                else:
                    source = firsts.at[micro, half]
                target = r_v.at[part, half, pl.ds(micro * rows, rows)]
                copies.append(pltpu.make_async_copy(source, target, r_sem.at[part, micro * 2 + half]))
        return copies

    lefts = [pltpu.make_async_copy(saved_s, s_v, in_sem.at[0]), pltpu.make_async_copy(saved_o, o_v, in_sem.at[1])]
    tiles = [
        pltpu.make_async_copy(sums, n_v.at[pl.ds(0, 2)], in_sem.at[2]),
        pltpu.make_async_copy(small, n_v.at[pl.ds(2, 2)], in_sem.at[3]),
    ]
    lefts[0].start()
    start_all(loads(0))
    lefts[0].wait()
    for part in range(1, 4):
        start_all(loads(part))
    start_all(lefts[1:] + tiles)
    turn_left(st_v, s_v, True)
    stores = []
    for part in range(4):
        if part == 3:
            lefts[1].wait()
            turn_left(lo_v, o_v, False)
        left = lo_v if part == 3 else st_v
        wait_all(loads(part))
        put_part(w_v, part, three_dots(left[0], left[1], r_v[part, 0], r_v[part, 1]))
        stores += start_all(slot_copies(info, sizes, axes, w_v, slots, out_sem, part))
    wait_all(tiles)
    lane = lax.broadcasted_iota(jnp.int32, (8, 256), 1)
    tile = jnp.where(lane == 3, jnp.sum(valids[...].astype(jnp.float32)), jnp.zeros((8, 256), jnp.float32))
    for index in range(3):
        tile = jnp.where(lane == index, n_v[0, 0, index] + n_v[1, 0, index], tile)
    for index in range(2):
        tile = jnp.where(lane == 4 + index, n_v[2, 0, index] + n_v[3, 0, index], tile)
    t_v[...] = tile
    unit_rows = w_v.shape[3]
    axis = axes[0]
    for by in range(sizes[axis]):

        @pl.when(lax.rem(info[1 + axis] + by, sizes[axis]) == 0)
        def _():
            target = slots[by].at[0, 0, 0, pl.ds(unit_rows, 8), pl.ds(0, 256)]
            copy = pltpu.make_async_copy(t_v, target, in_sem.at[0])
            copy.start()
            copy.wait()

    wait_all(stores)


def call(body, name, free, inputs, specs, outs, scratch, before, flops, limit):
    extra = list(before) if before is not None else []
    inputs = list(inputs[:free]) + in_hbm(list(inputs[free:])) + [TOKEN[0]]
    results = pl.pallas_call(
        functools.partial(body, len(extra)),
        out_shape=outs + [loose(8, 128)],
        in_specs=specs + [ANY] * (len(inputs) - len(specs) + len(extra)),
        out_specs=[ANY] * (len(outs) + 1),
        scratch_shapes=scratch,
        input_output_aliases={len(inputs) + i: i for i in range(len(extra))},
        compiler_params=pltpu.CompilerParams(vmem_limit_bytes=limit * 1024 * 1024),
        cost_estimate=pl.CostEstimate(flops=10**12, bytes_accessed=10**9, transcendentals=0),
        name=name,
    )(*inputs, *in_hbm(extra))
    TOKEN[0] = results[-1]
    return results[:-1]


def backward_back(info, alphas, upstreams, targets, before, sizes, axes):
    micros, rows, inner = before.shape
    parts = inner // 512
    vmem, dma = pltpu.VMEM, pltpu.SemaphoreType.DMA
    f32, bf16 = jnp.float32, jnp.bfloat16
    slots = slot_structs(sizes, axes)
    scratch = [
        vmem((micros, rows, D), f32),
        vmem((2, micros * rows, D), bf16),
        vmem((parts, micros * rows, 512), f32),
        vmem((2, 2, 512, micros * rows), bf16),
        vmem(unit_shape(sizes), f32),
        dma((parts + 1, 2)),
        dma((parts, copy_count(sizes, axes))),
    ]

    def body(extra, *refs):
        back_body(len(slots), sizes, axes, *refs)

    inputs = [info, alphas] + list(upstreams) + [targets, before]
    return call(body, "grad_back", 4, inputs, [SCALARS, SCALARS], slots, scratch, None, 5 * 10**9, 24)


def backward_inner(info, middle, befores, sizes, axes):
    micros, rows, _ = middle.shape
    vmem, dma = pltpu.VMEM, pltpu.SemaphoreType.DMA
    f32, bf16 = jnp.float32, jnp.bfloat16
    slots = slot_structs(sizes, axes)
    scratch = [
        vmem(middle.shape, f32),
        vmem((2, D, micros * rows), bf16),
        vmem((4, 2, micros * rows, 512), bf16),
        vmem(unit_shape(sizes), f32),
        dma((1,)),
        dma((4, 4)),
        dma((4, copy_count(sizes, axes))),
    ]

    def body(extra, *refs):
        inner_body(len(slots), sizes, axes, *refs)

    return call(body, "grad_inner", 1, [info, middle, befores], [SCALARS], slots, scratch, None, 5 * 10**9, 24)


def backward_attention(info, valids, stream, mixed, spreads, firsts, sums, small, sizes, axes):
    micros, rows, _ = stream.shape
    vmem, dma = pltpu.VMEM, pltpu.SemaphoreType.DMA
    f32, bf16 = jnp.float32, jnp.bfloat16
    slots = slot_structs(sizes, axes, 8)
    scratch = [
        vmem(stream.shape, f32),
        vmem(mixed.shape, f32),
        vmem((2, D, micros * rows), bf16),
        vmem((2, D, micros * rows), bf16),
        vmem((4, 2, micros * rows, 512), bf16),
        vmem(unit_shape(sizes), f32),
        vmem((4, 8, 128), f32),
        vmem((8, 256), f32),
        dma((4,)),
        dma((4, 4)),
        dma((4, copy_count(sizes, axes))),
    ]

    def body(extra, *refs):
        attention_body(len(slots), sizes, axes, *refs)

    inputs = [info, valids, stream, mixed, spreads, firsts, sums, small]
    return call(body, "grad_attention", 2, inputs, [SCALARS, LOCAL], slots, scratch, None, 5 * 10**9, 28)


def backward_chain(tick, info, alphas, segments, valids, targets, received, before, saved, weights, previous):
    micros, rows, inner = before.shape
    parts = inner // 512
    vmem, dma = pltpu.VMEM, pltpu.SemaphoreType.DMA
    f32, bf16 = jnp.float32, jnp.bfloat16
    wq, wk, wv, wo, wi, wb = weights
    outs = [
        pltpu.HBM((micros, 2, rows, inner), bf16),
        pltpu.HBM((micros, 2, rows, 3 * D), bf16),
        pltpu.HBM((micros, 2, rows, D), bf16),
        struct(micros, rows, D),
        struct(micros, 8, 128),
        struct(rows, D),
    ]
    scratch = [
        vmem((rows, D), f32),
        vmem((parts, rows, 512), f32),
        vmem((parts, D, 512), bf16),
        vmem((parts, 512, D), bf16),
        vmem((2, rows, D), bf16),
        vmem((rows, D), f32),
        vmem((2, rows, inner), bf16),
    ]
    scratch += [vmem(x.shape[1:], f32) for x in saved] + [vmem((D, D), bf16)] * 4
    scratch += [
        vmem((rows, rows), f32),
        vmem((rows, D), f32),
        vmem((D, rows), f32),
        vmem((HEADS // 2, 8, rows), f32),
        vmem((D, rows), f32),
        vmem((rows, D), f32),
        vmem((rows, D), f32),
        vmem((2, rows, 3 * D), bf16),
        vmem((2, rows, D), bf16),
        vmem((rows, D), f32),
        vmem((8, 128), f32),
        vmem((2, rows, 512), f32),
        vmem((2, 2, rows, 256), f32),
        vmem((2, 2, rows, 256), bf16),
        pltpu.SMEM(alphas.shape, f32),
        vmem((2,) + segments.shape, jnp.int32),
        dma((6,)),
        dma((parts, 3)),
        dma((4,)),
        dma((6,)),
        dma((3,)),
    ]

    def body(extra, *refs):
        chain_body(tick, extra, *refs)

    inputs = [info, TOKEN[0] if received is None else received, alphas, segments, valids, targets, before]
    inputs += list(saved) + [wi, wb, wq, wk, wv, wo]
    return call(body, "grad_chain", 2, inputs, [SCALARS], outs, scratch, previous, 2 * 10**10, 36)


def local_call(body, name, info, inputs, outs, scratch, specs=None, placed=()):
    inputs = [info, TOKEN[0]] + list(inputs)

    def parted(*refs):
        refs = refs[: len(inputs)] + refs[len(inputs) + len(placed) :]
        first = len(inputs)
        body(refs[0], refs[2:first], refs[first : first + len(outs)], refs[first + len(outs) + 1 :])

    results = pl.pallas_call(
        parted,
        out_shape=list(outs) + [loose(8, 128)],
        in_specs=[SCALARS] + [ANY] * (len(inputs) - 1 + len(placed)),
        out_specs=(specs or [ANY] * len(outs)) + [ANY],
        scratch_shapes=scratch,
        input_output_aliases={len(inputs) + i: i for i in range(len(placed))},
        compiler_params=pltpu.CompilerParams(vmem_limit_bytes=12 * 1024 * 1024),
        cost_estimate=pl.CostEstimate(flops=10**10, bytes_accessed=10**8, transcendentals=0),
        name=name,
    )(*inputs, *in_hbm(placed))
    TOKEN[0] = results[-1]
    return results[:-1]


def left_dims(done):
    return [axis for axis in (3, 2, 1, 0) if axis not in done]


def picked(ref, dims, axis, index):
    return ref.at[(slice(None),) * dims.index(axis) + (index,)]


def reduce_stage(sizes, order, step, info, arrays):
    shape = arrays[0].shape
    count = len(arrays)
    dims = left_dims(order[:step])
    parting = step < len(order) - 1
    if parting:
        axis = order[step]
        at = dims.index(axis)
        outs = [loose(*shape[:at], *shape[at + 1 :])] * sizes[axis]
    else:
        outs = [loose(*shape)]

    def body(info, ins, outs, scratch):
        held, sem = scratch
        wait_all(start_all([pltpu.make_async_copy(ref, held.at[i], sem.at[i]) for i, ref in enumerate(ins)]))
        total = held[0]
        for i in range(1, count):
            total = total + held[i]
        held[0] = total
        stores = []
        for by in range(len(outs)):
            source = held.at[0]
            if parting:
                source = picked(source, dims, axis, lax.rem(info[1 + axis] + by, sizes[axis]))
            stores.append(pltpu.make_async_copy(source, outs[by], sem.at[count + by]))
        wait_all(start_all(stores))

    scratch = [pltpu.VMEM((count,) + shape, jnp.float32), pltpu.SemaphoreType.DMA((count + len(outs),))]
    return local_call(body, "reduce_step", info, arrays, outs, scratch)


def place_stage(sizes, order, step, info, arrays):
    axis = order[step]
    dims = left_dims(order[:step])
    at = dims.index(axis)
    shape = arrays[0].shape
    count = sizes[axis]

    def body(info, ins, outs, scratch):
        copies = []
        for by in range(count):
            target = picked(outs[0], dims, axis, lax.rem(info[1 + axis] + count - by, count))
            copies.append(pltpu.make_async_copy(ins[by], target, scratch[0].at[by]))
        wait_all(start_all(copies))

    out = loose(*shape[:at], count, *shape[at:])
    return local_call(body, "place_step", info, arrays, [out], [pltpu.SemaphoreType.DMA((count,))])[0]


def out_copies(sizes, axis, info, kind, half, sources, outs, stage, sem):
    x, y, near, far = sizes
    rows = unit_shape(sizes)[3]
    depth = near * far // 4
    count = sizes[axis]
    copies = []

    def put(source, target):
        at = len(copies)
        load = pltpu.make_async_copy(source, stage.at[at], sem.at[0, at])
        copies.append((load, pltpu.make_async_copy(stage.at[at], target, sem.at[1, at])))

    for by, piece in sources:
        place = lax.rem(info[1 + axis] + count - by, count)
        for at in range(near * far if axis < 2 else far):
            if axis == 2:
                source = piece.at[at, :, :, pl.ds(0, rows)]
                z = at * near + place
            else:
                source = piece.at[at // near, at % near, :, pl.ds(0, rows)]
                z = at
            width = piece.shape[-1]
            first = half * width
            if kind == "rows":
                out, inside = outs[0], z
            elif kind == "columns":
                part = lax.div(z, depth) if axis == 2 else z // depth
                first = pl.multiple_of(part * D + first, 128) if axis == 2 else part * D + first
                out, inside = outs[0], lax.rem(z, depth) if axis == 2 else z % depth
            else:
                out, inside = outs[z // depth], z % depth
            lanes = pl.ds(first, width)
            if axis == 0:
                put(source, out.at[inside, :, place, :, lanes])
            elif axis == 1:
                put(source, out.at[inside, place, :, :, lanes])
            else:
                put(source, out.at[inside, :, :, :, lanes])
    start_all([load for load, _ in copies])
    for load, store in copies:
        load.wait()
        store.start()
    return [store for _, store in copies]


def out_scratch(sizes, axis, shape, pieces):
    rows, count = unit_shape(sizes)[3], pieces * (sizes[3] if axis == 2 else sizes[2] * sizes[3])
    inner = shape[1:3] if axis == 2 else shape[2:3]
    return [pltpu.VMEM((count, *inner, rows, shape[-1]), jnp.float32), pltpu.SemaphoreType.DMA((2, count))]


def out_shapes(sizes, kind):
    x, y, near, far = sizes
    rows = unit_shape(sizes)[3]
    depth = near * far // 4
    if kind == "rows":
        return [struct(near * far, y, x, rows, D)]
    if kind == "columns":
        return [struct(depth, y, x, rows, 4 * D)]
    return [struct(depth, y, x, rows, D)] * 4


def own_stage(sizes, axis, info, whole, kind, half, placed):
    def body(info, ins, outs, scratch):
        wait_all(out_copies(sizes, axis, info, kind, half, [(0, ins[0])], outs, *scratch))

    scratch = out_scratch(sizes, axis, whole.shape, 1)
    return local_call(body, "place_own", info, [whole], out_shapes(sizes, kind), scratch, None, placed)


def last_stage(sizes, axis, info, arrays, kind, half, placed):
    rows = unit_shape(sizes)[3]
    count = sizes[axis]
    shapes, specs = out_shapes(sizes, kind), None
    scratch = out_scratch(sizes, axis, arrays[0].shape, count - 1)
    has_small = arrays[0].shape[3] > rows
    if has_small:
        specs = [ANY] * len(shapes) + [LOCAL] * 2
        shapes += [loose(1, 2), loose(1, 3)]
        scratch += [pltpu.VMEM((8, 256), jnp.float32), pltpu.SemaphoreType.DMA((1,))]

    def body(info, ins, outs, scratch):
        sources = [(by, ins[by]) for by in range(1, count)]
        copies = out_copies(sizes, axis, info, kind, half, sources, outs, *scratch[:2])
        if has_small:
            tile_v, sem = scratch[2:]
            for by in range(count):

                @pl.when(info[1 + axis] == by)
                def _():
                    source = ins[by].at[0, 0, 0, pl.ds(rows, 8), pl.ds(0, 256)]
                    copy = pltpu.make_async_copy(source, tile_v, sem.at[0])
                    copy.start()
                    copy.wait()

            tile = tile_v[0:1, 0:128]
            outs[-2][...] = tile[:, 4:6]
            outs[-1][...] = jnp.sqrt(tile[:, 0:3] / (jnp.maximum(tile[:, 3:4], 1.0) * D))
        wait_all(copies)

    return local_call(body, "place_last", info, arrays, shapes, scratch, specs, placed)


def extents(count):
    bits = count.bit_length() - 1
    if 1 << bits != count:
        return (1, 1, 1, count)
    side = 1 << (bits // 3)
    depth = count // (side * side)
    near = 2 if depth > 1 else 1
    return (side, side, near, depth // near)


def shifted(value, axis, by, sizes):
    count = math.prod(sizes)
    stride, length = math.prod(sizes[:axis]), sizes[axis]
    pairs = []
    for chip in range(count):
        along = (chip // stride) % length
        pairs.append((chip, chip + ((along + by) % length - along) * stride))
    return lax.ppermute(value, "dp", pairs)


def summing(slots, order, kind, half, results, sizes, info):
    pieces = list(slots)
    steps = len(order)
    for step in range(1, steps + 1):
        axis = order[step - 1]
        pieces = [pieces[0]] + [
            shifted(pieces[by if step < steps else 0], axis, by, sizes) for by in range(1, sizes[axis])
        ]
        yield pieces[-1]
        pieces = reduce_stage(sizes, order, step, info, pieces)
    whole = pieces[0]
    for step in range(steps - 2, -1, -1):
        axis = order[step]
        copies = [whole] + [shifted(whole, axis, by, sizes) for by in range(1, sizes[axis])]
        yield copies[-1]
        if step:
            whole = place_stage(sizes, order, step, info, copies)
    placed = results.get(kind, ())
    results[kind] = own_stage(sizes, order[0], info, whole, kind, half, placed)
    yield
    outs = last_stage(sizes, order[0], info, copies, kind, half, results[kind])
    results[kind] = outs[: len(out_shapes(sizes, kind))]
    results["small"] = outs[len(results[kind]) :] or results.get("small")
    yield


def shards(stream_in, cotangent, segment_ids, pad_mask, w_query, w_key, w_value, w_out, w_in, w_back, alphas):
    weights = [weight[0] for weight in (w_query, w_key, w_value, w_out, w_in, w_back)]
    sizes = extents(lax.axis_size("dp"))
    chip = lax.axis_index("dp")
    section = lax.axis_index("section")
    places, left = [], chip
    for size in sizes:
        places.append(lax.rem(left, size))
        left = lax.div(left, size)
    info = jnp.stack([section] + places).astype(jnp.int32)
    TOKEN[0] = jnp.zeros((8, 128), jnp.float32)
    state, chain = None, None

    def forward_step(tick, received):
        return forward_tick(tick, info, alphas, segment_ids, pad_mask, stream_in, received, weights, state)

    def chain_step(tick, received):
        saved = state[2:7]
        return backward_chain(
            tick, info, alphas, segment_ids, pad_mask, cotangent, received, state[8], saved, weights, chain
        )

    received, upstreams = [None], [None]
    for tick in range(2):
        sent, state = forward_step(tick, received[tick])
        received.append(lax.ppermute(sent, "section", [(0, 1)]))
    for tick in range(3):
        *chain, sent = chain_step(tick, upstreams[tick])
        if tick < 2:
            upstreams.append(lax.ppermute(sent, "section", [(1, 0)]))
        if tick == 0:
            _, state = forward_step(2, received[2])
    acts, saved_s, _, _, _, saved_o, _, saved_m, saved_p, sums = state
    befores, spreads, firsts, passed, small = chain
    orders = {key: tuple("xynf".index(axis) for axis in order) for key, order in ORDERS.items()}
    results, streams = {}, {}

    def gradients(index):
        pair, kind = ("Bb", "Ii", "Aa")[index], ("rows", "columns", "four")[index]
        pair = [key for key in pair if key in orders]
        axes = [orders[key][0] for key in pair]
        if index == 0:
            slots = backward_back(info, alphas, upstreams[1:], cotangent, saved_p, sizes, axes)
        elif index == 1:
            slots = backward_inner(info, saved_m, befores, sizes, axes)
        else:
            slots = backward_attention(info, pad_mask, saved_s, saved_o, spreads, firsts, sums, small, sizes, axes)
        for half, key in enumerate(pair):
            count = sizes[axes[half]]
            streams[key] = summing(slots[:count], orders[key], kind, half, results, sizes, info)
            slots = slots[count:]

    made, steps, owned = 0, {}, set()
    for item in PROGRAM:
        if item == "|":
            gradients(made)
            made += 1
            continue
        steps[item] = steps.get(item, 0) + 1
        if steps[item] == 8:
            for key in [key for key in steps if steps[key] in (7, 8) and key not in owned]:
                owned.add(key)
                next(streams[key])
        next(streams[item])
    attention, inner, back = results["four"], results["columns"], results["rows"]
    return (
        acts[None, :, None],
        passed[None, :, None],
        attention[0].reshape(1, D, D),
        attention[1].reshape(1, D, D),
        attention[2].reshape(1, D, D),
        attention[3].reshape(1, D, D),
        inner[0].reshape(1, D, -1),
        back[0].reshape(1, -1, D),
        results["small"][0],
        results["small"][1],
    )


def solution(mesh):
    in_specs = (
        P(None, "dp", None, None),
        P(None, "dp", None, None),
        P(None, "dp", None),
        P(None, "dp", None),
        P("section", None, None),
        P("section", None, None),
        P("section", None, None),
        P("section", None, None),
        P("section", None, None),
        P("section", None, None),
        P("section", None),
    )
    out_specs = (
        P("section", None, "dp", None, None),
        P("section", None, "dp", None, None),
        P("section", None, None),
        P("section", None, None),
        P("section", None, None),
        P("section", None, None),
        P("section", None, None),
        P("section", None, None),
        P("section", None),
        P("section", None),
    )
    return jax.shard_map(shards, mesh=mesh, in_specs=in_specs, out_specs=out_specs, check_vma=False)
```
